512 devices in a mesh: space: 128 (over y, z, core), replicas: 4 (over x).
Axes of the slice: x: 4, y: 4, z: 16, core: 2. Of those that a mesh axis runs over, the one named last changes fastest.
Arguments:
- latents: bfloat16 [4, 32768, 128], P('replicas', 'space'), may hold values from -6 to 6
- pairs: int32 [4, 2, 131072], P('replicas', None, 'space'), may hold values from 0 to 319, as said below
- geometry: bfloat16 [4, 4, 131072], P('replicas', None, 'space'), may hold values from -6 to 6
- pair_count: int32 [4, 128], P('replicas', 'space'), may hold values from 256 to 1024, as said below
- cotangent: bfloat16 [4, 32768, 128], P('replicas', 'space'), may hold values from -6 to 6
- leaving: int32 [4, 256, 16], P('replicas', 'space'), may hold values from 0 to 255, as said below
- edge_in: bfloat16 [2, 260, 128], replicated, may hold values from -0.375 to 0.375
- edge_bias: float32 [2, 128], replicated, may hold values from -3 to 3
- edge_out: bfloat16 [2, 128, 128], replicated, may hold values from -0.5 to 0.5
- node_in: bfloat16 [2, 256, 128], replicated, may hold values from -0.375 to 0.375
- node_bias: float32 [2, 128], replicated, may hold values from -3 to 3
- node_out: bfloat16 [2, 128, 128], replicated, may hold values from -0.5 to 0.5
- gain: float32 [2, 128], replicated, may hold values from 0.1 to 1.9
Outputs:
- final_latents: bfloat16 [4, 32768, 128], P('replicas', 'space')
- grad_latents: float32 [4, 32768, 128], P('replicas', 'space')
- arrivals: bfloat16 [4, 256, 16, 128], P('replicas', 'space')
- grad_edge_in: float32 [2, 260, 128], replicated
- grad_edge_bias: float32 [2, 128], replicated
- grad_edge_out: float32 [2, 128, 128], replicated
- grad_node_in: float32 [2, 256, 128], replicated
- grad_node_bias: float32 [2, 128], replicated
- grad_node_out: float32 [2, 128, 128], replicated
- grad_gain: float32 [2, 128], replicated
The draws below stay inside these ranges and needn't reach their ends.
Inputs may be any that keep to these rules, and one draw needn't show every extreme that they name: `pairs`: in each domain's slots, the first row holds an owned particle, 32 to 287, and the second row a partner within 32 rows of it, never itself. `pair_count`: at least 256 in every domain; in each replica some domain has all 1024 slots live. `leaving`: the entries of a row are distinct; particles moving down lie among the first 32 rows of their domain, those moving up among the last 32.
All inputs are finite; a program needn't handle non-finite values.
Results may differ from the reference program's by a relative error of at most 0.02.
Values may be sent and summed in bfloat16 or wider, within the bound.
No kernel may reach another device: no remote copies, remote signals or barrier semaphores. Data moves between devices by JAX's collectives and lax.ppermute only.
A program may use at most 64 MiB of HBM per device.

```python
import jax
import jax.numpy as jnp
from jax import lax

L = 128
H = 128
G = 4
P_DEV = 256
STEPS = 2
HALO = 32
EMAX = 1024
MIG = 16
N_SPACE = 128
N_REPLICAS = 4


def draw_pairs(key, part):
    key = jax.random.fold_in(key, 11)
    rows = N_REPLICAS * N_SPACE
    key_owned, key_offset, key_sign = jax.random.split(key, 3)
    owned = jax.random.randint(key_owned, (rows, EMAX), HALO, HALO + P_DEV)
    offset = jax.random.randint(key_offset, (rows, EMAX), 1, HALO + 1)
    direction = 2 * jax.random.randint(key_sign, (rows, EMAX), 0, 2) - 1
    other = owned + direction * offset
    owned = owned.at[:, 0].set(HALO + P_DEV - 1).at[:, 1].set(HALO)
    other = other.at[:, 0].set(P_DEV + 2 * HALO - 1).at[:, 1].set(0)
    both = jnp.stack([owned, other], axis=0).reshape(2, N_REPLICAS, N_SPACE * EMAX)
    return jnp.transpose(both, (1, 0, 2)).astype(jnp.int32)


def draw_pair_count(key, part):
    key = jax.random.fold_in(key, 17)
    key_count, key_full = jax.random.split(key)
    counts = jax.random.randint(key_count, (N_REPLICAS, N_SPACE), EMAX // 4, EMAX + 1)
    fullest = jax.random.randint(key_full, (N_REPLICAS, 1), 0, N_SPACE)
    domain = jnp.arange(N_SPACE, dtype=jnp.int32)[None, :]
    return jnp.where(domain == fullest, EMAX, counts).astype(jnp.int32)


def pick_rows(key):
    order = jax.random.permutation(key, HALO - 1)[:MIG - 1] + 1
    return jnp.concatenate([jnp.zeros((1,), jnp.int32), order.astype(jnp.int32)])


def draw_leaving(key, part):
    key = jax.random.fold_in(key, 23)
    rows = N_REPLICAS * N_SPACE
    keys = jax.random.split(key, 2 * rows)
    picked = jax.vmap(pick_rows)(keys).reshape(rows, 2, MIG)
    moved = picked.at[:, 1].set(P_DEV - 1 - picked[:, 1])
    return moved.reshape(N_REPLICAS, 2 * N_SPACE, MIG).astype(jnp.int32)


def block_scale(rng, dims, cuts, low, high):
    loudness = 1.0
    for axis_at, shards_of in cuts:
        heights = jax.random.uniform(jax.random.fold_in(jax.random.fold_in(rng, 6), axis_at), (shards_of,), jnp.float32, low / len(cuts), high / len(cuts))
        loudness = loudness * jnp.repeat(jnp.exp(heights), dims[axis_at] // shards_of).reshape((-1,) + (1,) * (len(dims) - 1 - axis_at))
    return loudness


def normal_values(own_key, shape, scale, limit, shards=(), kind=jnp.bfloat16):
    level = block_scale(own_key, shape, shards, -0.22, 0.18) if shards else 1.0
    drawn = jax.random.normal(own_key, shape, jnp.float32) * scale * level
    return jnp.minimum(jnp.maximum(drawn, -limit), limit).astype(kind)


def setup_inputs(seed: int = 0) -> dict:
    splits = jax.random.split(jax.random.key(seed), 14)
    return {
        "latents": normal_values(splits[0], (N_REPLICAS, N_SPACE * P_DEV, L), 1.0, 6.0, ((0, 4), (1, 128))),
        "pairs": draw_pairs(jax.random.fold_in(splits[13], 71), 0),
        "geometry": normal_values(splits[2], (N_REPLICAS, G, N_SPACE * EMAX), 1.0, 6.0, ((0, 4), (2, 128))),
        "pair_count": draw_pair_count(jax.random.fold_in(splits[13], 71), 0),
        "cotangent": normal_values(splits[4], (N_REPLICAS, N_SPACE * P_DEV, L), 1.0, 6.0, ((0, 4), (1, 128))),
        "leaving": draw_leaving(jax.random.fold_in(splits[13], 71), 0),
        "edge_in": normal_values(splits[6], (STEPS, 2 * L + G, H), (2 * L + G) ** -0.5, 0.375),
        "edge_bias": normal_values(splits[7], (STEPS, H), 0.5, 3.0, (), jnp.float32),
        "edge_out": normal_values(splits[8], (STEPS, H, L), H ** -0.5, 0.5),
        "node_in": normal_values(splits[9], (STEPS, 2 * L, H), (2 * L) ** -0.5, 0.375),
        "node_bias": normal_values(splits[10], (STEPS, H), 0.5, 3.0, (), jnp.float32),
        "node_out": normal_values(splits[11], (STEPS, H, L), H ** -0.5, 0.5),
        "gain": jnp.clip(1.0 + 0.18 * jax.random.normal(splits[12], (STEPS, L), jnp.float32), 0.1, 1.9),
    }


eps = 1e-05

def silu_slope(value):
    sig = jax.nn.sigmoid(value)
    return sig * (1.0 + value * (1.0 - sig))

def edge_forward(rows_src, owned_rows, other_rows, features, live_slots, weight_in, bias_in, weight_out):
    left_rows = jnp.take(rows_src, owned_rows, axis=0)
    right_rows = jnp.take(rows_src, other_rows, axis=0)
    x_fwd = jnp.concatenate([left_rows, right_rows, features], axis=1)
    x_rev = jnp.concatenate([right_rows, left_rows, -features], axis=1)
    pre_fwd = jnp.dot(x_fwd, weight_in, preferred_element_type=jnp.float32) + bias_in
    pre_rev = jnp.dot(x_rev, weight_in, preferred_element_type=jnp.float32) + bias_in
    diff = (jax.nn.silu(pre_fwd) - jax.nn.silu(pre_rev)).astype(jnp.bfloat16)
    message = jnp.dot(diff, weight_out, preferred_element_type=jnp.float32) * live_slots[:, None]
    return (message, (x_fwd, x_rev, pre_fwd, pre_rev, diff))

def edge_backward(dagg, owned_rows, other_rows, live_slots, kept, weight_in, weight_out):
    x_fwd, x_rev, pre_fwd, pre_rev, diff = kept
    width = dagg.shape[1]
    dmessage = ((jnp.take(dagg, owned_rows, axis=0) - jnp.take(dagg, other_rows, axis=0)) * live_slots[:, None]).astype(jnp.bfloat16)
    out_term = jnp.dot(diff.T, dmessage, preferred_element_type=jnp.float32)
    dd = jnp.dot(dmessage, weight_out.T, preferred_element_type=jnp.float32)
    dfwd = (dd * silu_slope(pre_fwd)).astype(jnp.bfloat16)
    drev = (-dd * silu_slope(pre_rev)).astype(jnp.bfloat16)
    in_term = jnp.dot(x_fwd.T, dfwd, preferred_element_type=jnp.float32) + jnp.dot(x_rev.T, drev, preferred_element_type=jnp.float32)
    bias_term = lax.optimization_barrier(jnp.sum(dfwd.astype(jnp.float32) + drev.astype(jnp.float32), axis=0))
    leading = weight_in[:2 * width]
    dx_fwd = jnp.dot(dfwd, leading.T, preferred_element_type=jnp.float32)
    dx_rev = jnp.dot(drev, leading.T, preferred_element_type=jnp.float32)
    d_owned = dx_fwd[:, :width] + dx_rev[:, width:]
    d_other = dx_fwd[:, width:] + dx_rev[:, :width]
    return (d_owned, d_other, (in_term, bias_term, out_term))

def node_forward(latent, agg, weight_in, bias_in, weight_out, gain_row):
    joined = jnp.concatenate([latent, agg.astype(jnp.bfloat16)], axis=1)
    node_pre = jnp.dot(joined, weight_in, preferred_element_type=jnp.float32) + bias_in
    hidden = jax.nn.silu(node_pre).astype(jnp.bfloat16)
    out = jnp.dot(hidden, weight_out, preferred_element_type=jnp.float32)
    centred = out - lax.optimization_barrier(jnp.mean(out, axis=1, keepdims=True))
    inv_std = lax.rsqrt(lax.optimization_barrier(jnp.mean(centred * centred, axis=1, keepdims=True)) + eps)
    normed = centred * inv_std
    new_latent = (latent.astype(jnp.float32) + normed * gain_row).astype(jnp.bfloat16)
    return (new_latent, (joined, node_pre, hidden, normed, inv_std))

def node_backward(grad, kept, weight_in, weight_out, gain_row):
    joined, node_pre, hidden, normed, inv_std = kept
    width = grad.shape[1]
    gain_term = lax.optimization_barrier(jnp.sum(grad * normed, axis=0))
    dnorm = grad * gain_row
    dout = ((dnorm - lax.optimization_barrier(jnp.mean(dnorm, axis=1, keepdims=True)) - normed * lax.optimization_barrier(jnp.mean(dnorm * normed, axis=1, keepdims=True))) * inv_std).astype(jnp.bfloat16)
    out_term = jnp.dot(hidden.T, dout, preferred_element_type=jnp.float32)
    dhidden = jnp.dot(dout, weight_out.T, preferred_element_type=jnp.float32)
    dpre = (dhidden * silu_slope(node_pre)).astype(jnp.bfloat16)
    in_term = jnp.dot(joined.T, dpre, preferred_element_type=jnp.float32)
    bias_term = lax.optimization_barrier(jnp.sum(dpre.astype(jnp.float32), axis=0))
    dx = jnp.dot(dpre, weight_in.T, preferred_element_type=jnp.float32)
    return (grad + dx[:, :width], dx[:, width:], (in_term, bias_term, out_term, gain_term))

def replica(latents, pairs, geometry, pair_count, cotangent, leaving, weights):
    edge_in, edge_bias, edge_out, node_in, node_bias, node_out, gain = weights
    total = N_SPACE * P_DEV
    width = latents.shape[1]
    domain = jnp.arange(N_SPACE, dtype=jnp.int32)[:, None]
    offset = domain * P_DEV - HALO
    owned_all = (pairs[0].reshape(N_SPACE, EMAX) + offset) % total
    other_all = (pairs[1].reshape(N_SPACE, EMAX) + offset) % total
    feature_all = jnp.transpose(geometry.reshape(G, N_SPACE, EMAX), (1, 2, 0))
    live_all = (jnp.arange(EMAX, dtype=jnp.int32)[None, :] < pair_count[:, None]).astype(jnp.float32)
    blocks = (owned_all, other_all, feature_all, live_all)
    latent = latents
    history = []
    for layer in range(STEPS):

        def sweep(agg, block, layer=layer, latent=latent):
            owned_rows, other_rows, features, live_slots = block
            message, _ = edge_forward(latent, owned_rows, other_rows, features, live_slots, edge_in[layer], edge_bias[layer], edge_out[layer])
            return (agg.at[owned_rows].add(message).at[other_rows].add(-message), None)
        agg, _ = lax.scan(sweep, jnp.zeros((total, width), jnp.float32), blocks)
        new_latent, kept = node_forward(latent, agg, node_in[layer], node_bias[layer], node_out[layer], gain[layer])
        history.append((latent, kept))
        latent = new_latent
    grad = cotangent.astype(jnp.float32)
    per_layer = [None] * STEPS
    for layer in reversed(range(STEPS)):
        latent_in, kept = history[layer]
        dh_node, dagg, node_terms = node_backward(grad, kept, node_in[layer], node_out[layer], gain[layer])

        def back(carry, block, layer=layer, latent_in=latent_in, dagg=dagg):
            accum, in_acc, bias_acc, out_acc = carry
            owned_rows, other_rows, features, live_slots = block
            _, kept_edge = edge_forward(latent_in, owned_rows, other_rows, features, live_slots, edge_in[layer], edge_bias[layer], edge_out[layer])
            d_owned, d_other, terms = edge_backward(dagg, owned_rows, other_rows, live_slots, kept_edge, edge_in[layer], edge_out[layer])
            accum = accum.at[owned_rows].add(d_owned).at[other_rows].add(d_other)
            return ((accum, in_acc + terms[0], bias_acc + terms[1], out_acc + terms[2]), None)
        start = (jnp.zeros((total, width), jnp.float32), jnp.zeros(edge_in.shape[1:], jnp.float32), jnp.zeros(edge_bias.shape[1:], jnp.float32), jnp.zeros(edge_out.shape[1:], jnp.float32))
        (edge_dh, in_acc, bias_acc, out_acc), _ = lax.scan(back, start, blocks)
        grad = dh_node + edge_dh
        per_layer[layer] = (in_acc, bias_acc, out_acc) + node_terms
    grads = tuple((jnp.stack([entry[k] for entry in per_layer]) for k in range(7)))
    final = latent.reshape(N_SPACE, P_DEV, width)
    movers = leaving.reshape(N_SPACE, 2, MIG)
    down_rows = jnp.take_along_axis(final, movers[:, 0, :, None], axis=1)
    up_rows = jnp.take_along_axis(final, movers[:, 1, :, None], axis=1)
    from_upper = jnp.roll(down_rows, -1, axis=0)
    from_lower = jnp.roll(up_rows, 1, axis=0)
    arrivals = jnp.stack([from_upper, from_lower], axis=1).reshape(2 * N_SPACE, MIG, width)
    return (latent, grad, arrivals, grads)

def reference(latents, pairs, geometry, pair_count, cotangent, leaving, edge_in, edge_bias, edge_out, node_in, node_bias, node_out, gain):
    weights = (edge_in, edge_bias, edge_out, node_in, node_bias, node_out, gain)

    def one_replica(packed):
        return replica(*packed, weights)
    final, grad_latents, arrivals, grads = lax.map(one_replica, (latents, pairs, geometry, pair_count, cotangent, leaving))
    summed = tuple((lax.optimization_barrier(jnp.sum(entry, axis=0)) for entry in grads))
    return (final, grad_latents, arrivals) + summed
```

```python
import jax
import jax.numpy as jnp
from jax import lax
from jax.experimental import pallas as pl
from jax.experimental.pallas import tpu as pltpu
from jax.sharding import Mesh, PartitionSpec as P


F32 = jnp.float32
BF16 = jnp.bfloat16
L = 128
ROWS = 256
EMAX = 1024
BLK = 256
OWN_BLOCKS = EMAX // BLK
NB_BLOCKS = EMAX // 128
LAT_HALO = 128
COT_HALO = 64
SENT = LAT_HALO + COT_HALO + 64 + 16
D_AT = LAT_HALO + COT_HALO
X_AT = D_AT + 64
MIG = 16
MAIN = 1536
EXTRA = 14
EPS = 1e-05
VMEM_LIMIT = 48 * 1024 * 1024


def dot(a, b):
    return jnp.dot(a, b, preferred_element_type=F32)


def dot_nt(a, b):
    return lax.dot_general(a, b, (((1,), (1,)), ((), ())), preferred_element_type=F32)


def dot_tn(a, b):
    return lax.dot_general(a, b, (((0,), (0,)), ((), ())), preferred_element_type=F32)


def place(row):
    below = row < 0
    above = row >= ROWS
    out = jnp.where(below, -1 - row, row - ROWS)
    block = lax.shift_right_arithmetic(out, 5)
    inner = jnp.where(below, row + 32 * (block + 1), row - ROWS - 32 * block + 32)
    outside = jnp.logical_or(below, above)
    return jnp.where(outside, 64 * block + inner, row), outside


def pack_kernel(count_ref, lat_ref, cot_ref, pairs_ref, geo_ref, leav_ref, up_ref, down_ref):
    count = count_ref[0, 0]
    own = pairs_ref[0, 0:1, :]
    other = pairs_ref[0, 1:2, :]
    slot = lax.broadcasted_iota(jnp.int32, (1, EMAX), 1)
    live = slot < count
    geo = geo_ref[0].astype(F32)
    leav = leav_ref[0].astype(F32)

    def fill(ref, lat, cot, shift, movers, mover_shift):
        ref[0:LAT_HALO, :] = lat
        ref[LAT_HALO:D_AT, :] = cot
        i_row = own + shift
        j_row = other + shift
        inside = jnp.logical_and(
            jnp.logical_and(i_row >= -LAT_HALO, i_row < ROWS + LAT_HALO),
            jnp.logical_and(j_row >= -LAT_HALO, j_row < ROWS + LAT_HALO),
        )
        good = jnp.logical_and(live, inside)
        i_at, _ = place(i_row)
        j_at, j_hi = place(j_row)
        i_at = jnp.where(good, i_at, -1).astype(F32)
        j_at = jnp.where(good, j_at, -1).astype(F32)
        hi = jnp.where(j_hi, 1.0, 0.0).astype(F32)
        rows = jnp.concatenate([i_at, j_at, hi, jnp.ones((1, EMAX), F32), geo], axis=0)
        for t in range(4):
            two = [rows[:, 256 * t : 256 * t + 128], rows[:, 256 * t + 128 : 256 * t + 256]]
            ref[D_AT + 16 * t : D_AT + 16 * t + 16, :] = jnp.concatenate(two, axis=0).astype(BF16)
        tail = jnp.concatenate([movers + mover_shift, jnp.zeros((1, 128 - MIG), F32)], axis=1)
        ref[X_AT:SENT, :] = jnp.broadcast_to(tail, (16, 128)).astype(BF16)

    fill(up_ref, lat_ref[0, ROWS - LAT_HALO :, :], cot_ref[0, ROWS - COT_HALO :, :], -32 - ROWS, leav[1:2, :], -224.0)
    fill(down_ref, lat_ref[0, :LAT_HALO, :], cot_ref[0, :COT_HALO, :], ROWS - 32, leav[0:1, :], 32.0)


def main_kernel(
    chunks,
    count_ref,
    lat_ref,
    cot_ref,
    pairs_ref,
    geo_ref,
    low_ref,
    upp_ref,
    edge_in_ref,
    edge_bias_ref,
    edge_out_ref,
    node_in_ref,
    node_bias_ref,
    node_out_ref,
    gain_ref,
    final_ref,
    grad_ref,
    arr_ref,
    packed_ref,
    ohi,
    ohj,
    ohit,
    ohjt,
    jhi,
    dcol,
    drow,
    slope,
    t_nb,
    q_nb,
):
    lanes = lax.broadcasted_iota(jnp.int32, (BLK, BLK), 1).astype(F32)
    subs = lax.broadcasted_iota(jnp.int32, (BLK, BLK), 0).astype(F32)

    def prepare(block, rows, cols):
        ohi[block] = jnp.where(cols[:, 0:1] == lanes, 1.0, 0.0).astype(BF16)
        ohj[block] = jnp.where(cols[:, 1:2] == lanes, 1.0, 0.0).astype(BF16)
        ohit[block] = jnp.where(rows[0:1, :] == subs, 1.0, 0.0).astype(BF16)
        ohjt[block] = jnp.where(rows[1:2, :] == subs, 1.0, 0.0).astype(BF16)
        jhi[block] = jnp.broadcast_to(cols[:, 2:3], (BLK, L))
        dcol[block] = cols.astype(BF16)

    count = count_ref[0, 0]
    slot = lax.broadcasted_iota(jnp.int32, (1, EMAX), 1)
    live = slot < count
    i_at = pairs_ref[0, 0:1, :] - 32
    j_at, j_out = place(pairs_ref[0, 1:2, :] - 32)
    own_rows = jnp.concatenate(
        [
            jnp.where(live, i_at, -1).astype(F32),
            jnp.where(live, j_at, -1).astype(F32),
            jnp.where(j_out, 1.0, 0.0).astype(F32),
            jnp.ones((1, EMAX), F32),
            geo_ref[0].astype(F32),
        ],
        axis=0,
    )
    for k in range(OWN_BLOCKS):
        rows = own_rows[:, BLK * k : BLK * k + BLK]
        drow[k] = rows.astype(BF16)
        prepare(k, rows, jnp.transpose(rows))

    low_rows = low_ref[D_AT:X_AT, :].astype(F32)
    upp_rows = upp_ref[D_AT:X_AT, :].astype(F32)
    for k in range(NB_BLOCKS):
        rows = jnp.concatenate([low_rows[8 * k : 8 * k + 8], upp_rows[8 * k : 8 * k + 8]], axis=1)
        prepare(OWN_BLOCKS + k, rows, jnp.transpose(rows))

    def around(source_low, source_upp, width, height):
        parts = []
        for b in range(width // 32):
            parts.append(source_low[width - 32 * (b + 1) : width - 32 * b])
            parts.append(source_upp[32 * b : 32 * b + 32])
        if height > 2 * width:
            parts.append(jnp.zeros((height - 2 * width, L), parts[0].dtype))
        return jnp.concatenate(parts, axis=0)

    def halves(cat):
        return cat[:, :L], cat[:, L:]

    def edge_weights(layer):
        top = edge_in_ref[layer, 0:L, :]
        bottom = edge_in_ref[layer, L : 2 * L, :]
        straight = jnp.concatenate([top, bottom], axis=1)
        return straight, jnp.concatenate([bottom, top], axis=1)

    def forward_block(block, i_source, both, weights, geo_weights, bias, layer):
        at_i = dot(ohi[block], i_source).astype(BF16)
        lo, hi = halves(dot(ohj[block], both))
        is_hi = jhi[block] > 0.5
        at_j = jnp.where(is_hi, hi, lo).astype(BF16)
        pre = dot(jnp.concatenate([at_i, at_j], axis=1), weights) + dot(dcol[block], geo_weights) + bias
        sig = 0.5 * jnp.tanh(0.5 * pre) + 0.5
        act = pre * sig
        slope[layer, block] = sig + act * (1.0 - sig)
        diff = act[:, :L] - act[:, L:]
        none = jnp.zeros_like(diff)
        split = jnp.concatenate([jnp.where(is_hi, none, diff), jnp.where(is_hi, diff, none)], axis=1)
        return dot(ohit[block], diff.astype(BF16)), dot(ohjt[block], split.astype(BF16))

    def edge_forward(layer, h_lo, h_hi, nb_blocks):
        straight, crossed = edge_weights(layer)
        weights = jnp.concatenate([straight, crossed], axis=0)
        geo_top = edge_in_ref[layer, 2 * L : 2 * L + 4, :].astype(F32)
        geo_weights = jnp.concatenate(
            [jnp.zeros((4, 2 * L), F32), jnp.concatenate([geo_top, -geo_top], axis=1)], axis=0
        ).astype(BF16)
        bias_row = edge_bias_ref[layer : layer + 1, :]
        bias = jnp.concatenate([bias_row, bias_row], axis=1)
        both = jnp.concatenate([h_lo, h_hi], axis=1)
        t_nb[...] = jnp.zeros_like(t_nb)

        def body(k, carry):
            by_i, by_j = forward_block(OWN_BLOCKS + k, h_hi, both, weights, geo_weights, bias, layer)
            t_nb[:, :L] += -by_j[:, :L]
            t_nb[:, L:] += by_i - by_j[:, L:]
            return carry

        lax.fori_loop(0, nb_blocks, body, 0)
        own_lo = jnp.zeros((ROWS, L), F32)
        own_hi = jnp.zeros((ROWS, L), F32)
        for k in range(OWN_BLOCKS):
            by_i, by_j = forward_block(k, h_lo, both, weights, geo_weights, bias, layer)
            own_lo += by_i - by_j[:, :L]
            own_hi += -by_j[:, L:]
        return own_lo, own_hi

    def node_forward(layer, h, total):
        agg = dot(total.astype(BF16), edge_out_ref[layer]).astype(BF16)
        joined = jnp.concatenate([h, agg], axis=1)
        pre = dot(joined, node_in_ref[layer]) + node_bias_ref[layer : layer + 1, :]
        sig = 0.5 * jnp.tanh(0.5 * pre) + 0.5
        act = pre * sig
        hidden = act.astype(BF16)
        out = dot(hidden, node_out_ref[layer])
        centred = out - jnp.mean(out, axis=1, keepdims=True)
        inv = lax.rsqrt(jnp.mean(centred * centred, axis=1, keepdims=True) + EPS)
        normed = centred * inv
        new = (h.astype(F32) + normed * gain_ref[layer : layer + 1, :]).astype(BF16)
        return new, (joined, sig + act * (1.0 - sig), hidden, normed, inv)

    def node_backward(layer, grad, kept):
        size = grad.shape[0]
        joined, node_slope, hidden, normed, inv = (v[:size] for v in kept)
        gain_term = jnp.sum(grad[:ROWS] * normed[:ROWS], axis=0, keepdims=True)
        dnorm = grad * gain_ref[layer : layer + 1, :]
        mean_a = jnp.mean(dnorm, axis=1, keepdims=True)
        mean_b = jnp.mean(dnorm * normed, axis=1, keepdims=True)
        dout = ((dnorm - mean_a - normed * mean_b) * inv).astype(BF16)
        out_term = dot_tn(hidden[:ROWS], dout[:ROWS])
        dpre = (dot_nt(dout, node_out_ref[layer]) * node_slope).astype(BF16)
        in_term = dot_tn(joined[:ROWS], dpre[:ROWS])
        bias_term = jnp.sum(dpre[:ROWS].astype(F32), axis=0, keepdims=True)
        dx = dot_nt(dpre, node_in_ref[layer])
        return grad + dx[:, :L], dx[:, L:].astype(BF16), (in_term, bias_term, out_term, gain_term)

    def backward_block(block, i_source, both, layer):
        at_i = dot(ohi[block], i_source)
        lo, hi = halves(dot(ohj[block], both))
        is_hi = jhi[block] > 0.5
        dd = at_i - jnp.where(is_hi, hi, lo)
        dfwd = dd * slope[layer, block, :, :L]
        drev = -dd * slope[layer, block, :, L:]
        straight = jnp.concatenate([dfwd, drev], axis=1)
        crossed = jnp.concatenate([drev, dfwd], axis=1)
        wide = jnp.concatenate([is_hi, is_hi], axis=1)
        return straight.astype(BF16), crossed, wide

    def edge_backward(layer, e_lo, e_hi, nb_blocks, with_hi):
        both = jnp.concatenate([e_lo, e_hi], axis=1)
        q_nb[...] = jnp.zeros_like(q_nb)

        def body(k, carry):
            block = OWN_BLOCKS + k
            straight, crossed, is_hi = backward_block(block, e_hi, both, layer)
            none = jnp.zeros_like(crossed)
            q_nb[0:ROWS, :] += dot(ohjt[block], jnp.where(is_hi, none, crossed).astype(BF16))
            if with_hi:
                q_nb[ROWS:, :] += dot(ohjt[block], jnp.where(is_hi, crossed, none).astype(BF16)) + dot(
                    ohit[block], straight
                )
            return carry

        lax.fori_loop(0, nb_blocks, body, 0)
        q_lo = jnp.zeros((ROWS, 2 * L), F32)
        q_hi = jnp.zeros((ROWS, 2 * L), F32)
        geo = jnp.zeros((8, 2 * L), F32)
        for k in range(OWN_BLOCKS):
            straight, crossed, is_hi = backward_block(k, e_lo, both, layer)
            none = jnp.zeros_like(crossed)
            q_lo += dot(ohit[k], straight) + dot(ohjt[k], jnp.where(is_hi, none, crossed).astype(BF16))
            q_hi += dot(ohjt[k], jnp.where(is_hi, crossed, none).astype(BF16))
            geo += dot(drow[k], straight)
        return q_lo, q_hi, geo

    h0_lo = lat_ref[0]
    h0_hi = around(low_ref[0:LAT_HALO, :], upp_ref[0:LAT_HALO, :], LAT_HALO, ROWS)
    t0_lo, t0_hi = edge_forward(0, h0_lo, h0_hi, NB_BLOCKS)
    total0 = jnp.concatenate([t0_lo + t_nb[:, :L], t0_hi + t_nb[:, L:]], axis=0)
    h0 = jnp.concatenate([h0_lo, h0_hi], axis=0)
    h1, kept0 = node_forward(0, h0, total0)
    t1_lo, t1_hi = edge_forward(1, h1[:ROWS], h1[ROWS:], NB_BLOCKS)
    near = ROWS + 2 * COT_HALO
    total1 = jnp.concatenate([t1_lo + t_nb[:, :L], t1_hi[: near - ROWS] + t_nb[: near - ROWS, L:]], axis=0)
    h2, kept1 = node_forward(1, h1[:near], total1)
    final_ref[0] = h2[:ROWS]

    few = lax.broadcasted_iota(jnp.int32, (MIG, 2 * COT_HALO), 1).astype(F32)
    for k, ref in ((0, upp_ref), (1, low_ref)):
        movers = jnp.transpose(ref[X_AT:SENT, :].astype(F32))[0:MIG, 0:1]
        chosen = jnp.where(movers == few, 1.0, 0.0).astype(BF16)
        arr_ref[0, k] = dot(chosen, h2[ROWS:]).astype(BF16)

    def with_zeros(value):
        return jnp.concatenate([value, jnp.zeros((2 * ROWS - value.shape[0],) + value.shape[1:], value.dtype)], axis=0)

    def layer_back(layer, grad, kept, own_total, h, nb_blocks, keep_rows):
        part, dagg, node_terms = node_backward(layer, grad, kept)
        spread = with_zeros(dagg)
        e = with_zeros(dot_nt(dagg, edge_out_ref[layer]).astype(BF16))
        q_lo, q_hi, geo = edge_backward(layer, e[:ROWS], e[ROWS:], nb_blocks, keep_rows > ROWS)
        out_term = dot_tn(own_total.astype(BF16), spread)
        q_own = jnp.concatenate([q_lo, q_hi], axis=0)
        in_term = dot_tn(h, q_own.astype(BF16))
        straight, _ = edge_weights(layer)
        q_all = (q_own[:keep_rows] + q_nb[:keep_rows, :]).astype(BF16)
        new = part[:keep_rows] + dot_nt(q_all, straight)
        return new, (in_term, geo, out_term) + node_terms

    own1 = jnp.concatenate([t1_lo, t1_hi], axis=0)
    own0 = jnp.concatenate([t0_lo, t0_hi], axis=0)
    cot = jnp.concatenate(
        [cot_ref[0], around(low_ref[LAT_HALO:D_AT, :], upp_ref[LAT_HALO:D_AT, :], COT_HALO, 2 * COT_HALO)], axis=0
    ).astype(F32)
    grad1, terms1 = layer_back(1, cot, kept1, own1, h1, NB_BLOCKS, ROWS + 64)
    grad0, terms0 = layer_back(0, grad1, kept0, own0, h0, NB_BLOCKS, ROWS)
    grad_ref[0] = grad0

    size = MAIN // chunks
    per = -(-EXTRA // chunks)
    packed_ref[:, size:, :] = jnp.zeros((chunks, packed_ref.shape[1] - size, L), BF16)
    at = 0
    extra = 0
    for terms in (terms0, terms1):
        in_term, geo, out_term, node_in_term, node_bias_term, node_out_term, gain_term = terms
        for value in (in_term[:, :L], in_term[:, L:], out_term, node_in_term, node_out_term):
            value = value.astype(BF16)
            for r in range(0, value.shape[0], 16):
                packed_ref[at // size, pl.ds(at % size, 16), :] = value[r : r + 16]
                at += 16
        small = [geo[4 + g : 5 + g, :L] - geo[4 + g : 5 + g, L:] for g in range(4)]
        small += [geo[3:4, :L] + geo[3:4, L:], node_bias_term, gain_term]
        for value in small:
            spot = size + extra % per
            packed_ref[extra // per, spot : spot + 1, :] = value.astype(BF16)
            extra += 1


def fold_kernel(copies, in_ref, out_ref):
    total = in_ref[0].astype(F32)
    for k in range(1, in_ref.shape[0]):
        total += in_ref[k].astype(F32)
    total = total.astype(BF16)
    for k in range(copies):
        out_ref[k] = total


def fold(array, copies):
    return pl.pallas_call(
        lambda a, b: fold_kernel(copies, a, b),
        out_shape=jax.ShapeDtypeStruct((copies,) + array.shape[1:], BF16),
        in_specs=[pl.BlockSpec(memory_space=pltpu.VMEM)],
        out_specs=pl.BlockSpec(memory_space=pltpu.VMEM),
        compiler_params=pltpu.CompilerParams(vmem_limit_bytes=VMEM_LIMIT),
        name="fold",
    )(array)


def unpack_kernel(chunks, in_ref, edge_in, edge_bias, edge_out, node_in, node_bias, node_out, gain):
    size = MAIN // chunks
    per = -(-EXTRA // chunks)
    at = 0
    extra = 0
    for layer in range(2):
        for ref, rows in ((edge_in, 2 * L), (edge_out, L), (node_in, 2 * L), (node_out, L)):
            for r in range(0, rows, 16):
                ref[layer, r : r + 16, :] = in_ref[at // size, pl.ds(at % size, 16), :].astype(F32)
                at += 16
        small = []
        for _ in range(7):
            spot = size + extra % per
            small.append(in_ref[extra // per, spot : spot + 1, :].astype(F32))
            extra += 1
        edge_in[layer, 2 * L : 2 * L + 4, :] = jnp.concatenate(small[:4], axis=0)
        edge_bias[layer : layer + 1, :] = small[4]
        node_bias[layer : layer + 1, :] = small[5]
        gain[layer : layer + 1, :] = small[6]


def vmem(count):
    return [pl.BlockSpec(memory_space=pltpu.VMEM)] * count


def solution(mesh):
    n_space = mesh.shape["space"]
    n_x = mesh.shape["replicas"]
    n_c = 2
    n_z = min(16, n_space // n_c)
    n_y = n_space // (n_c * n_z)
    fine = Mesh(mesh.devices.reshape(n_y, n_z, n_c, n_x), ("y", "z", "c", "x"))
    space = ("y", "z", "c")
    group = ("y", "x", "c")
    chunks = n_y * n_x * n_c
    size = MAIN // chunks
    chunk_rows = size + -(-(-(-EXTRA // chunks)) // 8) * 8
    params = pltpu.CompilerParams(vmem_limit_bytes=VMEM_LIMIT)

    def on_device(latents, pairs, geometry, pair_count, cotangent, leaving, *weights):
        smem = pl.BlockSpec(memory_space=pltpu.SMEM)
        sent = jax.ShapeDtypeStruct((SENT, L), BF16)
        up, down = pl.pallas_call(
            pack_kernel,
            out_shape=(sent, sent),
            in_specs=[smem] + vmem(5),
            out_specs=tuple(vmem(2)),
            compiler_params=params,
            name="pack",
        )(pair_count, latents, cotangent, pairs, geometry, leaving)
        ring = range(n_space)
        low = lax.ppermute(up, space, [(i, (i + 1) % n_space) for i in ring])
        upp = lax.ppermute(down, space, [(i, (i - 1) % n_space) for i in ring])
        blocks = OWN_BLOCKS + NB_BLOCKS
        final, grad, arrivals, packed = pl.pallas_call(
            lambda *refs: main_kernel(chunks, *refs),
            out_shape=(
                jax.ShapeDtypeStruct((1, ROWS, L), BF16),
                jax.ShapeDtypeStruct((1, ROWS, L), F32),
                jax.ShapeDtypeStruct((1, 2, MIG, L), BF16),
                jax.ShapeDtypeStruct((chunks, chunk_rows, L), BF16),
            ),
            in_specs=[smem] + vmem(13),
            out_specs=tuple(vmem(4)),
            scratch_shapes=[
                pltpu.VMEM((blocks, BLK, BLK), BF16),
                pltpu.VMEM((blocks, BLK, BLK), BF16),
                pltpu.VMEM((blocks, BLK, BLK), BF16),
                pltpu.VMEM((blocks, BLK, BLK), BF16),
                pltpu.VMEM((blocks, BLK, L), F32),
                pltpu.VMEM((blocks, BLK, 8), BF16),
                pltpu.VMEM((OWN_BLOCKS, 8, BLK), BF16),
                pltpu.VMEM((2, blocks, BLK, 2 * L), F32),
                pltpu.VMEM((ROWS, 2 * L), F32),
                pltpu.VMEM((2 * ROWS, 2 * L), F32),
            ],
            compiler_params=params,
            name="steps",
        )(pair_count, latents, cotangent, pairs, geometry, low, upp, *weights)

        got = lax.all_to_all(packed, group, 0, 0, tiled=True)
        got = lax.all_to_all(fold(got, n_z), "z", 0, 0, tiled=True)
        got = lax.all_to_all(fold(got, chunks), group, 0, 0, tiled=True)

        grads = pl.pallas_call(
            lambda *refs: unpack_kernel(chunks, *refs),
            out_shape=tuple(jax.ShapeDtypeStruct(w.shape, F32) for w in weights),
            in_specs=vmem(1),
            out_specs=tuple(vmem(7)),
            compiler_params=params,
            name="unpack",
        )(got)
        return (final, grad, arrivals) + tuple(grads)

    return jax.shard_map(
        on_device,
        mesh=fine,
        in_specs=(
            P("x", space, None),
            P("x", None, space),
            P("x", None, space),
            P("x", space),
            P("x", space, None),
            P("x", space, None),
        )
        + (P(),) * 7,
        out_specs=(P("x", space, None), P("x", space, None), P("x", space, None, None)) + (P(),) * 7,
        check_vma=False,
    )
```

```python
import jax
import jax.numpy as jnp
from jax import lax
from jax.experimental import pallas as pl
from jax.experimental.pallas import tpu as pltpu
from jax.sharding import Mesh, PartitionSpec as P


F32 = jnp.float32
BF16 = jnp.bfloat16
L = 128
ROWS = 256
EMAX = 1024
BLK = 256
OWN_BLOCKS = EMAX // BLK
SIDE = 256
NB_BLK = 2 * SIDE
NB_BLOCKS = EMAX // SIDE
CHUNK = 64
LAT_HALO = 128
COT_HALO = 64
SENT = LAT_HALO + COT_HALO + 64 + 16
D_AT = LAT_HALO + COT_HALO
X_AT = D_AT + 64
MIG = 16
MAIN = 768
EXTRA = 7
EPS = 1e-05
VMEM_LIMIT = 48 * 1024 * 1024


def dot(a, b):
    return jnp.dot(a, b, preferred_element_type=F32)


def dot_nt(a, b):
    return lax.dot_general(a, b, (((1,), (1,)), ((), ())), preferred_element_type=F32)


def dot_tn(a, b):
    return lax.dot_general(a, b, (((0,), (0,)), ((), ())), preferred_element_type=F32)


def place(row):
    below = row < 0
    above = row >= ROWS
    out = jnp.where(below, -1 - row, row - ROWS)
    block = lax.shift_right_arithmetic(out, 5)
    inner = jnp.where(below, row + 32 * (block + 1), row - ROWS - 32 * block + 32)
    outside = jnp.logical_or(below, above)
    return jnp.where(outside, 64 * block + inner, row), outside


def masked(flag):
    return jnp.where(flag, 1.0, 0.0).astype(BF16)


def pack_kernel(
    count_ref, lat_ref, cot_ref, pairs_ref, geo_ref, leav_ref, a_ref, b_ref, pairs_v, geo_v, leav_v, sems
):
    first = lax.axis_index("c") == 0
    copies = [
        pltpu.make_async_copy(pairs_ref.at[0], pairs_v, sems.at[0]),
        pltpu.make_async_copy(geo_ref.at[0], geo_v, sems.at[1]),
        pltpu.make_async_copy(leav_ref.at[0], leav_v, sems.at[2]),
    ]
    ups = (first, jnp.logical_not(first))
    for k, ref in enumerate((a_ref, b_ref)):
        lat_at = pl.multiple_of(jnp.where(ups[k], ROWS - LAT_HALO, 0), LAT_HALO)
        cot_at = pl.multiple_of(jnp.where(ups[k], ROWS - COT_HALO, 0), COT_HALO)
        lat = lat_ref.at[0, pl.ds(lat_at, LAT_HALO), :]
        cot = cot_ref.at[0, pl.ds(cot_at, COT_HALO), :]
        copies.append(pltpu.make_async_copy(lat, ref.at[pl.ds(0, LAT_HALO), :], sems.at[3 + 2 * k]))
        copies.append(pltpu.make_async_copy(cot, ref.at[pl.ds(LAT_HALO, COT_HALO), :], sems.at[4 + 2 * k]))
    for copy in copies:
        copy.start()
    for copy in copies[:3]:
        copy.wait()

    live = lax.broadcasted_iota(jnp.int32, (1, EMAX), 1) < count_ref[...]
    own = pairs_v[0:1, :]
    other = pairs_v[1:2, :]
    geo = geo_v[...].astype(F32)
    leav = leav_v[...].astype(F32)
    rows, kinds = [], []
    for k in range(2):
        up = ups[k]
        shift = jnp.where(up, -32 - ROWS, ROWS - 32)
        i_row = own + shift
        j_row = other + shift
        far = jnp.where(up, -1 - jnp.maximum(i_row, j_row), jnp.minimum(i_row, j_row) - ROWS)
        kind = jnp.where(far < 0, 0, lax.shift_right_arithmetic(far, 5) + 1)
        kind = jnp.where(jnp.logical_and(live, kind < 4), kind, 4).astype(F32)
        i_at, _ = place(i_row)
        j_at, j_hi = place(j_row)
        keep = kind < 3.5
        i_at = jnp.where(keep, i_at + 1, 0).astype(F32)
        j_at = jnp.where(keep, j_at + 1, 0).astype(F32)
        hi = jnp.where(j_hi, 1.0, 0.0).astype(F32)
        rows.append(jnp.concatenate([i_at, j_at, hi, jnp.ones((1, EMAX), F32), geo], axis=0).astype(BF16))
        kinds.append(jnp.concatenate([kind[:, 128 * t : 128 * t + 128] for t in range(8)], axis=0))

    flags = [jnp.where(kinds[k] == c, 1.0, 0.0).astype(F32) for k in range(2) for c in range(4)]
    marks = jnp.concatenate(flags, axis=0).astype(BF16)
    row_i = lax.broadcasted_iota(jnp.int32, (128, 128), 0)
    col_i = lax.broadcasted_iota(jnp.int32, (128, 128), 1)
    inside = dot(marks, masked(row_i < col_i))
    sums = dot(marks, jnp.ones((128, 128), BF16))
    row_b = lax.broadcasted_iota(jnp.int32, (64, 64), 0)
    col_b = lax.broadcasted_iota(jnp.int32, (64, 64), 1)
    same = lax.shift_right_logical(row_b, 5) == lax.shift_right_logical(col_b, 5)
    before = dot(masked(jnp.logical_and(same, col_b < row_b)), sums.astype(BF16))
    at = inside + before
    lane = lax.broadcasted_iota(jnp.int32, (1, 128), 1)
    col_w = lax.broadcasted_iota(jnp.int32, (128, BLK), 1).astype(F32)
    for k, ref in enumerate((a_ref, b_ref)):
        up = ups[k]
        rank = jnp.full((8, 128), -1.0, F32)
        for c in range(4):
            here = 32 * k + 8 * c
            rank = jnp.where(kinds[k] == c, at[here : here + 8, :], rank)
        by_slot = jnp.transpose(rank)
        ends = [before[32 * k + 8 * c + 7, 0] + sums[32 * k + 8 * c + 7, 0] for c in range(4)]
        trips = lax.shift_right_logical(ends[3].astype(jnp.int32) + (BLK - 1), 8)
        ref[D_AT:X_AT, :] = jnp.zeros((X_AT - D_AT, L), BF16)

        def body(t, carry, ref=ref, by_slot=by_slot, source=rows[k]):
            wanted = col_w + (t * BLK).astype(F32)
            picks = [masked(by_slot[:, q : q + 1] == wanted) for q in range(8)]
            moved = dot(source, jnp.concatenate(picks, axis=0))
            spot = pl.multiple_of(D_AT + 16 * t, 16)
            ref[pl.ds(spot, 16), :] = jnp.concatenate([moved[:, :128], moved[:, 128:]], axis=0).astype(BF16)
            return carry

        lax.fori_loop(0, trips, body, 0)
        movers = jnp.where(up, leav[1:2, :] - 224.0, leav[0:1, :] + 32.0)
        tail = jnp.concatenate([movers, jnp.zeros((1, 128 - MIG), F32)], axis=1)
        for c in range(4):
            blocks = ((ends[c].astype(jnp.int32) + (SIDE - 1)) // SIDE).astype(F32)
            tail = jnp.where(lane == MIG + c, blocks, tail)
        ref[X_AT:SENT, :] = jnp.broadcast_to(tail, (16, 128)).astype(BF16)
    for copy in copies[3:]:
        copy.wait()


def main_kernel(
    chunks,
    count_ref,
    lat_ref,
    cot_ref,
    pairs_ref,
    geo_ref,
    a_ref,
    b_ref,
    edge_in_ref,
    edge_bias_ref,
    edge_out_ref,
    node_in_ref,
    node_bias_ref,
    node_out_ref,
    gain_ref,
    final_ref,
    grad_ref,
    arr_ref,
    keep_ref,
    send_ref,
    low_ref,
    upp_ref,
    own_oh,
    own_oht,
    own_hi,
    own_col,
    own_row,
    own_slope,
    nb_rows,
    nb_oh,
    nb_oht,
    nb_hi,
    nb_col,
    nb_slope,
    work_x,
    work_p,
    work_d,
    work_e,
    t_nb,
    q_nb,
    stage,
):
    first = lax.axis_index("c") == 0

    @pl.when(first)
    def _():
        low_ref[...] = b_ref[...]
        upp_ref[...] = a_ref[...]

    @pl.when(jnp.logical_not(first))
    def _():
        low_ref[...] = a_ref[...]
        upp_ref[...] = b_ref[...]

    def one_hots(rows, cols, size):
        lanes = lax.broadcasted_iota(jnp.int32, (size, BLK), 1).astype(F32) + 1.0
        subs = lax.broadcasted_iota(jnp.int32, (BLK, size), 0).astype(F32) + 1.0
        straight = [masked(cols[:, k : k + 1] == lanes) for k in range(2)]
        turned = [masked(rows[k : k + 1, :] == subs) for k in range(2)]
        return straight, turned

    live = lax.broadcasted_iota(jnp.int32, (1, EMAX), 1) < count_ref[...]
    i_at = pairs_ref[0, 0:1, :] - 32
    j_at, j_out = place(pairs_ref[0, 1:2, :] - 32)
    own_rows = jnp.concatenate(
        [
            jnp.where(live, i_at + 1, 0).astype(F32),
            jnp.where(live, j_at + 1, 0).astype(F32),
            jnp.where(j_out, 1.0, 0.0).astype(F32),
            jnp.ones((1, EMAX), F32),
            geo_ref[0].astype(F32),
        ],
        axis=0,
    )
    own_row[...] = own_rows.astype(BF16)
    for k in range(OWN_BLOCKS):
        here = slice(BLK * k, BLK * k + BLK)
        rows = own_rows[:, here]
        cols = jnp.transpose(rows)
        straight, turned = one_hots(rows, cols, BLK)
        for e in range(2):
            own_oh[e, here, :] = straight[e]
            own_oht[e, :, here] = turned[e]
        own_hi[here, :] = jnp.broadcast_to(cols[:, 2:3], (BLK, L))
        own_col[here, :] = cols.astype(BF16)

    info = jnp.maximum(low_ref[X_AT:SENT, :].astype(F32), upp_ref[X_AT:SENT, :].astype(F32))[0:1, :]
    lane = lax.broadcasted_iota(jnp.int32, (1, L), 1)
    reach = [jnp.sum(jnp.where(lane == MIG + c, info, 0.0)).astype(jnp.int32) for c in range(4)]
    low_rows = low_ref[D_AT:X_AT, :].astype(F32)
    upp_rows = upp_ref[D_AT:X_AT, :].astype(F32)
    for k in range(NB_BLOCKS):
        pieces = [v[r : r + 8] for v in (low_rows, upp_rows) for r in range(SIDE // 16 * k, SIDE // 16 * (k + 1), 8)]
        nb_rows[k] = jnp.concatenate(pieces, axis=1)

    def prepare(k, carry):
        rows = nb_rows[k]
        cols = jnp.transpose(rows)
        straight, turned = one_hots(rows, cols, NB_BLK)
        for e in range(2):
            nb_oh[e, k] = straight[e]
            nb_oht[e, k] = turned[e]
        nb_hi[k] = jnp.broadcast_to(cols[:, 2:3], (NB_BLK, L))
        nb_col[k] = cols.astype(BF16)
        return carry

    lax.fori_loop(0, reach[3], prepare, 0)

    def around(source_low, source_upp, width, height):
        parts = []
        for b in range(width // 32):
            parts.append(source_low[width - 32 * (b + 1) : width - 32 * b])
            parts.append(source_upp[32 * b : 32 * b + 32])
        if height > 2 * width:
            parts.append(jnp.zeros((height - 2 * width, L), parts[0].dtype))
        return jnp.concatenate(parts, axis=0)

    def edge_weights(layer):
        top = edge_in_ref[layer, 0:L, :]
        bottom = edge_in_ref[layer, L : 2 * L, :]
        straight = jnp.concatenate([top, bottom], axis=1)
        return straight, jnp.concatenate([bottom, top], axis=1)

    def forward_block(size, oh_i, oh_j, hi, col, slope, i_source, both, weights, geo_weights, bias):
        work_x[0:size, :L] = dot(oh_i, i_source).astype(BF16)
        work_p[0:size, :] = dot(oh_j, both)
        for r in range(0, size, CHUNK):
            here = slice(r, r + CHUNK)
            is_hi = hi[here, :] > 0.5
            work_x[here, L:] = jnp.where(is_hi, work_p[here, L:], work_p[here, :L]).astype(BF16)
        work_p[0:size, :] = dot(work_x[0:size, :], weights) + dot(col, geo_weights)
        for r in range(0, size, CHUNK):
            here = slice(r, r + CHUNK)
            pre = work_p[here, :] + bias
            sig = 0.5 * jnp.tanh(0.5 * pre) + 0.5
            act = pre * sig
            slope[here, :] = sig + act * (1.0 - sig)
            diff = act[:, :L] - act[:, L:]
            is_hi = hi[here, :] > 0.5
            none = jnp.zeros_like(diff)
            work_d[here, :L] = diff.astype(BF16)
            work_e[here, :L] = jnp.where(is_hi, none, diff).astype(BF16)
            work_e[here, L:] = jnp.where(is_hi, diff, none).astype(BF16)

    def edge_forward(layer, h_lo, h_hi, nb_blocks):
        straight, crossed = edge_weights(layer)
        weights = jnp.concatenate([straight, crossed], axis=0)
        geo_top = edge_in_ref[layer, 2 * L : 2 * L + 4, :].astype(F32)
        geo_weights = jnp.concatenate(
            [jnp.zeros((4, 2 * L), F32), jnp.concatenate([geo_top, -geo_top], axis=1)], axis=0
        ).astype(BF16)
        bias_row = edge_bias_ref[layer : layer + 1, :]
        bias = jnp.concatenate([bias_row, bias_row], axis=1)
        both = jnp.concatenate([h_lo, h_hi], axis=1)
        t_nb[...] = jnp.zeros_like(t_nb)

        def body(k, carry):
            forward_block(
                NB_BLK, nb_oh[0, k], nb_oh[1, k], nb_hi.at[k], nb_col[k], nb_slope.at[layer, k],
                h_hi, both, weights, geo_weights, bias,
            )
            by_j = dot(nb_oht[1, k], work_e[0:NB_BLK, :])
            t_nb[:, :L] += -by_j[:, :L]
            t_nb[:, L:] += dot(nb_oht[0, k], work_d[0:NB_BLK, :L]) - by_j[:, L:]
            return carry

        lax.fori_loop(0, nb_blocks, body, 0)
        forward_block(
            EMAX, own_oh[0], own_oh[1], own_hi, own_col[...], own_slope.at[layer],
            h_lo, both, weights, geo_weights, bias,
        )
        by_j = dot(own_oht[1], work_e[...])
        return dot(own_oht[0], work_d[:, :L]) - by_j[:, :L], -by_j[:, L:]

    def node_forward(layer, h, total):
        agg = dot(total.astype(BF16), edge_out_ref[layer]).astype(BF16)
        joined = jnp.concatenate([h, agg], axis=1)
        pre = dot(joined, node_in_ref[layer]) + node_bias_ref[layer : layer + 1, :]
        sig = 0.5 * jnp.tanh(0.5 * pre) + 0.5
        act = pre * sig
        hidden = act.astype(BF16)
        out = dot(hidden, node_out_ref[layer])
        centred = out - jnp.mean(out, axis=1, keepdims=True)
        inv = lax.rsqrt(jnp.mean(centred * centred, axis=1, keepdims=True) + EPS)
        normed = centred * inv
        new = (h.astype(F32) + normed * gain_ref[layer : layer + 1, :]).astype(BF16)
        return new, (joined, sig + act * (1.0 - sig), hidden, normed, inv)

    def node_backward(layer, grad, kept):
        size = grad.shape[0]
        joined, node_slope, hidden, normed, inv = (v[:size] for v in kept)
        gain_term = jnp.sum(grad[:ROWS] * normed[:ROWS], axis=0, keepdims=True)
        dnorm = grad * gain_ref[layer : layer + 1, :]
        mean_a = jnp.mean(dnorm, axis=1, keepdims=True)
        mean_b = jnp.mean(dnorm * normed, axis=1, keepdims=True)
        dout = ((dnorm - mean_a - normed * mean_b) * inv).astype(BF16)
        out_term = dot_tn(hidden[:ROWS], dout[:ROWS])
        dpre = (dot_nt(dout, node_out_ref[layer]) * node_slope).astype(BF16)
        in_term = dot_tn(joined[:ROWS], dpre[:ROWS])
        bias_term = jnp.sum(dpre[:ROWS].astype(F32), axis=0, keepdims=True)
        dx = dot_nt(dpre, node_in_ref[layer])
        return grad + dx[:, :L], dx[:, L:].astype(BF16), (in_term, bias_term, out_term, gain_term)

    def backward_block(size, oh_i, oh_j, hi, slope, i_source, both):
        work_p[0:size, :] = dot(oh_j, both)
        at_i = dot(oh_i, i_source)
        for r in range(0, size, CHUNK):
            here = slice(r, r + CHUNK)
            is_hi = hi[here, :] > 0.5
            dd = at_i[here, :] - jnp.where(is_hi, work_p[here, L:], work_p[here, :L])
            dfwd = dd * slope[here, :L]
            drev = -dd * slope[here, L:]
            none = jnp.zeros_like(dfwd)
            work_d[here, :L] = dfwd.astype(BF16)
            work_d[here, L:] = drev.astype(BF16)
            work_x[here, :L] = jnp.where(is_hi, none, drev).astype(BF16)
            work_x[here, L:] = jnp.where(is_hi, none, dfwd).astype(BF16)
            work_e[here, :L] = jnp.where(is_hi, drev, none).astype(BF16)
            work_e[here, L:] = jnp.where(is_hi, dfwd, none).astype(BF16)

    def edge_backward(layer, e_lo, e_hi, nb_blocks, with_hi):
        both = jnp.concatenate([e_lo, e_hi], axis=1)
        q_nb[...] = jnp.zeros_like(q_nb)

        def body(k, carry):
            backward_block(NB_BLK, nb_oh[0, k], nb_oh[1, k], nb_hi.at[k], nb_slope.at[layer, k], e_hi, both)
            q_nb[0:ROWS, :] += dot(nb_oht[1, k], work_x[0:NB_BLK, :])
            if with_hi:
                q_nb[ROWS:, :] += dot(nb_oht[1, k], work_e[0:NB_BLK, :]) + dot(nb_oht[0, k], work_d[0:NB_BLK, :])
            return carry

        lax.fori_loop(0, nb_blocks, body, 0)
        backward_block(EMAX, own_oh[0], own_oh[1], own_hi, own_slope.at[layer], e_lo, both)
        q_lo = dot(own_oht[0], work_d[...]) + dot(own_oht[1], work_x[...])
        q_hi = dot(own_oht[1], work_e[...])
        return q_lo, q_hi, dot(own_row[...], work_d[...])

    h0_lo = lat_ref[0]
    h0_hi = around(low_ref[0:LAT_HALO, :], upp_ref[0:LAT_HALO, :], LAT_HALO, ROWS)
    t0_lo, t0_hi = edge_forward(0, h0_lo, h0_hi, reach[3])
    total0 = jnp.concatenate([t0_lo + t_nb[:, :L], t0_hi + t_nb[:, L:]], axis=0)
    h0 = jnp.concatenate([h0_lo, h0_hi], axis=0)
    h1, kept0 = node_forward(0, h0, total0)
    t1_lo, t1_hi = edge_forward(1, h1[:ROWS], h1[ROWS:], reach[2])
    near = ROWS + 2 * COT_HALO
    total1 = jnp.concatenate([t1_lo + t_nb[:, :L], t1_hi[: near - ROWS] + t_nb[: near - ROWS, L:]], axis=0)
    h2, kept1 = node_forward(1, h1[:near], total1)
    final_ref[0] = h2[:ROWS]

    few = lax.broadcasted_iota(jnp.int32, (MIG, 2 * COT_HALO), 1).astype(F32)
    for k, ref in ((0, upp_ref), (1, low_ref)):
        movers = jnp.transpose(ref[X_AT:SENT, :].astype(F32))[0:MIG, 0:1]
        arr_ref[0, k] = dot(masked(movers == few), h2[ROWS:]).astype(BF16)

    def with_zeros(value):
        return jnp.concatenate([value, jnp.zeros((2 * ROWS - value.shape[0],) + value.shape[1:], value.dtype)], axis=0)

    def layer_back(layer, grad, kept, own_total, h, nb_blocks, keep_rows):
        part, dagg, node_terms = node_backward(layer, grad, kept)
        spread = with_zeros(dagg)
        e = with_zeros(dot_nt(dagg, edge_out_ref[layer]).astype(BF16))
        q_lo, q_hi, geo = edge_backward(layer, e[:ROWS], e[ROWS:], nb_blocks, keep_rows > ROWS)
        out_term = dot_tn(own_total.astype(BF16), spread)
        q_own = jnp.concatenate([q_lo, q_hi], axis=0)
        in_term = dot_tn(h, q_own.astype(BF16))
        straight, _ = edge_weights(layer)
        q_all = (q_own[:keep_rows] + q_nb[:keep_rows, :]).astype(BF16)
        new = part[:keep_rows] + dot_nt(q_all, straight)
        return new, (in_term, geo, out_term) + node_terms

    own1 = jnp.concatenate([t1_lo, t1_hi], axis=0)
    own0 = jnp.concatenate([t0_lo, t0_hi], axis=0)
    cot = jnp.concatenate(
        [cot_ref[0], around(low_ref[LAT_HALO:D_AT, :], upp_ref[LAT_HALO:D_AT, :], COT_HALO, 2 * COT_HALO)], axis=0
    ).astype(F32)
    grad1, terms1 = layer_back(1, cot, kept1, own1, h1, reach[1], ROWS + 64)
    grad0, terms0 = layer_back(0, grad1, kept0, own0, h0, reach[0], ROWS)
    grad_ref[0] = grad0

    size = MAIN // chunks
    per = -(-EXTRA // chunks)
    for layer, terms in enumerate((terms0, terms1)):
        in_term, geo, out_term, node_in_term, node_bias_term, node_out_term, gain_term = terms
        stage[layer, :, size:, :] = jnp.zeros((chunks, stage.shape[2] - size, L), BF16)
        at = 0
        for value in (in_term[:, :L], in_term[:, L:], out_term, node_in_term, node_out_term):
            value = value.astype(BF16)
            while value.shape[0]:
                take = min(value.shape[0], size - at % size)
                stage[layer, at // size, at % size : at % size + take, :] = value[:take]
                value = value[take:]
                at += take
        small = [geo[4 + g : 5 + g, :L] - geo[4 + g : 5 + g, L:] for g in range(4)]
        small += [geo[3:4, :L] + geo[3:4, L:], node_bias_term, gain_term]
        for extra, value in enumerate(small):
            spot = size + extra % per
            stage[layer, extra // per, spot : spot + 1, :] = value.astype(BF16)

    @pl.when(first)
    def _():
        keep_ref[...] = stage[0]
        send_ref[...] = stage[1]

    @pl.when(jnp.logical_not(first))
    def _():
        keep_ref[...] = stage[1]
        send_ref[...] = stage[0]


def fold_kernel(copies, in_ref, out_ref):
    total = in_ref[0].astype(F32)
    for k in range(1, in_ref.shape[0]):
        total += in_ref[k].astype(F32)
    total = total.astype(BF16)
    for k in range(copies):
        out_ref[k] = total


def fold(array, copies):
    return pl.pallas_call(
        lambda a, b: fold_kernel(copies, a, b),
        out_shape=jax.ShapeDtypeStruct((copies,) + array.shape[1:], BF16),
        in_specs=[pl.BlockSpec(memory_space=pltpu.VMEM)],
        out_specs=pl.BlockSpec(memory_space=pltpu.VMEM),
        compiler_params=pltpu.CompilerParams(vmem_limit_bytes=VMEM_LIMIT),
        name="fold",
    )(array)


def add_kernel(a_ref, b_ref, out_ref):
    out_ref[...] = (a_ref[...].astype(F32) + b_ref[...].astype(F32)).astype(BF16)


def add(a, b):
    return pl.pallas_call(
        add_kernel,
        out_shape=jax.ShapeDtypeStruct(a.shape, BF16),
        in_specs=vmem(2),
        out_specs=pl.BlockSpec(memory_space=pltpu.VMEM),
        compiler_params=pltpu.CompilerParams(vmem_limit_bytes=VMEM_LIMIT),
        name="add",
    )(a, b)


def unpack_kernel(chunks, mine_ref, other_ref, *outs):
    def write(layer, ref):
        edge_in, edge_bias, edge_out, node_in, node_bias, node_out, gain = outs
        size = MAIN // chunks
        per = -(-EXTRA // chunks)
        at = 0
        for out, rows in ((edge_in, 2 * L), (edge_out, L), (node_in, 2 * L), (node_out, L)):
            r = 0
            while r < rows:
                take = min(rows - r, size - at % size)
                out[layer, r : r + take, :] = ref[at // size, at % size : at % size + take, :].astype(F32)
                r += take
                at += take
        small = []
        for extra in range(EXTRA):
            spot = size + extra % per
            small.append(ref[extra // per, spot : spot + 1, :].astype(F32))
        edge_in[layer, 2 * L : 2 * L + 4, :] = jnp.concatenate(small[:4], axis=0)
        edge_bias[layer : layer + 1, :] = small[4]
        node_bias[layer : layer + 1, :] = small[5]
        gain[layer : layer + 1, :] = small[6]

    first = lax.axis_index("c") == 0

    @pl.when(first)
    def _():
        write(0, mine_ref)
        write(1, other_ref)

    @pl.when(jnp.logical_not(first))
    def _():
        write(1, mine_ref)
        write(0, other_ref)


def vmem(count):
    return [pl.BlockSpec(memory_space=pltpu.VMEM)] * count


def solution(mesh):
    n_space = mesh.shape["space"]
    n_x = mesh.shape["replicas"]
    n_c = 2
    n_z = min(16, n_space // n_c)
    n_y = n_space // (n_c * n_z)
    n_l = 2 if n_z > 4 else 1
    n_h = n_z // n_l
    fine = Mesh(mesh.devices.reshape(n_y, n_h, n_l, n_c, n_x), ("y", "zh", "zl", "c", "x"))
    space = ("y", "zh", "zl", "c")
    group = ("y", "zl", "x")
    chunks = n_y * n_l * n_x
    size = MAIN // chunks
    chunk_rows = size + -(-(-(-EXTRA // chunks)) // 8) * 8
    params = pltpu.CompilerParams(vmem_limit_bytes=VMEM_LIMIT)

    def on_device(latents, pairs, geometry, pair_count, cotangent, leaving, *weights):
        sent = jax.ShapeDtypeStruct((SENT, L), BF16)
        to_a, to_b = pl.pallas_call(
            pack_kernel,
            out_shape=(sent, sent),
            in_specs=vmem(1) + [pl.BlockSpec(memory_space=pl.ANY)] * 5,
            out_specs=tuple(vmem(2)),
            scratch_shapes=[
                pltpu.VMEM((2, EMAX), jnp.int32),
                pltpu.VMEM((4, EMAX), BF16),
                pltpu.VMEM((2, MIG), jnp.int32),
                pltpu.SemaphoreType.DMA((7,)),
            ],
            compiler_params=pltpu.CompilerParams(vmem_limit_bytes=60 * 1024 * 1024),
            name="pack",
        )(pair_count, latents, cotangent, pairs, geometry, leaving)
        half = range(n_space // 2)
        near = [(2 * i, 2 * i + 1) for i in half]
        cross = [(2 * i + 1, (2 * i + 2) % n_space) for i in half]
        from_a = lax.ppermute(to_a, space, near + [(j, i) for i, j in near])
        from_b = lax.ppermute(to_b, space, cross + [(j, i) for i, j in cross])
        final, grad, arrivals, keep, send = pl.pallas_call(
            lambda *refs: main_kernel(chunks, *refs),
            out_shape=(
                jax.ShapeDtypeStruct((1, ROWS, L), BF16),
                jax.ShapeDtypeStruct((1, ROWS, L), F32),
                jax.ShapeDtypeStruct((1, 2, MIG, L), BF16),
                jax.ShapeDtypeStruct((chunks, chunk_rows, L), BF16),
                jax.ShapeDtypeStruct((chunks, chunk_rows, L), BF16),
            ),
            in_specs=vmem(14),
            out_specs=tuple(vmem(5)),
            scratch_shapes=[
                pltpu.VMEM((SENT, L), BF16),
                pltpu.VMEM((SENT, L), BF16),
                pltpu.VMEM((2, EMAX, ROWS), BF16),
                pltpu.VMEM((2, ROWS, EMAX), BF16),
                pltpu.VMEM((EMAX, L), F32),
                pltpu.VMEM((EMAX, 8), BF16),
                pltpu.VMEM((8, EMAX), BF16),
                pltpu.VMEM((2, EMAX, 2 * L), F32),
                pltpu.VMEM((NB_BLOCKS, 8, NB_BLK), F32),
                pltpu.VMEM((2, NB_BLOCKS, NB_BLK, ROWS), BF16),
                pltpu.VMEM((2, NB_BLOCKS, ROWS, NB_BLK), BF16),
                pltpu.VMEM((NB_BLOCKS, NB_BLK, L), F32),
                pltpu.VMEM((NB_BLOCKS, NB_BLK, 8), BF16),
                pltpu.VMEM((2, NB_BLOCKS, NB_BLK, 2 * L), F32),
                pltpu.VMEM((EMAX, 2 * L), BF16),
                pltpu.VMEM((EMAX, 2 * L), F32),
                pltpu.VMEM((EMAX, 2 * L), BF16),
                pltpu.VMEM((EMAX, 2 * L), BF16),
                pltpu.VMEM((ROWS, 2 * L), F32),
                pltpu.VMEM((2 * ROWS, 2 * L), F32),
                pltpu.VMEM((2, chunks, chunk_rows, L), BF16),
            ],
            compiler_params=params,
            name="steps",
        )(pair_count, latents, cotangent, pairs, geometry, from_a, from_b, *weights)

        swap = [(0, 1), (1, 0)]
        got = add(keep, lax.ppermute(send, "c", swap))
        got = lax.all_to_all(got, group, 0, 0, tiled=True)
        got = lax.all_to_all(fold(got, n_h), "zh", 0, 0, tiled=True)
        got = lax.all_to_all(fold(got, chunks), group, 0, 0, tiled=True)

        grads = pl.pallas_call(
            lambda *refs: unpack_kernel(chunks, *refs),
            out_shape=tuple(jax.ShapeDtypeStruct(w.shape, F32) for w in weights),
            in_specs=vmem(2),
            out_specs=tuple(vmem(7)),
            compiler_params=params,
            name="unpack",
        )(got, lax.ppermute(got, "c", swap))
        return (final, grad, arrivals) + tuple(grads)

    return jax.shard_map(
        on_device,
        mesh=fine,
        in_specs=(
            P("x", space, None),
            P("x", None, space),
            P("x", None, space),
            P("x", space),
            P("x", space, None),
            P("x", space, None),
        )
        + (P(),) * 7,
        out_specs=(P("x", space, None), P("x", space, None), P("x", space, None, None)) + (P(),) * 7,
        check_vma=False,
    )
```

```python
import jax
import jax.numpy as jnp
from jax import lax
from jax.experimental import pallas as pl
from jax.experimental.pallas import tpu as pltpu
from jax.sharding import Mesh, PartitionSpec as P


F32 = jnp.float32
BF16 = jnp.bfloat16
L = 128
ROWS = 256
EMAX = 1024
BLK = 256
OWN_BLOCKS = EMAX // BLK
SIDE = 128
NB_BLOCKS = EMAX // SIDE
ALL_PAIRS = EMAX + 2 * EMAX
SURE = (1, 2, 3, 4)
CHUNK = 64
LAT_HALO = 128
COT_HALO = 64
SENT = LAT_HALO + COT_HALO + 64 + 16
D_AT = LAT_HALO + COT_HALO
X_AT = D_AT + 64
MIG = 16
MAIN = 768
EXTRA = 7
EPS = 1e-05
VMEM_LIMIT = 48 * 1024 * 1024


def dot(a, b):
    return jnp.dot(a, b, preferred_element_type=F32)


def dot_nt(a, b):
    return lax.dot_general(a, b, (((1,), (1,)), ((), ())), preferred_element_type=F32)


def dot_tn(a, b):
    return lax.dot_general(a, b, (((0,), (0,)), ((), ())), preferred_element_type=F32)


def place(row):
    below = row < 0
    above = row >= ROWS
    out = jnp.where(below, -1 - row, row - ROWS)
    block = lax.shift_right_arithmetic(out, 5)
    inner = jnp.where(below, row + 32 * (block + 1), row - ROWS - 32 * block + 32)
    outside = jnp.logical_or(below, above)
    return jnp.where(outside, 64 * block + inner, row), outside


def masked(flag):
    return jnp.where(flag, 1.0, 0.0).astype(BF16)


def pack_kernel(
    count_ref, lat_ref, cot_ref, pairs_ref, geo_ref, leav_ref, a_ref, b_ref, pairs_v, geo_v, leav_v, sems
):
    first = lax.axis_index("c") == 0
    copies = [
        pltpu.make_async_copy(pairs_ref.at[0], pairs_v, sems.at[0]),
        pltpu.make_async_copy(geo_ref.at[0], geo_v, sems.at[1]),
        pltpu.make_async_copy(leav_ref.at[0], leav_v, sems.at[2]),
    ]
    ups = (first, jnp.logical_not(first))
    for k, ref in enumerate((a_ref, b_ref)):
        lat_at = pl.multiple_of(jnp.where(ups[k], ROWS - LAT_HALO, 0), LAT_HALO)
        cot_at = pl.multiple_of(jnp.where(ups[k], ROWS - COT_HALO, 0), COT_HALO)
        lat = lat_ref.at[0, pl.ds(lat_at, LAT_HALO), :]
        cot = cot_ref.at[0, pl.ds(cot_at, COT_HALO), :]
        copies.append(pltpu.make_async_copy(lat, ref.at[pl.ds(0, LAT_HALO), :], sems.at[3 + 2 * k]))
        copies.append(pltpu.make_async_copy(cot, ref.at[pl.ds(LAT_HALO, COT_HALO), :], sems.at[4 + 2 * k]))
    for copy in copies:
        copy.start()
    for copy in copies[:3]:
        copy.wait()

    live = lax.broadcasted_iota(jnp.int32, (1, EMAX), 1) < count_ref[...]
    own = pairs_v[0:1, :]
    other = pairs_v[1:2, :]
    geo = geo_v[...].astype(F32)
    leav = leav_v[...].astype(F32)
    rows, kinds = [], []
    for k in range(2):
        up = ups[k]
        shift = jnp.where(up, -32 - ROWS, ROWS - 32)
        i_row = own + shift
        j_row = other + shift
        far = jnp.where(up, -1 - jnp.maximum(i_row, j_row), jnp.minimum(i_row, j_row) - ROWS)
        kind = jnp.where(far < 0, 0, lax.shift_right_arithmetic(far, 5) + 1)
        kind = jnp.where(jnp.logical_and(live, kind < 4), kind, 4).astype(F32)
        i_at, _ = place(i_row)
        j_at, j_hi = place(j_row)
        keep = kind < 3.5
        i_at = jnp.where(keep, i_at + 1, 0).astype(F32)
        j_at = jnp.where(keep, j_at + 1, 0).astype(F32)
        hi = jnp.where(j_hi, 1.0, 0.0).astype(F32)
        rows.append(jnp.concatenate([i_at, j_at, hi, jnp.ones((1, EMAX), F32), geo], axis=0).astype(BF16))
        kinds.append(jnp.concatenate([kind[:, 128 * t : 128 * t + 128] for t in range(8)], axis=0))

    flags = [jnp.where(kinds[k] == c, 1.0, 0.0).astype(F32) for k in range(2) for c in range(4)]
    marks = jnp.concatenate(flags, axis=0).astype(BF16)
    row_i = lax.broadcasted_iota(jnp.int32, (128, 128), 0)
    col_i = lax.broadcasted_iota(jnp.int32, (128, 128), 1)
    inside = dot(marks, masked(row_i < col_i))
    sums = dot(marks, jnp.ones((128, 128), BF16))
    row_b = lax.broadcasted_iota(jnp.int32, (64, 64), 0)
    col_b = lax.broadcasted_iota(jnp.int32, (64, 64), 1)
    same = lax.shift_right_logical(row_b, 5) == lax.shift_right_logical(col_b, 5)
    before = dot(masked(jnp.logical_and(same, col_b < row_b)), sums.astype(BF16))
    at = inside + before
    lane = lax.broadcasted_iota(jnp.int32, (1, 128), 1)
    col_w = lax.broadcasted_iota(jnp.int32, (128, BLK), 1).astype(F32)
    for k, ref in enumerate((a_ref, b_ref)):
        up = ups[k]
        rank = jnp.full((8, 128), -1.0, F32)
        for c in range(4):
            here = 32 * k + 8 * c
            rank = jnp.where(kinds[k] == c, at[here : here + 8, :], rank)
        by_slot = jnp.transpose(rank)
        ends = [before[32 * k + 8 * c + 7, 0] + sums[32 * k + 8 * c + 7, 0] for c in range(4)]
        trips = lax.shift_right_logical(ends[3].astype(jnp.int32) + (BLK - 1), 8)
        ref[D_AT:X_AT, :] = jnp.zeros((X_AT - D_AT, L), BF16)

        def body(t, carry, ref=ref, by_slot=by_slot, source=rows[k]):
            wanted = col_w + (t * BLK).astype(F32)
            picks = [masked(by_slot[:, q : q + 1] == wanted) for q in range(8)]
            moved = dot(source, jnp.concatenate(picks, axis=0))
            spot = pl.multiple_of(D_AT + 16 * t, 16)
            ref[pl.ds(spot, 16), :] = jnp.concatenate([moved[:, :128], moved[:, 128:]], axis=0).astype(BF16)
            return carry

        lax.fori_loop(0, trips, body, 0)
        movers = jnp.where(up, leav[1:2, :] - 224.0, leav[0:1, :] + 32.0)
        tail = jnp.concatenate([movers, jnp.zeros((1, 128 - MIG), F32)], axis=1)
        for c in range(4):
            blocks = ((ends[c].astype(jnp.int32) + (SIDE - 1)) // SIDE).astype(F32)
            tail = jnp.where(lane == MIG + c, blocks, tail)
        ref[X_AT:SENT, :] = jnp.broadcast_to(tail, (16, 128)).astype(BF16)
    for copy in copies[3:]:
        copy.wait()


def main_kernel(
    chunks,
    count_ref,
    lat_ref,
    cot_ref,
    pairs_ref,
    geo_ref,
    a_ref,
    b_ref,
    edge_in_ref,
    edge_bias_ref,
    edge_out_ref,
    node_in_ref,
    node_bias_ref,
    node_out_ref,
    gain_ref,
    final_ref,
    grad_ref,
    arr_ref,
    keep_ref,
    send_ref,
    low_ref,
    upp_ref,
    oh,
    oht,
    hi,
    col,
    own_row,
    slope,
    nb_rows,
    work_x,
    work_p,
    work_d,
    work_e,
    work_s,
    t_nb,
    q_nb,
    stage,
):
    first = lax.axis_index("c") == 0

    @pl.when(first)
    def _():
        low_ref[...] = b_ref[...]
        upp_ref[...] = a_ref[...]

    @pl.when(jnp.logical_not(first))
    def _():
        low_ref[...] = a_ref[...]
        upp_ref[...] = b_ref[...]

    lanes = lax.broadcasted_iota(jnp.int32, (BLK, ROWS), 1).astype(F32) + 1.0
    subs = lax.broadcasted_iota(jnp.int32, (ROWS, BLK), 0).astype(F32) + 1.0

    live = lax.broadcasted_iota(jnp.int32, (1, EMAX), 1) < count_ref[...]
    i_at = pairs_ref[0, 0:1, :] - 32
    j_at, j_out = place(pairs_ref[0, 1:2, :] - 32)
    own_rows = jnp.concatenate(
        [
            jnp.where(live, i_at + 1, 0).astype(F32),
            jnp.where(live, j_at + 1, 0).astype(F32),
            jnp.where(j_out, 1.0, 0.0).astype(F32),
            jnp.ones((1, EMAX), F32),
            geo_ref[0].astype(F32),
        ],
        axis=0,
    )
    own_row[...] = own_rows.astype(BF16)

    def prepare(at, rows):
        here = pl.ds(at, BLK)
        cols = jnp.transpose(rows)
        for e in range(2):
            oh[e, here, :] = masked(cols[:, e : e + 1] == lanes)
            oht[e, :, here] = masked(rows[e : e + 1, :] == subs)
        hi[here, :] = jnp.broadcast_to(cols[:, 2:3], (BLK, L))
        col[here, :] = cols.astype(BF16)

    for k in range(OWN_BLOCKS):
        prepare(BLK * k, own_rows[:, BLK * k : BLK * k + BLK])

    info = jnp.maximum(low_ref[X_AT:SENT, :].astype(F32), upp_ref[X_AT:SENT, :].astype(F32))[0:1, :]
    lane = lax.broadcasted_iota(jnp.int32, (1, L), 1)
    reach = [jnp.sum(jnp.where(lane == MIG + c, info, 0.0)).astype(jnp.int32) for c in range(4)]
    low_rows = low_ref[D_AT:X_AT, :].astype(F32)
    upp_rows = upp_ref[D_AT:X_AT, :].astype(F32)
    for k in range(NB_BLOCKS):
        nb_rows[k] = jnp.concatenate([low_rows[8 * k : 8 * k + 8], upp_rows[8 * k : 8 * k + 8]], axis=1)
    for k in range(SURE[3]):
        prepare(EMAX + BLK * k, nb_rows[k])

    def further(last, body):
        def step(k, carry):
            body(pl.multiple_of(EMAX + BLK * k, BLK))
            return carry

        lax.fori_loop(SURE[last], reach[last], step, 0)

    further(3, lambda at: prepare(at, nb_rows[(at - EMAX) // BLK]))

    def around(source_low, source_upp, width, height):
        parts = []
        for b in range(width // 32):
            parts.append(source_low[width - 32 * (b + 1) : width - 32 * b])
            parts.append(source_upp[32 * b : 32 * b + 32])
        if height > 2 * width:
            parts.append(jnp.zeros((height - 2 * width, L), parts[0].dtype))
        return jnp.concatenate(parts, axis=0)

    def edge_weights(layer):
        top = edge_in_ref[layer, 0:L, :]
        bottom = edge_in_ref[layer, L : 2 * L, :]
        straight = jnp.concatenate([top, bottom], axis=1)
        return straight, jnp.concatenate([bottom, top], axis=1)

    def chunks_of(at, size):
        return [pl.ds(at + r, CHUNK) for r in range(0, size, CHUNK)]

    def forward_rows(layer, parts, both, weights, geo_weights, bias):
        for at, size, source in parts:
            work_x[pl.ds(at, size), :L] = dot(oh[0, pl.ds(at, size), :], source).astype(BF16)
        at = parts[0][0]
        size = sum(part[1] for part in parts)
        rows = pl.ds(at, size)
        work_p[rows, :] = dot(oh[1, rows, :], both)
        for here in chunks_of(at, size):
            is_hi = hi[here, :] > 0.5
            work_x[here, L:] = jnp.where(is_hi, work_p[here, L:], work_p[here, :L]).astype(BF16)
        work_p[rows, :] = dot(work_x[rows, :], weights) + dot(col[rows, :], geo_weights)
        for here in chunks_of(at, size):
            pre = work_p[here, :] + bias
            sig = 0.5 * jnp.tanh(0.5 * pre) + 0.5
            act = pre * sig
            slope[layer, here, :] = sig + act * (1.0 - sig)
            diff = act[:, :L] - act[:, L:]
            is_hi = hi[here, :] > 0.5
            none = jnp.zeros_like(diff)
            work_d[here, :L] = diff.astype(BF16)
            work_e[here, :L] = jnp.where(is_hi, none, diff).astype(BF16)
            work_e[here, L:] = jnp.where(is_hi, diff, none).astype(BF16)

    def edge_forward(layer, h_lo, h_hi, last):
        straight, crossed = edge_weights(layer)
        weights = jnp.concatenate([straight, crossed], axis=0)
        geo_top = edge_in_ref[layer, 2 * L : 2 * L + 4, :].astype(F32)
        geo_weights = jnp.concatenate(
            [jnp.zeros((4, 2 * L), F32), jnp.concatenate([geo_top, -geo_top], axis=1)], axis=0
        ).astype(BF16)
        bias_row = edge_bias_ref[layer : layer + 1, :]
        bias = jnp.concatenate([bias_row, bias_row], axis=1)
        both = jnp.concatenate([h_lo, h_hi], axis=1)
        t_nb[...] = jnp.zeros_like(t_nb)

        def collect(at, size):
            rows = pl.ds(at, size)
            by_j = dot(oht[1, :, rows], work_e[rows, :])
            return dot(oht[0, :, rows], work_d[rows, :L]), by_j

        def more(at):
            forward_rows(layer, [(at, BLK, h_hi)], both, weights, geo_weights, bias)
            by_i, by_j = collect(at, BLK)
            t_nb[:, :L] += -by_j[:, :L]
            t_nb[:, L:] += by_i - by_j[:, L:]

        further(last, more)
        sure = BLK * SURE[last]
        forward_rows(layer, [(0, EMAX, h_lo), (EMAX, sure, h_hi)], both, weights, geo_weights, bias)
        by_i, by_j = collect(0, EMAX)
        nb_i, nb_j = collect(EMAX, sure)
        own = (by_i - by_j[:, :L], -by_j[:, L:])
        total = (own[0] - nb_j[:, :L] + t_nb[:, :L], own[1] + nb_i - nb_j[:, L:] + t_nb[:, L:])
        return own, total

    def node_forward(layer, h, total):
        agg = dot(total.astype(BF16), edge_out_ref[layer]).astype(BF16)
        joined = jnp.concatenate([h, agg], axis=1)
        pre = dot(joined, node_in_ref[layer]) + node_bias_ref[layer : layer + 1, :]
        sig = 0.5 * jnp.tanh(0.5 * pre) + 0.5
        act = pre * sig
        hidden = act.astype(BF16)
        out = dot(hidden, node_out_ref[layer])
        centred = out - jnp.mean(out, axis=1, keepdims=True)
        inv = lax.rsqrt(jnp.mean(centred * centred, axis=1, keepdims=True) + EPS)
        normed = centred * inv
        new = (h.astype(F32) + normed * gain_ref[layer : layer + 1, :]).astype(BF16)
        return new, (joined, sig + act * (1.0 - sig), hidden, normed, inv)

    def node_backward(layer, grad, kept):
        size = grad.shape[0]
        joined, node_slope, hidden, normed, inv = (v[:size] for v in kept)
        gain_term = jnp.sum(grad[:ROWS] * normed[:ROWS], axis=0, keepdims=True)
        dnorm = grad * gain_ref[layer : layer + 1, :]
        mean_a = jnp.mean(dnorm, axis=1, keepdims=True)
        mean_b = jnp.mean(dnorm * normed, axis=1, keepdims=True)
        dout = ((dnorm - mean_a - normed * mean_b) * inv).astype(BF16)
        out_term = dot_tn(hidden[:ROWS], dout[:ROWS])
        dpre = (dot_nt(dout, node_out_ref[layer]) * node_slope).astype(BF16)
        in_term = dot_tn(joined[:ROWS], dpre[:ROWS])
        bias_term = jnp.sum(dpre[:ROWS].astype(F32), axis=0, keepdims=True)
        dx = dot_nt(dpre, node_in_ref[layer])
        return grad + dx[:, :L], dx[:, L:].astype(BF16), (in_term, bias_term, out_term, gain_term)

    def backward_rows(layer, parts, both):
        for at, size, source in parts:
            work_s[pl.ds(at, size), :] = dot(oh[0, pl.ds(at, size), :], source)
        at = parts[0][0]
        size = sum(part[1] for part in parts)
        rows = pl.ds(at, size)
        work_p[rows, :] = dot(oh[1, rows, :], both)
        for here in chunks_of(at, size):
            is_hi = hi[here, :] > 0.5
            dd = work_s[here, :] - jnp.where(is_hi, work_p[here, L:], work_p[here, :L])
            dfwd = dd * slope[layer, here, :L]
            drev = -dd * slope[layer, here, L:]
            none = jnp.zeros_like(dfwd)
            work_d[here, :L] = dfwd.astype(BF16)
            work_d[here, L:] = drev.astype(BF16)
            work_x[here, :L] = jnp.where(is_hi, none, drev).astype(BF16)
            work_x[here, L:] = jnp.where(is_hi, none, dfwd).astype(BF16)
            work_e[here, :L] = jnp.where(is_hi, drev, none).astype(BF16)
            work_e[here, L:] = jnp.where(is_hi, dfwd, none).astype(BF16)

    def edge_backward(layer, e_lo, e_hi, last):
        both = jnp.concatenate([e_lo, e_hi], axis=1)
        q_nb[...] = jnp.zeros_like(q_nb)

        def nb_collect(at, size):
            rows = pl.ds(at, size)
            lo = dot(oht[1, :, rows], work_x[rows, :])
            if last == 0:
                return lo, None
            return lo, dot(oht[1, :, rows], work_e[rows, :]) + dot(oht[0, :, rows], work_d[rows, :])

        def more(at):
            backward_rows(layer, [(at, BLK, e_hi)], both)
            lo, up = nb_collect(at, BLK)
            q_nb[0:ROWS, :] += lo
            if last:
                q_nb[ROWS:, :] += up

        further(last, more)
        sure = BLK * SURE[last]
        backward_rows(layer, [(0, EMAX, e_lo), (EMAX, sure, e_hi)], both)
        rows = pl.ds(0, EMAX)
        q_lo = dot(oht[0, :, rows], work_d[rows, :]) + dot(oht[1, :, rows], work_x[rows, :])
        q_hi = dot(oht[1, :, rows], work_e[rows, :])
        nb_lo, nb_up = nb_collect(EMAX, sure)
        own = jnp.concatenate([q_lo, q_hi], axis=0)
        if last == 0:
            total = q_lo + nb_lo + q_nb[0:ROWS, :]
        else:
            total = own + jnp.concatenate([nb_lo, nb_up], axis=0) + q_nb[...]
        return own, total, dot(own_row[...], work_d[rows, :])

    h0_lo = lat_ref[0]
    h0_hi = around(low_ref[0:LAT_HALO, :], upp_ref[0:LAT_HALO, :], LAT_HALO, ROWS)
    own0, total0 = (jnp.concatenate(t, axis=0) for t in edge_forward(0, h0_lo, h0_hi, 3))
    h0 = jnp.concatenate([h0_lo, h0_hi], axis=0)
    h1, kept0 = node_forward(0, h0, total0)
    own1, total1 = (jnp.concatenate(t, axis=0) for t in edge_forward(1, h1[:ROWS], h1[ROWS:], 2))
    near = ROWS + 2 * COT_HALO
    h2, kept1 = node_forward(1, h1[:near], total1[:near])
    final_ref[0] = h2[:ROWS]

    few = lax.broadcasted_iota(jnp.int32, (MIG, 2 * COT_HALO), 1).astype(F32)
    for k, ref in ((0, upp_ref), (1, low_ref)):
        movers = jnp.transpose(ref[X_AT:SENT, :].astype(F32))[0:MIG, 0:1]
        arr_ref[0, k] = dot(masked(movers == few), h2[ROWS:]).astype(BF16)

    def with_zeros(value):
        return jnp.concatenate([value, jnp.zeros((2 * ROWS - value.shape[0],) + value.shape[1:], value.dtype)], axis=0)

    def layer_back(layer, grad, kept, own_total, h, last, keep_rows):
        part, dagg, node_terms = node_backward(layer, grad, kept)
        spread = with_zeros(dagg)
        e = with_zeros(dot_nt(dagg, edge_out_ref[layer]).astype(BF16))
        q_own, q_all, geo = edge_backward(layer, e[:ROWS], e[ROWS:], last)
        out_term = dot_tn(own_total.astype(BF16), spread)
        in_term = dot_tn(h, q_own.astype(BF16))
        straight, _ = edge_weights(layer)
        new = part[:keep_rows] + dot_nt(q_all[:keep_rows].astype(BF16), straight)
        return new, (in_term, geo, out_term) + node_terms

    cot = jnp.concatenate(
        [cot_ref[0], around(low_ref[LAT_HALO:D_AT, :], upp_ref[LAT_HALO:D_AT, :], COT_HALO, 2 * COT_HALO)], axis=0
    ).astype(F32)
    grad1, terms1 = layer_back(1, cot, kept1, own1, h1, 1, ROWS + 64)
    grad0, terms0 = layer_back(0, grad1, kept0, own0, h0, 0, ROWS)
    grad_ref[0] = grad0

    size = MAIN // chunks
    per = -(-EXTRA // chunks)
    for layer, terms in enumerate((terms0, terms1)):
        in_term, geo, out_term, node_in_term, node_bias_term, node_out_term, gain_term = terms
        stage[layer, :, size:, :] = jnp.zeros((chunks, stage.shape[2] - size, L), BF16)
        at = 0
        for value in (in_term[:, :L], in_term[:, L:], out_term, node_in_term, node_out_term):
            value = value.astype(BF16)
            while value.shape[0]:
                take = min(value.shape[0], size - at % size)
                stage[layer, at // size, at % size : at % size + take, :] = value[:take]
                value = value[take:]
                at += take
        small = [geo[4 + g : 5 + g, :L] - geo[4 + g : 5 + g, L:] for g in range(4)]
        small += [geo[3:4, :L] + geo[3:4, L:], node_bias_term, gain_term]
        for extra, value in enumerate(small):
            spot = size + extra % per
            stage[layer, extra // per, spot : spot + 1, :] = value.astype(BF16)

    @pl.when(first)
    def _():
        keep_ref[...] = stage[0]
        send_ref[...] = stage[1]

    @pl.when(jnp.logical_not(first))
    def _():
        keep_ref[...] = stage[1]
        send_ref[...] = stage[0]


def fold_kernel(copies, in_ref, out_ref):
    total = in_ref[0].astype(F32)
    for k in range(1, in_ref.shape[0]):
        total += in_ref[k].astype(F32)
    total = total.astype(BF16)
    for k in range(copies):
        out_ref[k] = total


def fold(array, copies):
    return pl.pallas_call(
        lambda a, b: fold_kernel(copies, a, b),
        out_shape=jax.ShapeDtypeStruct((copies,) + array.shape[1:], BF16),
        in_specs=[pl.BlockSpec(memory_space=pltpu.VMEM)],
        out_specs=pl.BlockSpec(memory_space=pltpu.VMEM),
        compiler_params=pltpu.CompilerParams(vmem_limit_bytes=VMEM_LIMIT),
        name="fold",
    )(array)


def add_kernel(a_ref, b_ref, out_ref):
    out_ref[...] = (a_ref[...].astype(F32) + b_ref[...].astype(F32)).astype(BF16)


def add(a, b):
    return pl.pallas_call(
        add_kernel,
        out_shape=jax.ShapeDtypeStruct(a.shape, BF16),
        in_specs=vmem(2),
        out_specs=pl.BlockSpec(memory_space=pltpu.VMEM),
        compiler_params=pltpu.CompilerParams(vmem_limit_bytes=VMEM_LIMIT),
        name="add",
    )(a, b)


def unpack_kernel(chunks, mine_ref, other_ref, *outs):
    def write(layer, ref):
        edge_in, edge_bias, edge_out, node_in, node_bias, node_out, gain = outs
        size = MAIN // chunks
        per = -(-EXTRA // chunks)
        at = 0
        for out, rows in ((edge_in, 2 * L), (edge_out, L), (node_in, 2 * L), (node_out, L)):
            r = 0
            while r < rows:
                take = min(rows - r, size - at % size)
                value = ref[at // size, at % size : at % size + take, :].astype(F32)
                if out is edge_in:
                    out[pl.ds(2 * r + layer, take, stride=2), :] = value
                else:
                    out[layer, r : r + take, :] = value
                r += take
                at += take
        small = []
        for extra in range(EXTRA):
            spot = size + extra % per
            small.append(ref[extra // per, spot : spot + 1, :].astype(F32))
        for g in range(4):
            edge_in[4 * L + 2 * g + layer : 4 * L + 2 * g + layer + 1, :] = small[g]
        edge_bias[layer : layer + 1, :] = small[4]
        node_bias[layer : layer + 1, :] = small[5]
        gain[layer : layer + 1, :] = small[6]

    first = lax.axis_index("c") == 0

    @pl.when(first)
    def _():
        write(0, mine_ref)
        write(1, other_ref)

    @pl.when(jnp.logical_not(first))
    def _():
        write(1, mine_ref)
        write(0, other_ref)


def vmem(count):
    return [pl.BlockSpec(memory_space=pltpu.VMEM)] * count


def solution(mesh):
    n_space = mesh.shape["space"]
    n_x = mesh.shape["replicas"]
    n_c = 2
    n_z = min(16, n_space // n_c)
    n_y = n_space // (n_c * n_z)
    n_l = 2 if n_z > 4 else 1
    n_h = n_z // n_l
    fine = Mesh(mesh.devices.reshape(n_y, n_h, n_l, n_c, n_x), ("y", "zh", "zl", "c", "x"))
    space = ("y", "zh", "zl", "c")
    group = ("y", "zl", "x")
    chunks = n_y * n_l * n_x
    size = MAIN // chunks
    chunk_rows = size + -(-(-(-EXTRA // chunks)) // 8) * 8
    params = pltpu.CompilerParams(vmem_limit_bytes=VMEM_LIMIT)

    def on_device(latents, pairs, geometry, pair_count, cotangent, leaving, *weights):
        sent = jax.ShapeDtypeStruct((SENT, L), BF16)
        to_a, to_b = pl.pallas_call(
            pack_kernel,
            out_shape=(sent, sent),
            in_specs=vmem(1) + [pl.BlockSpec(memory_space=pl.ANY)] * 5,
            out_specs=tuple(vmem(2)),
            scratch_shapes=[
                pltpu.VMEM((2, EMAX), jnp.int32),
                pltpu.VMEM((4, EMAX), BF16),
                pltpu.VMEM((2, MIG), jnp.int32),
                pltpu.SemaphoreType.DMA((7,)),
            ],
            compiler_params=pltpu.CompilerParams(vmem_limit_bytes=60 * 1024 * 1024),
            name="pack",
        )(pair_count, latents, cotangent, pairs, geometry, leaving)
        half = range(n_space // 2)
        near = [(2 * i, 2 * i + 1) for i in half]
        cross = [(2 * i + 1, (2 * i + 2) % n_space) for i in half]
        from_a = lax.ppermute(to_a, space, near + [(j, i) for i, j in near])
        from_b = lax.ppermute(to_b, space, cross + [(j, i) for i, j in cross])
        final, grad, arrivals, keep, send = pl.pallas_call(
            lambda *refs: main_kernel(chunks, *refs),
            out_shape=(
                jax.ShapeDtypeStruct((1, ROWS, L), BF16),
                jax.ShapeDtypeStruct((1, ROWS, L), F32),
                jax.ShapeDtypeStruct((1, 2, MIG, L), BF16),
                jax.ShapeDtypeStruct((chunks, chunk_rows, L), BF16),
                jax.ShapeDtypeStruct((chunks, chunk_rows, L), BF16),
            ),
            in_specs=vmem(14),
            out_specs=tuple(vmem(5)),
            scratch_shapes=[
                pltpu.VMEM((SENT, L), BF16),
                pltpu.VMEM((SENT, L), BF16),
                pltpu.VMEM((2, ALL_PAIRS, ROWS), BF16),
                pltpu.VMEM((2, ROWS, ALL_PAIRS), BF16),
                pltpu.VMEM((ALL_PAIRS, L), F32),
                pltpu.VMEM((ALL_PAIRS, 8), BF16),
                pltpu.VMEM((8, EMAX), BF16),
                pltpu.VMEM((2, ALL_PAIRS, 2 * L), F32),
                pltpu.VMEM((NB_BLOCKS, 8, BLK), F32),
                pltpu.VMEM((ALL_PAIRS, 2 * L), BF16),
                pltpu.VMEM((ALL_PAIRS, 2 * L), F32),
                pltpu.VMEM((ALL_PAIRS, 2 * L), BF16),
                pltpu.VMEM((ALL_PAIRS, 2 * L), BF16),
                pltpu.VMEM((ALL_PAIRS, L), F32),
                pltpu.VMEM((ROWS, 2 * L), F32),
                pltpu.VMEM((2 * ROWS, 2 * L), F32),
                pltpu.VMEM((2, chunks, chunk_rows, L), BF16),
            ],
            compiler_params=params,
            name="steps",
        )(pair_count, latents, cotangent, pairs, geometry, from_a, from_b, *weights)

        swap = [(0, 1), (1, 0)]
        got = add(keep, lax.ppermute(send, "c", swap))
        got = lax.all_to_all(got, group, 0, 0, tiled=True)
        got = lax.all_to_all(fold(got, n_h), "zh", 0, 0, tiled=True)
        got = lax.all_to_all(fold(got, chunks), group, 0, 0, tiled=True)

        grads = pl.pallas_call(
            lambda *refs: unpack_kernel(chunks, *refs),
            out_shape=(jax.ShapeDtypeStruct((2 * weights[0].shape[1], L), F32),)
            + tuple(jax.ShapeDtypeStruct(w.shape, F32) for w in weights[1:]),
            in_specs=vmem(2),
            out_specs=tuple(vmem(7)),
            compiler_params=params,
            name="unpack",
        )(got, lax.ppermute(got, "c", swap))
        edge_in_grad = jnp.transpose(grads[0].reshape(-1, 2, L), (1, 0, 2))
        return (final, grad, arrivals, edge_in_grad) + tuple(grads[1:])

    return jax.shard_map(
        on_device,
        mesh=fine,
        in_specs=(
            P("x", space, None),
            P("x", None, space),
            P("x", None, space),
            P("x", space),
            P("x", space, None),
            P("x", space, None),
        )
        + (P(),) * 7,
        out_specs=(P("x", space, None), P("x", space, None), P("x", space, None, None)) + (P(),) * 7,
        check_vma=False,
    )
```

```python
import jax
import jax.numpy as jnp
from jax import lax
from jax.experimental import pallas as pl
from jax.experimental.pallas import tpu as pltpu
from jax.sharding import Mesh, PartitionSpec as P


F32 = jnp.float32
BF16 = jnp.bfloat16
L = 128
ROWS = 256
EMAX = 1024
BLK = 256
OWN_BLOCKS = EMAX // BLK
SIDE = 128
NB_BLOCKS = EMAX // SIDE
ALL_PAIRS = EMAX + 2 * EMAX
SURE = (1, 2, 3, 4)
CHUNK = 64
LAT_HALO = 128
COT_HALO = 64
SENT = LAT_HALO + COT_HALO + 64 + 16
D_AT = LAT_HALO + COT_HALO
X_AT = D_AT + 64
MIG = 16
MAIN = 768
EXTRA = 7
EPS = 1e-05
VMEM_LIMIT = 48 * 1024 * 1024


def dot(a, b):
    return jnp.dot(a, b, preferred_element_type=F32)


def dot_nt(a, b):
    return lax.dot_general(a, b, (((1,), (1,)), ((), ())), preferred_element_type=F32)


def dot_tn(a, b):
    return lax.dot_general(a, b, (((0,), (0,)), ((), ())), preferred_element_type=F32)


def place(row):
    below = row < 0
    above = row >= ROWS
    out = jnp.where(below, -1 - row, row - ROWS)
    block = lax.shift_right_arithmetic(out, 5)
    inner = jnp.where(below, row + 32 * (block + 1), row - ROWS - 32 * block + 32)
    outside = jnp.logical_or(below, above)
    return jnp.where(outside, 64 * block + inner, row), outside


def masked(flag):
    return jnp.where(flag, 1.0, 0.0).astype(BF16)


def pack_kernel(
    count_ref, lat_ref, cot_ref, pairs_ref, geo_ref, leav_ref, a_ref, b_ref, count_v, pairs_v, geo_v, leav_v, sems
):
    first = lax.axis_index("c") == 0
    copies = [
        pltpu.make_async_copy(pairs_ref.at[0], pairs_v, sems.at[0]),
        pltpu.make_async_copy(geo_ref.at[0], geo_v, sems.at[1]),
        pltpu.make_async_copy(leav_ref.at[0], leav_v, sems.at[2]),
        pltpu.make_async_copy(count_ref, count_v, sems.at[7]),
    ]
    ups = (first, jnp.logical_not(first))
    for k, ref in enumerate((a_ref, b_ref)):
        lat_at = pl.multiple_of(jnp.where(ups[k], ROWS - LAT_HALO, 0), LAT_HALO)
        cot_at = pl.multiple_of(jnp.where(ups[k], ROWS - COT_HALO, 0), COT_HALO)
        lat = lat_ref.at[0, pl.ds(lat_at, LAT_HALO), :]
        cot = cot_ref.at[0, pl.ds(cot_at, COT_HALO), :]
        copies.append(pltpu.make_async_copy(lat, ref.at[pl.ds(0, LAT_HALO), :], sems.at[3 + 2 * k]))
        copies.append(pltpu.make_async_copy(cot, ref.at[pl.ds(LAT_HALO, COT_HALO), :], sems.at[4 + 2 * k]))
    for copy in copies:
        copy.start()
    for copy in copies[:4]:
        copy.wait()

    live = lax.broadcasted_iota(jnp.int32, (1, EMAX), 1) < count_v[...]
    own = pairs_v[0:1, :]
    other = pairs_v[1:2, :]
    geo = geo_v[...].astype(F32)
    leav = leav_v[...].astype(F32)
    rows, kinds = [], []
    for k in range(2):
        up = ups[k]
        shift = jnp.where(up, -32 - ROWS, ROWS - 32)
        i_row = own + shift
        j_row = other + shift
        far = jnp.where(up, -1 - jnp.maximum(i_row, j_row), jnp.minimum(i_row, j_row) - ROWS)
        kind = jnp.where(far < 0, 0, lax.shift_right_arithmetic(far, 5) + 1)
        kind = jnp.where(jnp.logical_and(live, kind < 4), kind, 4).astype(F32)
        i_at, _ = place(i_row)
        j_at, j_hi = place(j_row)
        keep = kind < 3.5
        i_at = jnp.where(keep, i_at + 1, 0).astype(F32)
        j_at = jnp.where(keep, j_at + 1, 0).astype(F32)
        hi = jnp.where(j_hi, 1.0, 0.0).astype(F32)
        rows.append(jnp.concatenate([i_at, j_at, hi, jnp.ones((1, EMAX), F32), geo], axis=0).astype(BF16))
        kinds.append(jnp.concatenate([kind[:, 128 * t : 128 * t + 128] for t in range(8)], axis=0))

    flags = [jnp.where(kinds[k] == c, 1.0, 0.0).astype(F32) for k in range(2) for c in range(4)]
    marks = jnp.concatenate(flags, axis=0).astype(BF16)
    row_i = lax.broadcasted_iota(jnp.int32, (128, 128), 0)
    col_i = lax.broadcasted_iota(jnp.int32, (128, 128), 1)
    inside = dot(marks, masked(row_i < col_i))
    sums = dot(marks, jnp.ones((128, 128), BF16))
    row_b = lax.broadcasted_iota(jnp.int32, (64, 64), 0)
    col_b = lax.broadcasted_iota(jnp.int32, (64, 64), 1)
    same = lax.shift_right_logical(row_b, 5) == lax.shift_right_logical(col_b, 5)
    before = dot(masked(jnp.logical_and(same, col_b < row_b)), sums.astype(BF16))
    at = inside + before
    lane = lax.broadcasted_iota(jnp.int32, (1, 128), 1)
    col_w = lax.broadcasted_iota(jnp.int32, (128, BLK), 1).astype(F32)
    places = []
    for k in range(2):
        rank = jnp.full((8, 128), -1.0, F32)
        for c in range(4):
            here = 32 * k + 8 * c
            rank = jnp.where(kinds[k] == c, at[here : here + 8, :], rank)
        places.append(jnp.transpose(rank))

    def move(k, t, shift):
        picks = [masked(places[k][:, q : q + 1] == col_w + shift) for q in range(8)]
        moved = dot(rows[k], jnp.concatenate(picks, axis=0))
        ref = (a_ref, b_ref)[k]
        spot = D_AT + 16 * t
        if not isinstance(t, int):
            spot = pl.multiple_of(spot, 16)
        ref[pl.ds(spot, 16), :] = jnp.concatenate([moved[:, :128], moved[:, 128:]], axis=0).astype(BF16)

    for t in range(2):
        for k in range(2):
            move(k, t, float(BLK * t))
    for k, ref in enumerate((a_ref, b_ref)):
        up = ups[k]
        ends = [before[32 * k + 8 * c + 7, 0] + sums[32 * k + 8 * c + 7, 0] for c in range(4)]
        trips = lax.shift_right_logical(ends[3].astype(jnp.int32) + (BLK - 1), 8)
        ref[D_AT + 32 : X_AT, :] = jnp.zeros((X_AT - D_AT - 32, L), BF16)

        def body(t, carry, k=k):
            move(k, t, (t * BLK).astype(F32))
            return carry

        lax.fori_loop(2, trips, body, 0)
        movers = jnp.where(up, leav[1:2, :] - 224.0, leav[0:1, :] + 32.0)
        tail = jnp.concatenate([movers, jnp.zeros((1, 128 - MIG), F32)], axis=1)
        for c in range(4):
            blocks = ((ends[c].astype(jnp.int32) + (SIDE - 1)) // SIDE).astype(F32)
            tail = jnp.where(lane == MIG + c, blocks, tail)
        ref[X_AT:SENT, :] = jnp.broadcast_to(tail, (16, 128)).astype(BF16)
    for copy in copies[4:]:
        copy.wait()


def grids():
    lanes = lax.broadcasted_iota(jnp.int32, (BLK, ROWS), 1).astype(F32) + 1.0
    subs = lax.broadcasted_iota(jnp.int32, (ROWS, BLK), 0).astype(F32) + 1.0
    return lanes, subs


def set_block(at, rows, lanes, subs, oh, oht, hi, col):
    here = pl.ds(at, BLK)
    cols = jnp.transpose(rows)
    for e in range(2):
        oh[e, here, :] = masked(cols[:, e : e + 1] == lanes)
        oht[e, :, here] = masked(rows[e : e + 1, :] == subs)
    hi[here, :] = jnp.broadcast_to(cols[:, 2:3], (BLK, L))
    col[here, :] = cols.astype(BF16)


def own_kernel(count_ref, pairs_ref, geo_ref, bias_e, bias_n, gain, oh, oht, hi, col, row, bias_e_out, bias_n_out, gain_out):
    bias_e_out[...] = bias_e[...]
    bias_n_out[...] = bias_n[...]
    gain_out[...] = gain[...]
    live = lax.broadcasted_iota(jnp.int32, (1, EMAX), 1) < count_ref[...]
    i_at = pairs_ref[0, 0:1, :] - 32
    j_at, j_out = place(pairs_ref[0, 1:2, :] - 32)
    rows = jnp.concatenate(
        [
            jnp.where(live, i_at + 1, 0).astype(F32),
            jnp.where(live, j_at + 1, 0).astype(F32),
            jnp.where(j_out, 1.0, 0.0).astype(F32),
            jnp.ones((1, EMAX), F32),
            geo_ref[0].astype(F32),
        ],
        axis=0,
    )
    row[...] = rows.astype(BF16)
    lanes, subs = grids()
    for k in range(OWN_BLOCKS):
        set_block(BLK * k, rows[:, BLK * k : BLK * k + BLK], lanes, subs, oh, oht, hi, col)


def main_kernel(
    chunks,
    lat_ref,
    cot_ref,
    own_oh,
    own_oht,
    own_hi,
    own_col,
    own_row,
    a_ref,
    b_ref,
    edge_in_ref,
    edge_bias_ref,
    edge_out_ref,
    node_in_ref,
    node_bias_ref,
    node_out_ref,
    gain_ref,
    final_ref,
    grad_ref,
    arr_ref,
    keep_ref,
    send_ref,
    low_ref,
    upp_ref,
    nb_oh,
    nb_oht,
    nb_hi,
    nb_col,
    slope,
    nb_rows,
    work_x,
    work_p,
    work_d,
    work_e,
    work_s,
    t_nb,
    q_nb,
    stage,
    final_v,
    arr_v,
    grad_v,
    sems,
):
    first = lax.axis_index("c") == 0

    @pl.when(first)
    def _():
        low_ref[...] = b_ref[...]
        upp_ref[...] = a_ref[...]

    @pl.when(jnp.logical_not(first))
    def _():
        low_ref[...] = a_ref[...]
        upp_ref[...] = b_ref[...]

    lanes, subs = grids()
    own_refs = (own_oh, own_oht, own_hi, own_col)
    nb_refs = (nb_oh, nb_oht, nb_hi, nb_col)
    own_part = (own_refs, 0, EMAX, 0)

    def nb_part(at, size):
        return nb_refs, at, size, EMAX + at

    info = jnp.maximum(low_ref[X_AT:SENT, :].astype(F32), upp_ref[X_AT:SENT, :].astype(F32))[0:1, :]
    lane = lax.broadcasted_iota(jnp.int32, (1, L), 1)
    reach = [jnp.sum(jnp.where(lane == MIG + c, info, 0.0)).astype(jnp.int32) for c in range(4)]
    low_rows = low_ref[D_AT:X_AT, :].astype(F32)
    upp_rows = upp_ref[D_AT:X_AT, :].astype(F32)
    for k in range(NB_BLOCKS):
        nb_rows[k] = jnp.concatenate([low_rows[8 * k : 8 * k + 8], upp_rows[8 * k : 8 * k + 8]], axis=1)
    for k in range(SURE[3]):
        set_block(BLK * k, nb_rows[k], lanes, subs, *nb_refs)

    def further(last, body):
        def step(k, carry):
            body(pl.multiple_of(BLK * k, BLK))
            return carry

        lax.fori_loop(SURE[last], reach[last], step, 0)

    further(3, lambda at: set_block(at, nb_rows[at // BLK], lanes, subs, *nb_refs))

    def around(source_low, source_upp, width, height):
        parts = []
        for b in range(width // 32):
            parts.append(source_low[width - 32 * (b + 1) : width - 32 * b])
            parts.append(source_upp[32 * b : 32 * b + 32])
        if height > 2 * width:
            parts.append(jnp.zeros((height - 2 * width, L), parts[0].dtype))
        return jnp.concatenate(parts, axis=0)

    def edge_weights(layer):
        top = edge_in_ref[layer, 0:L, :]
        bottom = edge_in_ref[layer, L : 2 * L, :]
        straight = jnp.concatenate([top, bottom], axis=1)
        return straight, jnp.concatenate([bottom, top], axis=1)

    def whole(parts):
        return pl.ds(parts[0][3], sum(part[2] for part in parts))

    def pieces(parts):
        for refs, at, size, to in parts:
            for r in range(0, size, CHUNK):
                yield refs[2].at[pl.ds(at + r, CHUNK), :], pl.ds(to + r, CHUNK)

    def gather(parts, sources, both, by_i):
        for (refs, at, size, to), source in zip(parts, sources):
            by_i[pl.ds(to, size), :L] = dot(refs[0][0, pl.ds(at, size), :], source).astype(by_i.dtype)
            work_p[pl.ds(to, size), :] = dot(refs[0][1, pl.ds(at, size), :], both)

    def forward_rows(layer, parts, sources, both, weights, geo_weights, bias):
        gather(parts, sources, both, work_x)
        for hi, here in pieces(parts):
            is_hi = hi[...] > 0.5
            work_x[here, L:] = jnp.where(is_hi, work_p[here, L:], work_p[here, :L]).astype(BF16)
        for refs, at, size, to in parts:
            rows = pl.ds(to, size)
            work_p[rows, :] = dot(work_x[rows, :], weights) + dot(refs[3][pl.ds(at, size), :], geo_weights)
        for hi, here in pieces(parts):
            pre = work_p[here, :] + bias
            sig = 0.5 * jnp.tanh(0.5 * pre) + 0.5
            act = pre * sig
            slope[layer, here, :] = sig + act * (1.0 - sig)
            diff = act[:, :L] - act[:, L:]
            is_hi = hi[...] > 0.5
            none = jnp.zeros_like(diff)
            work_d[here, :L] = diff.astype(BF16)
            work_e[here, :L] = jnp.where(is_hi, none, diff).astype(BF16)
            work_e[here, L:] = jnp.where(is_hi, diff, none).astype(BF16)

    def edge_forward(layer, h_lo, h_hi, last):
        straight, crossed = edge_weights(layer)
        weights = jnp.concatenate([straight, crossed], axis=0)
        geo_top = edge_in_ref[layer, 2 * L : 2 * L + 4, :].astype(F32)
        geo_weights = jnp.concatenate(
            [jnp.zeros((4, 2 * L), F32), jnp.concatenate([geo_top, -geo_top], axis=1)], axis=0
        ).astype(BF16)
        bias_row = edge_bias_ref[layer : layer + 1, :]
        bias = jnp.concatenate([bias_row, bias_row], axis=1)
        both = jnp.concatenate([h_lo, h_hi], axis=1)
        t_nb[...] = jnp.zeros_like(t_nb)

        def collect(part):
            refs, at, size, to = part
            rows = pl.ds(to, size)
            by_j = dot(refs[1][1, :, pl.ds(at, size)], work_e[rows, :])
            return dot(refs[1][0, :, pl.ds(at, size)], work_d[rows, :L]), by_j

        def more(at):
            part = nb_part(at, BLK)
            forward_rows(layer, [part], [h_hi], both, weights, geo_weights, bias)
            by_i, by_j = collect(part)
            t_nb[:, :L] += -by_j[:, :L]
            t_nb[:, L:] += by_i - by_j[:, L:]

        further(last, more)
        parts = [own_part, nb_part(0, BLK * SURE[last])]
        forward_rows(layer, parts, [h_lo, h_hi], both, weights, geo_weights, bias)
        by_i, by_j = collect(parts[0])
        nb_i, nb_j = collect(parts[1])
        own = (by_i - by_j[:, :L], -by_j[:, L:])
        total = (own[0] - nb_j[:, :L] + t_nb[:, :L], own[1] + nb_i - nb_j[:, L:] + t_nb[:, L:])
        return own, total

    def node_forward(layer, h, total):
        agg = dot(total.astype(BF16), edge_out_ref[layer]).astype(BF16)
        joined = jnp.concatenate([h, agg], axis=1)
        pre = dot(joined, node_in_ref[layer]) + node_bias_ref[layer : layer + 1, :]
        sig = 0.5 * jnp.tanh(0.5 * pre) + 0.5
        act = pre * sig
        hidden = act.astype(BF16)
        out = dot(hidden, node_out_ref[layer])
        centred = out - jnp.mean(out, axis=1, keepdims=True)
        inv = lax.rsqrt(jnp.mean(centred * centred, axis=1, keepdims=True) + EPS)
        normed = centred * inv
        new = (h.astype(F32) + normed * gain_ref[layer : layer + 1, :]).astype(BF16)
        return new, (joined, sig + act * (1.0 - sig), hidden, normed, inv)

    def node_backward(layer, grad, kept):
        size = grad.shape[0]
        joined, node_slope, hidden, normed, inv = (v[:size] for v in kept)
        gain_term = jnp.sum(grad[:ROWS] * normed[:ROWS], axis=0, keepdims=True)
        dnorm = grad * gain_ref[layer : layer + 1, :]
        mean_a = jnp.mean(dnorm, axis=1, keepdims=True)
        mean_b = jnp.mean(dnorm * normed, axis=1, keepdims=True)
        dout = ((dnorm - mean_a - normed * mean_b) * inv).astype(BF16)
        out_term = dot_tn(hidden[:ROWS], dout[:ROWS])
        dpre = (dot_nt(dout, node_out_ref[layer]) * node_slope).astype(BF16)
        in_term = dot_tn(joined[:ROWS], dpre[:ROWS])
        bias_term = jnp.sum(dpre[:ROWS].astype(F32), axis=0, keepdims=True)
        dx = dot_nt(dpre, node_in_ref[layer])
        return grad + dx[:, :L], dx[:, L:].astype(BF16), (in_term, bias_term, out_term, gain_term)

    def backward_rows(layer, parts, sources, both):
        gather(parts, sources, both, work_s)
        for hi, here in pieces(parts):
            is_hi = hi[...] > 0.5
            dd = work_s[here, :] - jnp.where(is_hi, work_p[here, L:], work_p[here, :L])
            dfwd = dd * slope[layer, here, :L]
            drev = -dd * slope[layer, here, L:]
            none = jnp.zeros_like(dfwd)
            work_d[here, :L] = dfwd.astype(BF16)
            work_d[here, L:] = drev.astype(BF16)
            work_x[here, :L] = jnp.where(is_hi, none, drev).astype(BF16)
            work_x[here, L:] = jnp.where(is_hi, none, dfwd).astype(BF16)
            work_e[here, :L] = jnp.where(is_hi, drev, none).astype(BF16)
            work_e[here, L:] = jnp.where(is_hi, dfwd, none).astype(BF16)

    def edge_backward(layer, e_lo, e_hi, last):
        both = jnp.concatenate([e_lo, e_hi], axis=1)
        q_nb[...] = jnp.zeros_like(q_nb)

        def nb_collect(part):
            refs, at, size, to = part
            rows, cols = pl.ds(to, size), pl.ds(at, size)
            lo = dot(refs[1][1, :, cols], work_x[rows, :])
            if last == 0:
                return lo, None
            return lo, dot(refs[1][1, :, cols], work_e[rows, :]) + dot(refs[1][0, :, cols], work_d[rows, :])

        def more(at):
            part = nb_part(at, BLK)
            backward_rows(layer, [part], [e_hi], both)
            lo, up = nb_collect(part)
            q_nb[0:ROWS, :] += lo
            if last:
                q_nb[ROWS:, :] += up

        further(last, more)
        parts = [own_part, nb_part(0, BLK * SURE[last])]
        backward_rows(layer, parts, [e_lo, e_hi], both)
        rows = pl.ds(0, EMAX)
        q_lo = dot(own_oht[0], work_d[rows, :]) + dot(own_oht[1], work_x[rows, :])
        q_hi = dot(own_oht[1], work_e[rows, :])
        nb_lo, nb_up = nb_collect(parts[1])
        own = jnp.concatenate([q_lo, q_hi], axis=0)
        if last == 0:
            total = q_lo + nb_lo + q_nb[0:ROWS, :]
        else:
            total = own + jnp.concatenate([nb_lo, nb_up], axis=0) + q_nb[...]
        return own, total, dot(own_row[...], work_d[rows, :])

    h0_lo = lat_ref[0]
    h0_hi = around(low_ref[0:LAT_HALO, :], upp_ref[0:LAT_HALO, :], LAT_HALO, ROWS)
    own0, total0 = (jnp.concatenate(t, axis=0) for t in edge_forward(0, h0_lo, h0_hi, 3))
    h0 = jnp.concatenate([h0_lo, h0_hi], axis=0)
    h1, kept0 = node_forward(0, h0, total0)
    own1, total1 = (jnp.concatenate(t, axis=0) for t in edge_forward(1, h1[:ROWS], h1[ROWS:], 2))
    near = ROWS + 2 * COT_HALO
    h2, kept1 = node_forward(1, h1[:near], total1[:near])
    final_v[...] = h2[:ROWS]

    few = lax.broadcasted_iota(jnp.int32, (MIG, 2 * COT_HALO), 1).astype(F32)
    for k, ref in ((0, upp_ref), (1, low_ref)):
        movers = jnp.transpose(ref[X_AT:SENT, :].astype(F32))[0:MIG, 0:1]
        arr_v[k] = dot(masked(movers == few), h2[ROWS:]).astype(BF16)
    copies = [
        pltpu.make_async_copy(final_v, final_ref.at[0], sems.at[0]),
        pltpu.make_async_copy(arr_v, arr_ref.at[0], sems.at[1]),
        pltpu.make_async_copy(grad_v, grad_ref.at[0], sems.at[2]),
    ]
    copies[0].start()
    copies[1].start()

    def with_zeros(value):
        return jnp.concatenate([value, jnp.zeros((2 * ROWS - value.shape[0],) + value.shape[1:], value.dtype)], axis=0)

    def layer_back(layer, grad, kept, own_total, h, last, keep_rows):
        part, dagg, node_terms = node_backward(layer, grad, kept)
        spread = with_zeros(dagg)
        e = with_zeros(dot_nt(dagg, edge_out_ref[layer]).astype(BF16))
        q_own, q_all, geo = edge_backward(layer, e[:ROWS], e[ROWS:], last)
        out_term = dot_tn(own_total.astype(BF16), spread)
        in_term = dot_tn(h, q_own.astype(BF16))
        straight, _ = edge_weights(layer)
        new = part[:keep_rows] + dot_nt(q_all[:keep_rows].astype(BF16), straight)
        return new, (in_term, geo, out_term) + node_terms

    cot = jnp.concatenate(
        [cot_ref[0], around(low_ref[LAT_HALO:D_AT, :], upp_ref[LAT_HALO:D_AT, :], COT_HALO, 2 * COT_HALO)], axis=0
    ).astype(F32)
    grad1, terms1 = layer_back(1, cot, kept1, own1, h1, 1, ROWS + 64)
    grad0, terms0 = layer_back(0, grad1, kept0, own0, h0, 0, ROWS)
    grad_v[...] = grad0
    copies[2].start()

    size = MAIN // chunks
    per = -(-EXTRA // chunks)
    for layer, terms in enumerate((terms0, terms1)):
        in_term, geo, out_term, node_in_term, node_bias_term, node_out_term, gain_term = terms
        stage[layer, :, size:, :] = jnp.zeros((chunks, stage.shape[2] - size, L), BF16)
        at = 0
        for value in (in_term[:, :L], in_term[:, L:], out_term, node_in_term, node_out_term):
            value = value.astype(BF16)
            while value.shape[0]:
                take = min(value.shape[0], size - at % size)
                stage[layer, at // size, at % size : at % size + take, :] = value[:take]
                value = value[take:]
                at += take
        small = [geo[4 + g : 5 + g, :L] - geo[4 + g : 5 + g, L:] for g in range(4)]
        small += [geo[3:4, :L] + geo[3:4, L:], node_bias_term, gain_term]
        for extra, value in enumerate(small):
            spot = size + extra % per
            stage[layer, extra // per, spot : spot + 1, :] = value.astype(BF16)

    @pl.when(first)
    def _():
        keep_ref[...] = stage[0]
        send_ref[...] = stage[1]

    @pl.when(jnp.logical_not(first))
    def _():
        keep_ref[...] = stage[1]
        send_ref[...] = stage[0]

    for copy in copies:
        copy.wait()


def fold_kernel(copies, in_ref, out_ref):
    total = in_ref[0].astype(F32)
    for k in range(1, in_ref.shape[0]):
        total += in_ref[k].astype(F32)
    total = total.astype(BF16)
    for k in range(copies):
        out_ref[k] = total


def fold(array, copies):
    return pl.pallas_call(
        lambda a, b: fold_kernel(copies, a, b),
        out_shape=jax.ShapeDtypeStruct((copies,) + array.shape[1:], BF16),
        in_specs=[pl.BlockSpec(memory_space=pltpu.VMEM)],
        out_specs=pl.BlockSpec(memory_space=pltpu.VMEM),
        compiler_params=pltpu.CompilerParams(vmem_limit_bytes=VMEM_LIMIT),
        name="fold",
    )(array)


def add_kernel(a_ref, b_ref, out_ref):
    out_ref[...] = (a_ref[...].astype(F32) + b_ref[...].astype(F32)).astype(BF16)


def add(a, b):
    return pl.pallas_call(
        add_kernel,
        out_shape=jax.ShapeDtypeStruct(a.shape, BF16),
        in_specs=vmem(2),
        out_specs=pl.BlockSpec(memory_space=pltpu.VMEM),
        compiler_params=pltpu.CompilerParams(vmem_limit_bytes=VMEM_LIMIT),
        name="add",
    )(a, b)


def unpack_kernel(chunks, mine_ref, other_ref, *outs):
    def write(layer, ref):
        edge_in, edge_bias, edge_out, node_in, node_bias, node_out, gain = outs
        size = MAIN // chunks
        per = -(-EXTRA // chunks)
        at = 0
        for out, rows in ((edge_in, 2 * L), (edge_out, L), (node_in, 2 * L), (node_out, L)):
            r = 0
            while r < rows:
                take = min(rows - r, size - at % size)
                value = ref[at // size, at % size : at % size + take, :].astype(F32)
                if out is edge_in:
                    out[pl.ds(2 * r + layer, take, stride=2), :] = value
                else:
                    out[layer, r : r + take, :] = value
                r += take
                at += take
        small = []
        for extra in range(EXTRA):
            spot = size + extra % per
            small.append(ref[extra // per, spot : spot + 1, :].astype(F32))
        for g in range(4):
            edge_in[4 * L + 2 * g + layer : 4 * L + 2 * g + layer + 1, :] = small[g]
        edge_bias[layer : layer + 1, :] = small[4]
        node_bias[layer : layer + 1, :] = small[5]
        gain[layer : layer + 1, :] = small[6]

    first = lax.axis_index("c") == 0

    @pl.when(first)
    def _():
        write(0, mine_ref)
        write(1, other_ref)

    @pl.when(jnp.logical_not(first))
    def _():
        write(1, mine_ref)
        write(0, other_ref)


def vmem(count):
    return [pl.BlockSpec(memory_space=pltpu.VMEM)] * count


def solution(mesh):
    n_space = mesh.shape["space"]
    n_x = mesh.shape["replicas"]
    n_c = 2
    n_z = min(16, n_space // n_c)
    n_y = n_space // (n_c * n_z)
    n_l = 2 if n_z > 4 else 1
    n_h = n_z // n_l
    fine = Mesh(mesh.devices.reshape(n_y, n_h, n_l, n_c, n_x), ("y", "zh", "zl", "c", "x"))
    space = ("y", "zh", "zl", "c")
    group = ("zl", "y", "x")
    chunks = n_y * n_l * n_x
    size = MAIN // chunks
    chunk_rows = size + -(-(-(-EXTRA // chunks)) // 8) * 8
    params = pltpu.CompilerParams(vmem_limit_bytes=VMEM_LIMIT)

    def on_device(latents, pairs, geometry, pair_count, cotangent, leaving, *weights):
        sent = jax.ShapeDtypeStruct((SENT, L), BF16)
        to_a, to_b = pl.pallas_call(
            pack_kernel,
            out_shape=(sent, sent),
            in_specs=[pl.BlockSpec(memory_space=pltpu.HBM)] * 6,
            out_specs=tuple(vmem(2)),
            scratch_shapes=[
                pltpu.VMEM((1, 1), jnp.int32),
                pltpu.VMEM((2, EMAX), jnp.int32),
                pltpu.VMEM((4, EMAX), BF16),
                pltpu.VMEM((2, MIG), jnp.int32),
                pltpu.SemaphoreType.DMA((8,)),
            ],
            compiler_params=pltpu.CompilerParams(vmem_limit_bytes=60 * 1024 * 1024),
            name="pack",
        )(pair_count, latents, cotangent, pairs, geometry, leaving)
        half = range(n_space // 2)
        near = [(2 * i, 2 * i + 1) for i in half]
        cross = [(2 * i + 1, (2 * i + 2) % n_space) for i in half]
        from_a = lax.ppermute(to_a, space, near + [(j, i) for i, j in near])
        from_b = lax.ppermute(to_b, space, cross + [(j, i) for i, j in cross])
        own = pl.pallas_call(
            own_kernel,
            out_shape=(
                jax.ShapeDtypeStruct((2, EMAX, ROWS), BF16),
                jax.ShapeDtypeStruct((2, ROWS, EMAX), BF16),
                jax.ShapeDtypeStruct((EMAX, L), F32),
                jax.ShapeDtypeStruct((EMAX, 8), BF16),
                jax.ShapeDtypeStruct((8, EMAX), BF16),
            )
            + (jax.ShapeDtypeStruct((2, L), F32),) * 3,
            in_specs=vmem(6),
            out_specs=tuple(vmem(8)),
            compiler_params=pltpu.CompilerParams(vmem_limit_bytes=16 * 1024 * 1024),
            cost_estimate=pl.CostEstimate(flops=2000000, bytes_accessed=8000000, transcendentals=0),
            name="own",
        )(pair_count, pairs, geometry, weights[1], weights[4], weights[6])
        final, grad, arrivals, keep, send = pl.pallas_call(
            lambda *refs: main_kernel(chunks, *refs),
            out_shape=(
                jax.ShapeDtypeStruct((1, ROWS, L), BF16),
                jax.ShapeDtypeStruct((1, ROWS, L), F32),
                jax.ShapeDtypeStruct((1, 2, MIG, L), BF16),
                jax.ShapeDtypeStruct((chunks, chunk_rows, L), BF16),
                jax.ShapeDtypeStruct((chunks, chunk_rows, L), BF16),
            ),
            in_specs=vmem(16),
            out_specs=tuple([pl.BlockSpec(memory_space=pl.ANY)] * 3 + vmem(2)),
            scratch_shapes=[
                pltpu.VMEM((SENT, L), BF16),
                pltpu.VMEM((SENT, L), BF16),
                pltpu.VMEM((2, 2 * EMAX, ROWS), BF16),
                pltpu.VMEM((2, ROWS, 2 * EMAX), BF16),
                pltpu.VMEM((2 * EMAX, L), F32),
                pltpu.VMEM((2 * EMAX, 8), BF16),
                pltpu.VMEM((2, ALL_PAIRS, 2 * L), F32),
                pltpu.VMEM((NB_BLOCKS, 8, BLK), F32),
                pltpu.VMEM((ALL_PAIRS, 2 * L), BF16),
                pltpu.VMEM((ALL_PAIRS, 2 * L), F32),
                pltpu.VMEM((ALL_PAIRS, 2 * L), BF16),
                pltpu.VMEM((ALL_PAIRS, 2 * L), BF16),
                pltpu.VMEM((ALL_PAIRS, L), F32),
                pltpu.VMEM((ROWS, 2 * L), F32),
                pltpu.VMEM((2 * ROWS, 2 * L), F32),
                pltpu.VMEM((2, chunks, chunk_rows, L), BF16),
                pltpu.VMEM((ROWS, L), BF16),
                pltpu.VMEM((2, MIG, L), BF16),
                pltpu.VMEM((ROWS, L), F32),
                pltpu.SemaphoreType.DMA((3,)),
            ],
            compiler_params=params,
            name="steps",
        )(
            latents, cotangent, *own[:5], from_a, from_b,
            weights[0], own[5], weights[2], weights[3], own[6], weights[5], own[7],
        )

        swap = [(0, 1), (1, 0)]
        got = add(keep, lax.ppermute(send, "c", swap))
        got = lax.all_to_all(got, group, 0, 0, tiled=True)
        got = lax.all_to_all(fold(got, n_h), "zh", 0, 0, tiled=True)
        got = lax.all_to_all(fold(got, chunks), group, 0, 0, tiled=True)

        grads = pl.pallas_call(
            lambda *refs: unpack_kernel(chunks, *refs),
            out_shape=(jax.ShapeDtypeStruct((2 * weights[0].shape[1], L), F32),)
            + tuple(jax.ShapeDtypeStruct(w.shape, F32) for w in weights[1:]),
            in_specs=vmem(2),
            out_specs=tuple(vmem(7)),
            compiler_params=params,
            name="unpack",
        )(got, lax.ppermute(got, "c", swap))
        edge_in_grad = jnp.transpose(grads[0].reshape(-1, 2, L), (1, 0, 2))
        return (final, grad, arrivals, edge_in_grad) + tuple(grads[1:])

    return jax.shard_map(
        on_device,
        mesh=fine,
        in_specs=(
            P("x", space, None),
            P("x", None, space),
            P("x", None, space),
            P("x", space),
            P("x", space, None),
            P("x", space, None),
        )
        + (P(),) * 7,
        out_specs=(P("x", space, None), P("x", space, None), P("x", space, None, None)) + (P(),) * 7,
        check_vma=False,
    )
```

```python
import jax
import jax.numpy as jnp
from jax import lax
from jax.experimental import pallas as pl
from jax.experimental.pallas import tpu as pltpu
from jax.sharding import Mesh, PartitionSpec as P


F32 = jnp.float32
BF16 = jnp.bfloat16
L = 128
ROWS = 256
EMAX = 1024
BLK = 256
OWN_BLOCKS = EMAX // BLK
SIDE = 128
NB_BLOCKS = EMAX // SIDE
ALL_PAIRS = EMAX + 2 * EMAX
SURE = (1, 2, 3, 4)
CHUNK = 64
LAT_HALO = 128
COT_HALO = 64
SENT = LAT_HALO + COT_HALO + 64 + 16
D_AT = LAT_HALO + COT_HALO
X_AT = D_AT + 64
MIG = 16
MAIN = 1536
EXTRA = 14
EPS = 1e-05
VMEM_LIMIT = 48 * 1024 * 1024


def dot(a, b):
    return jnp.dot(a, b, preferred_element_type=F32)


def dot_nt(a, b):
    return lax.dot_general(a, b, (((1,), (1,)), ((), ())), preferred_element_type=F32)


def dot_tn(a, b):
    return lax.dot_general(a, b, (((0,), (0,)), ((), ())), preferred_element_type=F32)


def place(row):
    below = row < 0
    above = row >= ROWS
    out = jnp.where(below, -1 - row, row - ROWS)
    block = lax.shift_right_arithmetic(out, 5)
    inner = jnp.where(below, row + 32 * (block + 1), row - ROWS - 32 * block + 32)
    outside = jnp.logical_or(below, above)
    return jnp.where(outside, 64 * block + inner, row), outside


def masked(flag):
    return jnp.where(flag, 1.0, 0.0).astype(BF16)


def pack_kernel(
    count_ref, lat_ref, cot_ref, pairs_ref, geo_ref, leav_ref, b_ref, a_ref, count_v, pairs_v, geo_v, leav_v, sems
):
    first = lax.axis_index("c") == 0
    copies = [
        pltpu.make_async_copy(pairs_ref.at[0], pairs_v, sems.at[0]),
        pltpu.make_async_copy(geo_ref.at[0], geo_v, sems.at[1]),
        pltpu.make_async_copy(leav_ref.at[0], leav_v, sems.at[2]),
        pltpu.make_async_copy(count_ref, count_v, sems.at[7]),
    ]
    ups = (first, jnp.logical_not(first))
    for k, ref in enumerate((a_ref, b_ref)):
        lat_at = pl.multiple_of(jnp.where(ups[k], ROWS - LAT_HALO, 0), LAT_HALO)
        cot_at = pl.multiple_of(jnp.where(ups[k], ROWS - COT_HALO, 0), COT_HALO)
        lat = lat_ref.at[0, pl.ds(lat_at, LAT_HALO), :]
        cot = cot_ref.at[0, pl.ds(cot_at, COT_HALO), :]
        copies.append(pltpu.make_async_copy(lat, ref.at[pl.ds(0, LAT_HALO), :], sems.at[3 + 2 * k]))
        copies.append(pltpu.make_async_copy(cot, ref.at[pl.ds(LAT_HALO, COT_HALO), :], sems.at[4 + 2 * k]))
    for copy in copies:
        copy.start()
    for copy in copies[:4]:
        copy.wait()

    live = lax.broadcasted_iota(jnp.int32, (1, EMAX), 1) < count_v[...]
    own = pairs_v[0:1, :]
    other = pairs_v[1:2, :]
    geo = geo_v[...].astype(F32)
    leav = leav_v[...].astype(F32)
    rows, kinds = [], []
    for k in range(2):
        up = ups[k]
        shift = jnp.where(up, -32 - ROWS, ROWS - 32)
        i_row = own + shift
        j_row = other + shift
        far = jnp.where(up, -1 - jnp.maximum(i_row, j_row), jnp.minimum(i_row, j_row) - ROWS)
        kind = jnp.where(far < 0, 0, lax.shift_right_arithmetic(far, 5) + 1)
        kind = jnp.where(jnp.logical_and(live, kind < 4), kind, 4).astype(F32)
        i_at, _ = place(i_row)
        j_at, j_hi = place(j_row)
        keep = kind < 3.5
        i_at = jnp.where(keep, i_at + 1, 0).astype(F32)
        j_at = jnp.where(keep, j_at + 1, 0).astype(F32)
        hi = jnp.where(j_hi, 1.0, 0.0).astype(F32)
        rows.append(jnp.concatenate([i_at, j_at, hi, jnp.ones((1, EMAX), F32), geo], axis=0).astype(BF16))
        kinds.append(jnp.concatenate([kind[:, 128 * t : 128 * t + 128] for t in range(8)], axis=0))

    flags = [jnp.where(kinds[k] == c, 1.0, 0.0).astype(F32) for k in range(2) for c in range(4)]
    marks = jnp.concatenate(flags, axis=0).astype(BF16)
    row_i = lax.broadcasted_iota(jnp.int32, (128, 128), 0)
    col_i = lax.broadcasted_iota(jnp.int32, (128, 128), 1)
    inside = dot(marks, masked(row_i < col_i))
    sums = dot(marks, jnp.ones((128, 128), BF16))
    row_b = lax.broadcasted_iota(jnp.int32, (64, 64), 0)
    col_b = lax.broadcasted_iota(jnp.int32, (64, 64), 1)
    same = lax.shift_right_logical(row_b, 5) == lax.shift_right_logical(col_b, 5)
    before = dot(masked(jnp.logical_and(same, col_b < row_b)), sums.astype(BF16))
    at = inside + before
    lane = lax.broadcasted_iota(jnp.int32, (1, 128), 1)
    col_w = lax.broadcasted_iota(jnp.int32, (128, BLK), 1).astype(F32)
    places = []
    for k in range(2):
        rank = jnp.full((8, 128), -1.0, F32)
        for c in range(4):
            here = 32 * k + 8 * c
            rank = jnp.where(kinds[k] == c, at[here : here + 8, :], rank)
        places.append(jnp.transpose(rank))

    def move(k, t, shift):
        picks = [masked(places[k][:, q : q + 1] == col_w + shift) for q in range(8)]
        moved = dot(rows[k], jnp.concatenate(picks, axis=0))
        ref = (a_ref, b_ref)[k]
        spot = D_AT + 16 * t
        if not isinstance(t, int):
            spot = pl.multiple_of(spot, 16)
        ref[pl.ds(spot, 16), :] = jnp.concatenate([moved[:, :128], moved[:, 128:]], axis=0).astype(BF16)

    for t in range(2):
        for k in range(2):
            move(k, t, float(BLK * t))
    for k, ref in enumerate((a_ref, b_ref)):
        up = ups[k]
        ends = [before[32 * k + 8 * c + 7, 0] + sums[32 * k + 8 * c + 7, 0] for c in range(4)]
        trips = lax.shift_right_logical(ends[3].astype(jnp.int32) + (BLK - 1), 8)
        ref[D_AT + 32 : X_AT, :] = jnp.zeros((X_AT - D_AT - 32, L), BF16)

        def body(t, carry, k=k):
            move(k, t, (t * BLK).astype(F32))
            return carry

        lax.fori_loop(2, trips, body, 0)
        movers = jnp.where(up, leav[1:2, :] - 224.0, leav[0:1, :] + 32.0)
        tail = jnp.concatenate([movers, jnp.zeros((1, 128 - MIG), F32)], axis=1)
        for c in range(4):
            blocks = ((ends[c].astype(jnp.int32) + (SIDE - 1)) // SIDE).astype(F32)
            tail = jnp.where(lane == MIG + c, blocks, tail)
        ref[X_AT:SENT, :] = jnp.broadcast_to(tail, (16, 128)).astype(BF16)
    for copy in copies[4:]:
        copy.wait()


def grids():
    lanes = lax.broadcasted_iota(jnp.int32, (BLK, ROWS), 1).astype(F32) + 1.0
    subs = lax.broadcasted_iota(jnp.int32, (ROWS, BLK), 0).astype(F32) + 1.0
    return lanes, subs


def set_block(at, rows, lanes, subs, oh, oht, hi, col):
    here = pl.ds(at, BLK)
    cols = jnp.transpose(rows)
    for e in range(2):
        oh[e, here, :] = masked(cols[:, e : e + 1] == lanes)
        oht[e, :, here] = masked(rows[e : e + 1, :] == subs)
    hi[here, :] = jnp.broadcast_to(cols[:, 2:3], (BLK, L))
    col[here, :] = cols.astype(BF16)


def own_kernel(count_ref, pairs_ref, geo_ref, bias_e, bias_n, gain, oh, oht, hi, col, row, bias_e_out, bias_n_out, gain_out):
    bias_e_out[...] = bias_e[...]
    bias_n_out[...] = bias_n[...]
    gain_out[...] = gain[...]
    live = lax.broadcasted_iota(jnp.int32, (1, EMAX), 1) < count_ref[...]
    i_at = pairs_ref[0, 0:1, :] - 32
    j_at, j_out = place(pairs_ref[0, 1:2, :] - 32)
    rows = jnp.concatenate(
        [
            jnp.where(live, i_at + 1, 0).astype(F32),
            jnp.where(live, j_at + 1, 0).astype(F32),
            jnp.where(j_out, 1.0, 0.0).astype(F32),
            jnp.ones((1, EMAX), F32),
            geo_ref[0].astype(F32),
        ],
        axis=0,
    )
    row[...] = rows.astype(BF16)
    lanes, subs = grids()
    for k in range(OWN_BLOCKS):
        set_block(BLK * k, rows[:, BLK * k : BLK * k + BLK], lanes, subs, oh, oht, hi, col)


def main_kernel(
    chunks,
    lat_ref,
    cot_ref,
    own_oh,
    own_oht,
    own_hi,
    own_col,
    own_row,
    b_ref,
    a_ref,
    edge_in_ref,
    edge_bias_ref,
    edge_out_ref,
    node_in_ref,
    node_bias_ref,
    node_out_ref,
    gain_ref,
    final_ref,
    grad_ref,
    arr_ref,
    packed_ref,
    low_ref,
    upp_ref,
    nb_oh,
    nb_oht,
    nb_hi,
    nb_col,
    slope,
    nb_rows,
    work_x,
    work_p,
    work_d,
    work_e,
    work_s,
    t_nb,
    q_nb,
    final_v,
    arr_v,
    grad_v,
    sems,
):
    first = lax.axis_index("c") == 0

    @pl.when(first)
    def _():
        low_ref[...] = b_ref[...]
        upp_ref[...] = a_ref[...]

    @pl.when(jnp.logical_not(first))
    def _():
        low_ref[...] = a_ref[...]
        upp_ref[...] = b_ref[...]

    lanes, subs = grids()
    own_refs = (own_oh, own_oht, own_hi, own_col)
    nb_refs = (nb_oh, nb_oht, nb_hi, nb_col)
    own_part = (own_refs, 0, EMAX, 0)

    def nb_part(at, size):
        return nb_refs, at, size, EMAX + at

    info = jnp.maximum(low_ref[X_AT:SENT, :].astype(F32), upp_ref[X_AT:SENT, :].astype(F32))[0:1, :]
    lane = lax.broadcasted_iota(jnp.int32, (1, L), 1)
    reach = [jnp.sum(jnp.where(lane == MIG + c, info, 0.0)).astype(jnp.int32) for c in range(4)]
    low_rows = low_ref[D_AT:X_AT, :].astype(F32)
    upp_rows = upp_ref[D_AT:X_AT, :].astype(F32)
    for k in range(NB_BLOCKS):
        nb_rows[k] = jnp.concatenate([low_rows[8 * k : 8 * k + 8], upp_rows[8 * k : 8 * k + 8]], axis=1)
    for k in range(SURE[3]):
        set_block(BLK * k, nb_rows[k], lanes, subs, *nb_refs)

    def further(last, body):
        def step(k, carry):
            body(pl.multiple_of(BLK * k, BLK))
            return carry

        lax.fori_loop(SURE[last], reach[last], step, 0)

    further(3, lambda at: set_block(at, nb_rows[at // BLK], lanes, subs, *nb_refs))

    def around(source_low, source_upp, width, height):
        parts = []
        for b in range(width // 32):
            parts.append(source_low[width - 32 * (b + 1) : width - 32 * b])
            parts.append(source_upp[32 * b : 32 * b + 32])
        if height > 2 * width:
            parts.append(jnp.zeros((height - 2 * width, L), parts[0].dtype))
        return jnp.concatenate(parts, axis=0)

    def edge_weights(layer):
        top = edge_in_ref[layer, 0:L, :]
        bottom = edge_in_ref[layer, L : 2 * L, :]
        straight = jnp.concatenate([top, bottom], axis=1)
        return straight, jnp.concatenate([bottom, top], axis=1)

    def whole(parts):
        return pl.ds(parts[0][3], sum(part[2] for part in parts))

    def pieces(parts):
        for refs, at, size, to in parts:
            for r in range(0, size, CHUNK):
                yield refs[2].at[pl.ds(at + r, CHUNK), :], pl.ds(to + r, CHUNK)

    def gather(parts, sources, both, by_i):
        for (refs, at, size, to), source in zip(parts, sources):
            by_i[pl.ds(to, size), :L] = dot(refs[0][0, pl.ds(at, size), :], source).astype(by_i.dtype)
            work_p[pl.ds(to, size), :] = dot(refs[0][1, pl.ds(at, size), :], both)

    def forward_rows(layer, parts, sources, both, weights, geo_weights, bias):
        gather(parts, sources, both, work_x)
        for hi, here in pieces(parts):
            is_hi = hi[...] > 0.5
            work_x[here, L:] = jnp.where(is_hi, work_p[here, L:], work_p[here, :L]).astype(BF16)
        for refs, at, size, to in parts:
            rows = pl.ds(to, size)
            work_p[rows, :] = dot(work_x[rows, :], weights) + dot(refs[3][pl.ds(at, size), :], geo_weights)
        for hi, here in pieces(parts):
            pre = work_p[here, :] + bias
            sig = 0.5 * jnp.tanh(0.5 * pre) + 0.5
            act = pre * sig
            slope[layer, here, :] = sig + act * (1.0 - sig)
            diff = act[:, :L] - act[:, L:]
            is_hi = hi[...] > 0.5
            none = jnp.zeros_like(diff)
            work_d[here, :L] = diff.astype(BF16)
            work_e[here, :L] = jnp.where(is_hi, none, diff).astype(BF16)
            work_e[here, L:] = jnp.where(is_hi, diff, none).astype(BF16)

    def edge_forward(layer, h_lo, h_hi, last):
        straight, crossed = edge_weights(layer)
        weights = jnp.concatenate([straight, crossed], axis=0)
        geo_top = edge_in_ref[layer, 2 * L : 2 * L + 4, :].astype(F32)
        geo_weights = jnp.concatenate(
            [jnp.zeros((4, 2 * L), F32), jnp.concatenate([geo_top, -geo_top], axis=1)], axis=0
        ).astype(BF16)
        bias_row = edge_bias_ref[layer : layer + 1, :]
        bias = jnp.concatenate([bias_row, bias_row], axis=1)
        both = jnp.concatenate([h_lo, h_hi], axis=1)
        t_nb[...] = jnp.zeros_like(t_nb)

        def collect(part):
            refs, at, size, to = part
            rows = pl.ds(to, size)
            by_j = dot(refs[1][1, :, pl.ds(at, size)], work_e[rows, :])
            return dot(refs[1][0, :, pl.ds(at, size)], work_d[rows, :L]), by_j

        def more(at):
            part = nb_part(at, BLK)
            forward_rows(layer, [part], [h_hi], both, weights, geo_weights, bias)
            by_i, by_j = collect(part)
            t_nb[:, :L] += -by_j[:, :L]
            t_nb[:, L:] += by_i - by_j[:, L:]

        further(last, more)
        parts = [own_part, nb_part(0, BLK * SURE[last])]
        forward_rows(layer, parts, [h_lo, h_hi], both, weights, geo_weights, bias)
        by_i, by_j = collect(parts[0])
        nb_i, nb_j = collect(parts[1])
        own = (by_i - by_j[:, :L], -by_j[:, L:])
        total = (own[0] - nb_j[:, :L] + t_nb[:, :L], own[1] + nb_i - nb_j[:, L:] + t_nb[:, L:])
        return own, total

    def node_forward(layer, h, total):
        agg = dot(total.astype(BF16), edge_out_ref[layer]).astype(BF16)
        joined = jnp.concatenate([h, agg], axis=1)
        pre = dot(joined, node_in_ref[layer]) + node_bias_ref[layer : layer + 1, :]
        sig = 0.5 * jnp.tanh(0.5 * pre) + 0.5
        act = pre * sig
        hidden = act.astype(BF16)
        out = dot(hidden, node_out_ref[layer])
        centred = out - jnp.mean(out, axis=1, keepdims=True)
        inv = lax.rsqrt(jnp.mean(centred * centred, axis=1, keepdims=True) + EPS)
        normed = centred * inv
        new = (h.astype(F32) + normed * gain_ref[layer : layer + 1, :]).astype(BF16)
        return new, (joined, sig + act * (1.0 - sig), hidden, normed, inv)

    def node_backward(layer, grad, kept):
        size = grad.shape[0]
        joined, node_slope, hidden, normed, inv = (v[:size] for v in kept)
        gain_term = jnp.sum(grad[:ROWS] * normed[:ROWS], axis=0, keepdims=True)
        dnorm = grad * gain_ref[layer : layer + 1, :]
        mean_a = jnp.mean(dnorm, axis=1, keepdims=True)
        mean_b = jnp.mean(dnorm * normed, axis=1, keepdims=True)
        dout = ((dnorm - mean_a - normed * mean_b) * inv).astype(BF16)
        out_term = dot_tn(hidden[:ROWS], dout[:ROWS])
        dpre = (dot_nt(dout, node_out_ref[layer]) * node_slope).astype(BF16)
        in_term = dot_tn(joined[:ROWS], dpre[:ROWS])
        bias_term = jnp.sum(dpre[:ROWS].astype(F32), axis=0, keepdims=True)
        dx = dot_nt(dpre, node_in_ref[layer])
        return grad + dx[:, :L], dx[:, L:].astype(BF16), (in_term, bias_term, out_term, gain_term)

    def backward_rows(layer, parts, sources, both):
        gather(parts, sources, both, work_s)
        for hi, here in pieces(parts):
            is_hi = hi[...] > 0.5
            dd = work_s[here, :] - jnp.where(is_hi, work_p[here, L:], work_p[here, :L])
            dfwd = dd * slope[layer, here, :L]
            drev = -dd * slope[layer, here, L:]
            none = jnp.zeros_like(dfwd)
            work_d[here, :L] = dfwd.astype(BF16)
            work_d[here, L:] = drev.astype(BF16)
            work_x[here, :L] = jnp.where(is_hi, none, drev).astype(BF16)
            work_x[here, L:] = jnp.where(is_hi, none, dfwd).astype(BF16)
            work_e[here, :L] = jnp.where(is_hi, drev, none).astype(BF16)
            work_e[here, L:] = jnp.where(is_hi, dfwd, none).astype(BF16)

    def edge_backward(layer, e_lo, e_hi, last):
        both = jnp.concatenate([e_lo, e_hi], axis=1)
        q_nb[...] = jnp.zeros_like(q_nb)

        def nb_collect(part):
            refs, at, size, to = part
            rows, cols = pl.ds(to, size), pl.ds(at, size)
            lo = dot(refs[1][1, :, cols], work_x[rows, :])
            if last == 0:
                return lo, None
            return lo, dot(refs[1][1, :, cols], work_e[rows, :]) + dot(refs[1][0, :, cols], work_d[rows, :])

        def more(at):
            part = nb_part(at, BLK)
            backward_rows(layer, [part], [e_hi], both)
            lo, up = nb_collect(part)
            q_nb[0:ROWS, :] += lo
            if last:
                q_nb[ROWS:, :] += up

        further(last, more)
        parts = [own_part, nb_part(0, BLK * SURE[last])]
        backward_rows(layer, parts, [e_lo, e_hi], both)
        rows = pl.ds(0, EMAX)
        q_lo = dot(own_oht[0], work_d[rows, :]) + dot(own_oht[1], work_x[rows, :])
        q_hi = dot(own_oht[1], work_e[rows, :])
        nb_lo, nb_up = nb_collect(parts[1])
        own = jnp.concatenate([q_lo, q_hi], axis=0)
        if last == 0:
            total = q_lo + nb_lo + q_nb[0:ROWS, :]
        else:
            total = own + jnp.concatenate([nb_lo, nb_up], axis=0) + q_nb[...]
        return own, total, dot(own_row[...], work_d[rows, :])

    h0_lo = lat_ref[0]
    h0_hi = around(low_ref[0:LAT_HALO, :], upp_ref[0:LAT_HALO, :], LAT_HALO, ROWS)
    own0, total0 = (jnp.concatenate(t, axis=0) for t in edge_forward(0, h0_lo, h0_hi, 3))
    h0 = jnp.concatenate([h0_lo, h0_hi], axis=0)
    h1, kept0 = node_forward(0, h0, total0)
    own1, total1 = (jnp.concatenate(t, axis=0) for t in edge_forward(1, h1[:ROWS], h1[ROWS:], 2))
    near = ROWS + 2 * COT_HALO
    h2, kept1 = node_forward(1, h1[:near], total1[:near])
    final_v[...] = h2[:ROWS]

    few = lax.broadcasted_iota(jnp.int32, (MIG, 2 * COT_HALO), 1).astype(F32)
    for k, ref in ((0, upp_ref), (1, low_ref)):
        movers = jnp.transpose(ref[X_AT:SENT, :].astype(F32))[0:MIG, 0:1]
        arr_v[k] = dot(masked(movers == few), h2[ROWS:]).astype(BF16)
    copies = [
        pltpu.make_async_copy(final_v, final_ref.at[0], sems.at[0]),
        pltpu.make_async_copy(arr_v, arr_ref.at[0], sems.at[1]),
        pltpu.make_async_copy(grad_v, grad_ref.at[0], sems.at[2]),
    ]
    copies[0].start()
    copies[1].start()

    def with_zeros(value):
        return jnp.concatenate([value, jnp.zeros((2 * ROWS - value.shape[0],) + value.shape[1:], value.dtype)], axis=0)

    def layer_back(layer, grad, kept, own_total, h, last, keep_rows):
        part, dagg, node_terms = node_backward(layer, grad, kept)
        spread = with_zeros(dagg)
        e = with_zeros(dot_nt(dagg, edge_out_ref[layer]).astype(BF16))
        q_own, q_all, geo = edge_backward(layer, e[:ROWS], e[ROWS:], last)
        out_term = dot_tn(own_total.astype(BF16), spread)
        in_term = dot_tn(h, q_own.astype(BF16))
        straight, _ = edge_weights(layer)
        new = part[:keep_rows] + dot_nt(q_all[:keep_rows].astype(BF16), straight)
        return new, (in_term, geo, out_term) + node_terms

    cot = jnp.concatenate(
        [cot_ref[0], around(low_ref[LAT_HALO:D_AT, :], upp_ref[LAT_HALO:D_AT, :], COT_HALO, 2 * COT_HALO)], axis=0
    ).astype(F32)
    grad1, terms1 = layer_back(1, cot, kept1, own1, h1, 1, ROWS + 64)
    grad0, terms0 = layer_back(0, grad1, kept0, own0, h0, 0, ROWS)
    grad_v[...] = grad0
    copies[2].start()

    size = MAIN // chunks
    per = -(-EXTRA // chunks)
    packed_ref[:, size:, :] = jnp.zeros((chunks, packed_ref.shape[1] - size, L), BF16)
    at = 0
    extra = 0
    for terms in (terms0, terms1):
        in_term, geo, out_term, node_in_term, node_bias_term, node_out_term, gain_term = terms
        for value in (in_term[:, :L], in_term[:, L:], out_term, node_in_term, node_out_term):
            value = value.astype(BF16)
            while value.shape[0]:
                take = min(value.shape[0], size - at % size)
                packed_ref[at // size, at % size : at % size + take, :] = value[:take]
                value = value[take:]
                at += take
        small = [geo[4 + g : 5 + g, :L] - geo[4 + g : 5 + g, L:] for g in range(4)]
        small += [geo[3:4, :L] + geo[3:4, L:], node_bias_term, gain_term]
        for value in small:
            spot = size + extra % per
            packed_ref[extra // per, spot : spot + 1, :] = value.astype(BF16)
            extra += 1

    for copy in copies:
        copy.wait()


def fold_kernel(copies, in_ref, *refs):
    total = in_ref[0].astype(F32)
    for k in range(1, in_ref.shape[0]):
        total += in_ref[k].astype(F32)
    if len(refs) > 1:
        total += refs[0][...].astype(F32)
    total = total.astype(BF16)
    if copies is None:
        refs[-1][...] = total
    else:
        for k in range(copies):
            refs[-1][k] = total


def fold(copies, array, *more):
    shape = array.shape[1:] if copies is None else (copies,) + array.shape[1:]
    return pl.pallas_call(
        lambda *refs: fold_kernel(copies, *refs),
        out_shape=jax.ShapeDtypeStruct(shape, BF16),
        in_specs=vmem(1 + len(more)),
        out_specs=pl.BlockSpec(memory_space=pltpu.VMEM),
        compiler_params=pltpu.CompilerParams(vmem_limit_bytes=VMEM_LIMIT),
        name="fold",
    )(array, *more)


def unpack_kernel(chunks, ref, edge_in, edge_bias, edge_out, node_in, node_bias, node_out, gain):
    size = MAIN // chunks
    per = -(-EXTRA // chunks)
    at = 0
    extra = 0
    for layer in range(2):
        for out, rows in ((edge_in, 2 * L), (edge_out, L), (node_in, 2 * L), (node_out, L)):
            r = 0
            while r < rows:
                take = min(rows - r, size - at % size)
                value = ref[at // size, at % size : at % size + take, :].astype(F32)
                if out is edge_in:
                    out[pl.ds(2 * r + layer, take, stride=2), :] = value
                else:
                    out[layer, r : r + take, :] = value
                r += take
                at += take
        small = []
        for _ in range(7):
            spot = size + extra % per
            small.append(ref[extra // per, spot : spot + 1, :].astype(F32))
            extra += 1
        for g in range(4):
            edge_in[4 * L + 2 * g + layer : 4 * L + 2 * g + layer + 1, :] = small[g]
        edge_bias[layer : layer + 1, :] = small[4]
        node_bias[layer : layer + 1, :] = small[5]
        gain[layer : layer + 1, :] = small[6]


def vmem(count):
    return [pl.BlockSpec(memory_space=pltpu.VMEM)] * count


def solution(mesh):
    n_space = mesh.shape["space"]
    n_x = mesh.shape["replicas"]
    n_c = 2
    n_z = min(16, n_space // n_c)
    n_y = n_space // (n_c * n_z)
    n_l = 2 if n_z > 4 else 1
    n_h = n_z // n_l
    fine = Mesh(mesh.devices.reshape(n_y, n_h, n_l, n_c, n_x), ("y", "zh", "zl", "c", "x"))
    space = ("y", "zh", "zl", "c")
    group = ("zl", "y", "x")
    chunks = n_y * n_l * n_x
    size = MAIN // chunks
    chunk_rows = size + -(-(-(-EXTRA // chunks)) // 8) * 8
    params = pltpu.CompilerParams(vmem_limit_bytes=VMEM_LIMIT)

    def on_device(latents, pairs, geometry, pair_count, cotangent, leaving, *weights):
        sent = jax.ShapeDtypeStruct((SENT, L), BF16)
        to_b, to_a = pl.pallas_call(
            pack_kernel,
            out_shape=(sent, sent),
            in_specs=[pl.BlockSpec(memory_space=pltpu.HBM)] * 6,
            out_specs=tuple(vmem(2)),
            scratch_shapes=[
                pltpu.VMEM((1, 1), jnp.int32),
                pltpu.VMEM((2, EMAX), jnp.int32),
                pltpu.VMEM((4, EMAX), BF16),
                pltpu.VMEM((2, MIG), jnp.int32),
                pltpu.SemaphoreType.DMA((8,)),
            ],
            compiler_params=pltpu.CompilerParams(vmem_limit_bytes=60 * 1024 * 1024),
            name="pack",
        )(pair_count, latents, cotangent, pairs, geometry, leaving)
        half = range(n_space // 2)
        near = [(2 * i, 2 * i + 1) for i in half]
        cross = [(2 * i + 1, (2 * i + 2) % n_space) for i in half]
        from_b = lax.ppermute(to_b, space, cross + [(j, i) for i, j in cross])
        from_a = lax.ppermute(to_a, space, near + [(j, i) for i, j in near])
        own = pl.pallas_call(
            own_kernel,
            out_shape=(
                jax.ShapeDtypeStruct((2, EMAX, ROWS), BF16),
                jax.ShapeDtypeStruct((2, ROWS, EMAX), BF16),
                jax.ShapeDtypeStruct((EMAX, L), F32),
                jax.ShapeDtypeStruct((EMAX, 8), BF16),
                jax.ShapeDtypeStruct((8, EMAX), BF16),
            )
            + (jax.ShapeDtypeStruct((2, L), F32),) * 3,
            in_specs=vmem(6),
            out_specs=tuple(vmem(8)),
            compiler_params=pltpu.CompilerParams(vmem_limit_bytes=16 * 1024 * 1024),
            cost_estimate=pl.CostEstimate(flops=2000000, bytes_accessed=8000000, transcendentals=0),
            name="own",
        )(pair_count, pairs, geometry, weights[1], weights[4], weights[6])
        final, grad, arrivals, packed = pl.pallas_call(
            lambda *refs: main_kernel(chunks, *refs),
            out_shape=(
                jax.ShapeDtypeStruct((1, ROWS, L), BF16),
                jax.ShapeDtypeStruct((1, ROWS, L), F32),
                jax.ShapeDtypeStruct((1, 2, MIG, L), BF16),
                jax.ShapeDtypeStruct((chunks, chunk_rows, L), BF16),
            ),
            in_specs=vmem(16),
            out_specs=tuple([pl.BlockSpec(memory_space=pl.ANY)] * 3 + vmem(1)),
            scratch_shapes=[
                pltpu.VMEM((SENT, L), BF16),
                pltpu.VMEM((SENT, L), BF16),
                pltpu.VMEM((2, 2 * EMAX, ROWS), BF16),
                pltpu.VMEM((2, ROWS, 2 * EMAX), BF16),
                pltpu.VMEM((2 * EMAX, L), F32),
                pltpu.VMEM((2 * EMAX, 8), BF16),
                pltpu.VMEM((2, ALL_PAIRS, 2 * L), F32),
                pltpu.VMEM((NB_BLOCKS, 8, BLK), F32),
                pltpu.VMEM((ALL_PAIRS, 2 * L), BF16),
                pltpu.VMEM((ALL_PAIRS, 2 * L), F32),
                pltpu.VMEM((ALL_PAIRS, 2 * L), BF16),
                pltpu.VMEM((ALL_PAIRS, 2 * L), BF16),
                pltpu.VMEM((ALL_PAIRS, L), F32),
                pltpu.VMEM((ROWS, 2 * L), F32),
                pltpu.VMEM((2 * ROWS, 2 * L), F32),
                pltpu.VMEM((ROWS, L), BF16),
                pltpu.VMEM((2, MIG, L), BF16),
                pltpu.VMEM((ROWS, L), F32),
                pltpu.SemaphoreType.DMA((3,)),
            ],
            compiler_params=params,
            name="steps",
        )(
            latents, cotangent, *own[:5], from_b, from_a,
            weights[0], own[5], weights[2], weights[3], own[6], weights[5], own[7],
        )

        got = fold(None, lax.all_to_all(packed, group, 0, 0, tiled=True))
        got = fold(n_h, got[None], lax.ppermute(got, "c", [(0, 1), (1, 0)]))
        got = lax.all_to_all(got, "zh", 0, 0, tiled=True)
        got = lax.all_to_all(fold(chunks, got), group, 0, 0, tiled=True)

        grads = pl.pallas_call(
            lambda *refs: unpack_kernel(chunks, *refs),
            out_shape=(jax.ShapeDtypeStruct((2 * weights[0].shape[1], L), F32),)
            + tuple(jax.ShapeDtypeStruct(w.shape, F32) for w in weights[1:]),
            in_specs=vmem(1),
            out_specs=tuple(vmem(7)),
            compiler_params=params,
            name="unpack",
        )(got)
        edge_in_grad = jnp.transpose(grads[0].reshape(-1, 2, L), (1, 0, 2))
        return (final, grad, arrivals, edge_in_grad) + tuple(grads[1:])

    return jax.shard_map(
        on_device,
        mesh=fine,
        in_specs=(
            P("x", space, None),
            P("x", None, space),
            P("x", None, space),
            P("x", space),
            P("x", space, None),
            P("x", space, None),
        )
        + (P(),) * 7,
        out_specs=(P("x", space, None), P("x", space, None), P("x", space, None, None)) + (P(),) * 7,
        check_vma=False,
    )
```

```python
import jax
import jax.numpy as jnp
from jax import lax
from jax.experimental import pallas as pl
from jax.experimental.pallas import tpu as pltpu
from jax.sharding import Mesh, PartitionSpec as P


F32 = jnp.float32
BF16 = jnp.bfloat16
L = 128
ROWS = 256
EMAX = 1024
BLK = 256
OWN_BLOCKS = EMAX // BLK
SIDE = 128
NB_BLOCKS = EMAX // SIDE
ALL_PAIRS = EMAX + 2 * EMAX
SURE = (1, 2, 3, 4)
CHUNK = 64
LAT_HALO = 128
COT_HALO = 64
SENT = LAT_HALO + COT_HALO + 64 + 16
D_AT = LAT_HALO + COT_HALO
X_AT = D_AT + 64
MIG = 16
MAIN = 1536
EXTRA = 14
EPS = 1e-05
VMEM_LIMIT = 48 * 1024 * 1024


def dot(a, b):
    return jnp.dot(a, b, preferred_element_type=F32)


def dot_nt(a, b):
    return lax.dot_general(a, b, (((1,), (1,)), ((), ())), preferred_element_type=F32)


def dot_tn(a, b):
    return lax.dot_general(a, b, (((0,), (0,)), ((), ())), preferred_element_type=F32)


def place(row):
    below = row < 0
    above = row >= ROWS
    out = jnp.where(below, -1 - row, row - ROWS)
    block = lax.shift_right_arithmetic(out, 5)
    inner = jnp.where(below, row + 32 * (block + 1), row - ROWS - 32 * block + 32)
    outside = jnp.logical_or(below, above)
    return jnp.where(outside, 64 * block + inner, row), outside


def masked(flag):
    return jnp.where(flag, 1.0, 0.0).astype(BF16)


def pack_kernel(
    count_ref, lat_ref, cot_ref, pairs_ref, geo_ref, leav_ref, b_ref, a_ref, count_v, pairs_v, geo_v, leav_v, sems
):
    first = lax.axis_index("c") == 0
    copies = [
        pltpu.make_async_copy(pairs_ref.at[0], pairs_v, sems.at[0]),
        pltpu.make_async_copy(geo_ref.at[0], geo_v, sems.at[1]),
        pltpu.make_async_copy(leav_ref.at[0], leav_v, sems.at[2]),
        pltpu.make_async_copy(count_ref, count_v, sems.at[7]),
    ]
    ups = (first, jnp.logical_not(first))
    for k, ref in enumerate((a_ref, b_ref)):
        lat_at = pl.multiple_of(jnp.where(ups[k], ROWS - LAT_HALO, 0), LAT_HALO)
        cot_at = pl.multiple_of(jnp.where(ups[k], ROWS - COT_HALO, 0), COT_HALO)
        lat = lat_ref.at[0, pl.ds(lat_at, LAT_HALO), :]
        cot = cot_ref.at[0, pl.ds(cot_at, COT_HALO), :]
        copies.append(pltpu.make_async_copy(lat, ref.at[pl.ds(0, LAT_HALO), :], sems.at[3 + 2 * k]))
        copies.append(pltpu.make_async_copy(cot, ref.at[pl.ds(LAT_HALO, COT_HALO), :], sems.at[4 + 2 * k]))
    for copy in copies:
        copy.start()
    for copy in copies[:4]:
        copy.wait()

    live = lax.broadcasted_iota(jnp.int32, (1, EMAX), 1) < count_v[...]
    own = pairs_v[0:1, :]
    other = pairs_v[1:2, :]
    geo = geo_v[...].astype(F32)
    leav = leav_v[...].astype(F32)
    rows, kinds = [], []
    for k in range(2):
        up = ups[k]
        shift = jnp.where(up, -32 - ROWS, ROWS - 32)
        i_row = own + shift
        j_row = other + shift
        far = jnp.where(up, -1 - jnp.maximum(i_row, j_row), jnp.minimum(i_row, j_row) - ROWS)
        kind = jnp.where(far < 0, 0, lax.shift_right_arithmetic(far, 5) + 1)
        kind = jnp.where(jnp.logical_and(live, kind < 4), kind, 4).astype(F32)
        i_at, _ = place(i_row)
        j_at, j_hi = place(j_row)
        keep = kind < 3.5
        i_at = jnp.where(keep, i_at + 1, 0).astype(F32)
        j_at = jnp.where(keep, j_at + 1, 0).astype(F32)
        hi = jnp.where(j_hi, 1.0, 0.0).astype(F32)
        rows.append(jnp.concatenate([i_at, j_at, hi, jnp.ones((1, EMAX), F32), geo], axis=0).astype(BF16))
        kinds.append(jnp.concatenate([kind[:, 128 * t : 128 * t + 128] for t in range(8)], axis=0))

    flags = [jnp.where(kinds[k] == c, 1.0, 0.0).astype(F32) for k in range(2) for c in range(4)]
    marks = jnp.concatenate(flags, axis=0).astype(BF16)
    row_i = lax.broadcasted_iota(jnp.int32, (128, 128), 0)
    col_i = lax.broadcasted_iota(jnp.int32, (128, 128), 1)
    inside = dot(marks, masked(row_i < col_i))
    sums = dot(marks, jnp.ones((128, 128), BF16))
    row_b = lax.broadcasted_iota(jnp.int32, (64, 64), 0)
    col_b = lax.broadcasted_iota(jnp.int32, (64, 64), 1)
    same = lax.shift_right_logical(row_b, 5) == lax.shift_right_logical(col_b, 5)
    before = dot(masked(jnp.logical_and(same, col_b < row_b)), sums.astype(BF16))
    at = inside + before
    lane = lax.broadcasted_iota(jnp.int32, (1, 128), 1)
    col_w = lax.broadcasted_iota(jnp.int32, (128, BLK), 1).astype(F32)
    places = []
    for k in range(2):
        rank = jnp.full((8, 128), -1.0, F32)
        for c in range(4):
            here = 32 * k + 8 * c
            rank = jnp.where(kinds[k] == c, at[here : here + 8, :], rank)
        places.append(jnp.transpose(rank))

    def move(k, t, shift):
        picks = [masked(places[k][:, q : q + 1] == col_w + shift) for q in range(8)]
        moved = dot(rows[k], jnp.concatenate(picks, axis=0))
        ref = (a_ref, b_ref)[k]
        spot = D_AT + 16 * t
        if not isinstance(t, int):
            spot = pl.multiple_of(spot, 16)
        ref[pl.ds(spot, 16), :] = jnp.concatenate([moved[:, :128], moved[:, 128:]], axis=0).astype(BF16)

    for t in range(2):
        for k in range(2):
            move(k, t, float(BLK * t))
    for k, ref in enumerate((a_ref, b_ref)):
        up = ups[k]
        ends = [before[32 * k + 8 * c + 7, 0] + sums[32 * k + 8 * c + 7, 0] for c in range(4)]
        trips = lax.shift_right_logical(ends[3].astype(jnp.int32) + (BLK - 1), 8)
        ref[D_AT + 32 : X_AT, :] = jnp.zeros((X_AT - D_AT - 32, L), BF16)

        def body(t, carry, k=k):
            move(k, t, (t * BLK).astype(F32))
            return carry

        lax.fori_loop(2, trips, body, 0)
        movers = jnp.where(up, leav[1:2, :] - 224.0, leav[0:1, :] + 32.0)
        tail = jnp.concatenate([movers, jnp.zeros((1, 128 - MIG), F32)], axis=1)
        for c in range(4):
            blocks = ((ends[c].astype(jnp.int32) + (SIDE - 1)) // SIDE).astype(F32)
            tail = jnp.where(lane == MIG + c, blocks, tail)
        ref[X_AT:SENT, :] = jnp.broadcast_to(tail, (16, 128)).astype(BF16)
    for copy in copies[4:]:
        copy.wait()


def grids():
    lanes = lax.broadcasted_iota(jnp.int32, (BLK, ROWS), 1).astype(F32) + 1.0
    subs = lax.broadcasted_iota(jnp.int32, (ROWS, BLK), 0).astype(F32) + 1.0
    return lanes, subs


def set_block(at, rows, lanes, subs, oh, oht, hi, col):
    here = pl.ds(at, BLK)
    cols = jnp.transpose(rows)
    for e in range(2):
        oh[e, here, :] = masked(cols[:, e : e + 1] == lanes)
        oht[e, :, here] = masked(rows[e : e + 1, :] == subs)
    hi[here, :] = jnp.broadcast_to(cols[:, 2:3], (BLK, L))
    col[here, :] = cols.astype(BF16)


def own_kernel(count_ref, pairs_ref, geo_ref, bias_e, bias_n, gain, oh, oht, hi, col, row, bias_e_out, bias_n_out, gain_out):
    bias_e_out[...] = bias_e[...]
    bias_n_out[...] = bias_n[...]
    gain_out[...] = gain[...]
    live = lax.broadcasted_iota(jnp.int32, (1, EMAX), 1) < count_ref[...]
    i_at = pairs_ref[0, 0:1, :] - 32
    j_at, j_out = place(pairs_ref[0, 1:2, :] - 32)
    rows = jnp.concatenate(
        [
            jnp.where(live, i_at + 1, 0).astype(F32),
            jnp.where(live, j_at + 1, 0).astype(F32),
            jnp.where(j_out, 1.0, 0.0).astype(F32),
            jnp.ones((1, EMAX), F32),
            geo_ref[0].astype(F32),
        ],
        axis=0,
    )
    row[...] = rows.astype(BF16)
    lanes, subs = grids()
    for k in range(OWN_BLOCKS):
        set_block(BLK * k, rows[:, BLK * k : BLK * k + BLK], lanes, subs, oh, oht, hi, col)


def main_kernel(
    chunks,
    lat_ref,
    cot_ref,
    own_oh,
    own_oht,
    own_hi,
    own_col,
    own_row,
    b_ref,
    a_ref,
    edge_in_rows,
    edge_bias_ref,
    edge_out_ref,
    node_in_ref,
    node_bias_ref,
    node_out_ref,
    gain_ref,
    final_ref,
    grad_ref,
    arr_ref,
    packed_ref,
    low_ref,
    upp_ref,
    nb_oh,
    nb_oht,
    nb_hi,
    nb_col,
    slope,
    nb_rows,
    work_x,
    work_p,
    work_d,
    work_e,
    work_s,
    t_nb,
    q_nb,
    final_v,
    arr_v,
    grad_v,
    edge_in_wide,
    edge_in_ref,
    sems,
):
    first = lax.axis_index("c") == 0

    @pl.when(first)
    def _():
        low_ref[...] = b_ref[...]
        upp_ref[...] = a_ref[...]

    @pl.when(jnp.logical_not(first))
    def _():
        low_ref[...] = a_ref[...]
        upp_ref[...] = b_ref[...]

    lanes, subs = grids()
    own_refs = (own_oh, own_oht, own_hi, own_col)
    nb_refs = (nb_oh, nb_oht, nb_hi, nb_col)
    own_part = (own_refs, 0, EMAX, 0)

    def nb_part(at, size):
        return nb_refs, at, size, EMAX + at

    info = jnp.maximum(low_ref[X_AT:SENT, :].astype(F32), upp_ref[X_AT:SENT, :].astype(F32))[0:1, :]
    lane = lax.broadcasted_iota(jnp.int32, (1, L), 1)
    reach = [jnp.sum(jnp.where(lane == MIG + c, info, 0.0)).astype(jnp.int32) for c in range(4)]
    low_rows = low_ref[D_AT:X_AT, :].astype(F32)
    upp_rows = upp_ref[D_AT:X_AT, :].astype(F32)
    for k in range(NB_BLOCKS):
        nb_rows[k] = jnp.concatenate([low_rows[8 * k : 8 * k + 8], upp_rows[8 * k : 8 * k + 8]], axis=1)
    def further(last, body):
        def step(k, carry):
            body(pl.multiple_of(BLK * k, BLK))
            return carry

        lax.fori_loop(SURE[last], reach[last], step, 0)

    edge_in_wide[...] = edge_in_rows[...].astype(F32)
    for layer in range(2):
        edge_in_ref[layer] = edge_in_wide[pl.ds(layer, edge_in_wide.shape[0] // 2, stride=2), :].astype(BF16)

    def around(source_low, source_upp, width, height):
        parts = []
        for b in range(width // 32):
            parts.append(source_low[width - 32 * (b + 1) : width - 32 * b])
            parts.append(source_upp[32 * b : 32 * b + 32])
        if height > 2 * width:
            parts.append(jnp.zeros((height - 2 * width, L), parts[0].dtype))
        return jnp.concatenate(parts, axis=0)

    def edge_weights(layer):
        top = edge_in_ref[layer, 0:L, :]
        bottom = edge_in_ref[layer, L : 2 * L, :]
        straight = jnp.concatenate([top, bottom], axis=1)
        return straight, jnp.concatenate([bottom, top], axis=1)

    def whole(parts):
        return pl.ds(parts[0][3], sum(part[2] for part in parts))

    def pieces(parts):
        for refs, at, size, to in parts:
            for r in range(0, size, CHUNK):
                yield refs[2].at[pl.ds(at + r, CHUNK), :], pl.ds(to + r, CHUNK)

    def gather(parts, sources, both, by_i):
        for (refs, at, size, to), source in zip(parts, sources):
            by_i[pl.ds(to, size), :L] = dot(refs[0][0, pl.ds(at, size), :], source).astype(by_i.dtype)
            work_p[pl.ds(to, size), :] = dot(refs[0][1, pl.ds(at, size), :], both)

    def forward_pre(parts, sources, constants):
        both, weights, geo_weights, _ = constants
        gather(parts, sources, both, work_x)
        for hi, here in pieces(parts):
            is_hi = hi[...] > 0.5
            work_x[here, L:] = jnp.where(is_hi, work_p[here, L:], work_p[here, :L]).astype(BF16)
        for refs, at, size, to in parts:
            rows = pl.ds(to, size)
            work_p[rows, :] = dot(work_x[rows, :], weights) + dot(refs[3][pl.ds(at, size), :], geo_weights)

    def forward_act(layer, parts, constants):
        bias = constants[3]
        for hi, here in pieces(parts):
            pre = work_p[here, :] + bias
            sig = 0.5 * jnp.tanh(0.5 * pre) + 0.5
            act = pre * sig
            slope[layer, here, :] = sig + act * (1.0 - sig)
            diff = act[:, :L] - act[:, L:]
            is_hi = hi[...] > 0.5
            none = jnp.zeros_like(diff)
            work_d[here, :L] = diff.astype(BF16)
            work_e[here, :L] = jnp.where(is_hi, none, diff).astype(BF16)
            work_e[here, L:] = jnp.where(is_hi, diff, none).astype(BF16)

    def edge_constants(layer, h_lo, h_hi):
        straight, crossed = edge_weights(layer)
        weights = jnp.concatenate([straight, crossed], axis=0)
        geo_top = edge_in_ref[layer, 2 * L : 2 * L + 4, :].astype(F32)
        geo_weights = jnp.concatenate(
            [jnp.zeros((4, 2 * L), F32), jnp.concatenate([geo_top, -geo_top], axis=1)], axis=0
        ).astype(BF16)
        bias_row = edge_bias_ref[layer : layer + 1, :]
        bias = jnp.concatenate([bias_row, bias_row], axis=1)
        return jnp.concatenate([h_lo, h_hi], axis=1), weights, geo_weights, bias

    def edge_forward(layer, h_lo, h_hi, last, constants, begun):
        t_nb[...] = jnp.zeros_like(t_nb)

        def collect(part):
            refs, at, size, to = part
            rows = pl.ds(to, size)
            by_j = dot(refs[1][1, :, pl.ds(at, size)], work_e[rows, :])
            return dot(refs[1][0, :, pl.ds(at, size)], work_d[rows, :L]), by_j

        def more(at):
            part = nb_part(at, BLK)
            forward_pre([part], [h_hi], constants)
            forward_act(layer, [part], constants)
            by_i, by_j = collect(part)
            t_nb[:, :L] += -by_j[:, :L]
            t_nb[:, L:] += by_i - by_j[:, L:]

        further(last, more)
        parts = [own_part, nb_part(0, BLK * SURE[last])]
        if begun:
            forward_pre(parts[1:], [h_hi], constants)
        else:
            forward_pre(parts, [h_lo, h_hi], constants)
        forward_act(layer, parts, constants)
        by_i, by_j = collect(parts[0])
        nb_i, nb_j = collect(parts[1])
        own = (by_i - by_j[:, :L], -by_j[:, L:])
        total = (own[0] - nb_j[:, :L] + t_nb[:, :L], own[1] + nb_i - nb_j[:, L:] + t_nb[:, L:])
        return own, total

    def node_forward(layer, h, total):
        total = total.astype(BF16)
        weights = jnp.concatenate([node_in_ref[layer, :L, :], through[layer]], axis=0)
        pre = dot(jnp.concatenate([h, total], axis=1), weights) + node_bias_ref[layer : layer + 1, :]
        agg = dot(total[:ROWS], edge_out_ref[layer]).astype(BF16)
        joined = jnp.concatenate([h[:ROWS], agg], axis=1)
        sig = 0.5 * jnp.tanh(0.5 * pre) + 0.5
        act = pre * sig
        hidden = act.astype(BF16)
        out = dot(hidden, node_out_ref[layer])
        centred = out - jnp.mean(out, axis=1, keepdims=True)
        inv = lax.rsqrt(jnp.mean(centred * centred, axis=1, keepdims=True) + EPS)
        normed = centred * inv
        new = (h.astype(F32) + normed * gain_ref[layer : layer + 1, :]).astype(BF16)
        return new, (joined, sig + act * (1.0 - sig), hidden, normed, inv)

    def node_backward(layer, grad, kept):
        size = grad.shape[0]
        joined = kept[0]
        node_slope, hidden, normed, inv = (v[:size] for v in kept[1:])
        gain_term = jnp.sum(grad[:ROWS] * normed[:ROWS], axis=0, keepdims=True)
        dnorm = grad * gain_ref[layer : layer + 1, :]
        mean_a = jnp.mean(dnorm, axis=1, keepdims=True)
        mean_b = jnp.mean(dnorm * normed, axis=1, keepdims=True)
        dout = ((dnorm - mean_a - normed * mean_b) * inv).astype(BF16)
        out_term = dot_tn(hidden[:ROWS], dout[:ROWS])
        dpre = (dot_nt(dout, node_out_ref[layer]) * node_slope).astype(BF16)
        in_term = dot_tn(joined, dpre[:ROWS])
        bias_term = jnp.sum(dpre[:ROWS].astype(F32), axis=0, keepdims=True)
        dx = dot_nt(dpre, node_in_ref[layer])
        e = dot_nt(dpre, through[layer]).astype(BF16)
        return grad + dx[:, :L], dx[:, L:].astype(BF16), e, (in_term, bias_term, out_term, gain_term)

    def backward_rows(layer, parts, sources, both):
        gather(parts, sources, both, work_s)
        for hi, here in pieces(parts):
            is_hi = hi[...] > 0.5
            dd = work_s[here, :] - jnp.where(is_hi, work_p[here, L:], work_p[here, :L])
            dfwd = dd * slope[layer, here, :L]
            drev = -dd * slope[layer, here, L:]
            none = jnp.zeros_like(dfwd)
            work_d[here, :L] = dfwd.astype(BF16)
            work_d[here, L:] = drev.astype(BF16)
            work_x[here, :L] = jnp.where(is_hi, none, drev).astype(BF16)
            work_x[here, L:] = jnp.where(is_hi, none, dfwd).astype(BF16)
            work_e[here, :L] = jnp.where(is_hi, drev, none).astype(BF16)
            work_e[here, L:] = jnp.where(is_hi, dfwd, none).astype(BF16)

    def edge_backward(layer, e_lo, e_hi, last):
        both = jnp.concatenate([e_lo, e_hi], axis=1)
        q_nb[...] = jnp.zeros_like(q_nb)

        def nb_collect(part):
            refs, at, size, to = part
            rows, cols = pl.ds(to, size), pl.ds(at, size)
            lo = dot(refs[1][1, :, cols], work_x[rows, :])
            if last == 0:
                return lo, None
            return lo, dot(refs[1][1, :, cols], work_e[rows, :]) + dot(refs[1][0, :, cols], work_d[rows, :])

        def more(at):
            part = nb_part(at, BLK)
            backward_rows(layer, [part], [e_hi], both)
            lo, up = nb_collect(part)
            q_nb[0:ROWS, :] += lo
            if last:
                q_nb[ROWS:, :] += up

        further(last, more)
        parts = [own_part, nb_part(0, BLK * SURE[last])]
        backward_rows(layer, parts, [e_lo, e_hi], both)
        rows = pl.ds(0, EMAX)
        q_lo = dot(own_oht[0], work_d[rows, :]) + dot(own_oht[1], work_x[rows, :])
        q_hi = dot(own_oht[1], work_e[rows, :])
        nb_lo, nb_up = nb_collect(parts[1])
        own = jnp.concatenate([q_lo, q_hi], axis=0)
        if last == 0:
            total = q_lo + nb_lo + q_nb[0:ROWS, :]
        else:
            total = own + jnp.concatenate([nb_lo, nb_up], axis=0) + q_nb[...]
        return own, total, dot(own_row[...], work_d[rows, :])

    h0_lo = lat_ref[0]
    h0_hi = around(low_ref[0:LAT_HALO, :], upp_ref[0:LAT_HALO, :], LAT_HALO, ROWS)
    constants0 = edge_constants(0, h0_lo, h0_hi)
    forward_pre([own_part], [h0_lo], constants0)
    for k in range(SURE[3]):
        set_block(BLK * k, nb_rows[k], lanes, subs, *nb_refs)
    through = [dot(edge_out_ref[s], node_in_ref[s, L:, :]).astype(BF16) for s in range(2)]
    further(3, lambda at: set_block(at, nb_rows[at // BLK], lanes, subs, *nb_refs))
    own0, total0 = (jnp.concatenate(t, axis=0) for t in edge_forward(0, h0_lo, h0_hi, 3, constants0, True))
    h0 = jnp.concatenate([h0_lo, h0_hi], axis=0)
    h1, kept0 = node_forward(0, h0, total0)
    h1_lo, h1_hi = h1[:ROWS], h1[ROWS:]
    constants1 = edge_constants(1, h1_lo, h1_hi)
    own1, total1 = (jnp.concatenate(t, axis=0) for t in edge_forward(1, h1_lo, h1_hi, 2, constants1, False))
    near = ROWS + 2 * COT_HALO
    h2, kept1 = node_forward(1, h1[:near], total1[:near])
    final_v[...] = h2[:ROWS]

    few = lax.broadcasted_iota(jnp.int32, (MIG, 2 * COT_HALO), 1).astype(F32)
    for k, ref in ((0, upp_ref), (1, low_ref)):
        movers = jnp.transpose(ref[X_AT:SENT, :].astype(F32))[0:MIG, 0:1]
        arr_v[k] = dot(masked(movers == few), h2[ROWS:]).astype(BF16)
    copies = [
        pltpu.make_async_copy(final_v, final_ref.at[0], sems.at[0]),
        pltpu.make_async_copy(arr_v, arr_ref.at[0], sems.at[1]),
        pltpu.make_async_copy(grad_v, grad_ref.at[0], sems.at[2]),
    ]
    copies[0].start()
    copies[1].start()

    def with_zeros(value):
        return jnp.concatenate([value, jnp.zeros((2 * ROWS - value.shape[0],) + value.shape[1:], value.dtype)], axis=0)

    def layer_back(layer, grad, kept, own_total, h, last, keep_rows):
        part, dagg, e, node_terms = node_backward(layer, grad, kept)
        spread = with_zeros(dagg)
        e = with_zeros(e)
        q_own, q_all, geo = edge_backward(layer, e[:ROWS], e[ROWS:], last)
        out_term = dot_tn(own_total.astype(BF16), spread)
        in_term = dot_tn(h, q_own.astype(BF16))
        straight, _ = edge_weights(layer)
        new = part[:keep_rows] + dot_nt(q_all[:keep_rows].astype(BF16), straight)
        return new, (in_term, geo, out_term) + node_terms

    cot = jnp.concatenate(
        [cot_ref[0], around(low_ref[LAT_HALO:D_AT, :], upp_ref[LAT_HALO:D_AT, :], COT_HALO, 2 * COT_HALO)], axis=0
    ).astype(F32)
    grad1, terms1 = layer_back(1, cot, kept1, own1, h1, 1, ROWS + 64)
    grad0, terms0 = layer_back(0, grad1, kept0, own0, h0, 0, ROWS)
    grad_v[...] = grad0
    copies[2].start()

    size = MAIN // chunks
    per = -(-EXTRA // chunks)
    packed_ref[:, size:, :] = jnp.zeros((chunks, packed_ref.shape[1] - size, L), BF16)
    at = 0
    extra = 0
    for terms in (terms0, terms1):
        in_term, geo, out_term, node_in_term, node_bias_term, node_out_term, gain_term = terms
        for value in (in_term[:, :L], in_term[:, L:], out_term, node_in_term, node_out_term):
            value = value.astype(BF16)
            while value.shape[0]:
                take = min(value.shape[0], size - at % size)
                packed_ref[at // size, at % size : at % size + take, :] = value[:take]
                value = value[take:]
                at += take
        small = [geo[4 + g : 5 + g, :L] - geo[4 + g : 5 + g, L:] for g in range(4)]
        small += [geo[3:4, :L] + geo[3:4, L:], node_bias_term, gain_term]
        for value in small:
            spot = size + extra % per
            packed_ref[extra // per, spot : spot + 1, :] = value.astype(BF16)
            extra += 1

    for copy in copies:
        copy.wait()


def fold_kernel(copies, in_ref, *refs):
    total = in_ref[0].astype(F32)
    for k in range(1, in_ref.shape[0]):
        total += in_ref[k].astype(F32)
    if len(refs) > 1:
        total += refs[0][...].astype(F32)
    total = total.astype(BF16)
    if copies is None:
        refs[-1][...] = total
    else:
        for k in range(copies):
            refs[-1][k] = total


def fold(copies, array, *more):
    shape = array.shape[1:] if copies is None else (copies,) + array.shape[1:]
    return pl.pallas_call(
        lambda *refs: fold_kernel(copies, *refs),
        out_shape=jax.ShapeDtypeStruct(shape, BF16),
        in_specs=vmem(1 + len(more)),
        out_specs=pl.BlockSpec(memory_space=pltpu.VMEM),
        compiler_params=pltpu.CompilerParams(vmem_limit_bytes=VMEM_LIMIT),
        name="fold",
    )(array, *more)


def unpack_kernel(chunks, ref, edge_in, edge_bias, edge_out, node_in, node_bias, node_out, gain):
    size = MAIN // chunks
    per = -(-EXTRA // chunks)
    at = 0
    extra = 0
    for layer in range(2):
        for out, rows in ((edge_in, 2 * L), (edge_out, L), (node_in, 2 * L), (node_out, L)):
            r = 0
            while r < rows:
                take = min(rows - r, size - at % size)
                value = ref[at // size, at % size : at % size + take, :].astype(F32)
                if out is edge_in:
                    out[pl.ds(2 * r + layer, take, stride=2), :] = value
                else:
                    out[layer, r : r + take, :] = value
                r += take
                at += take
        small = []
        for _ in range(7):
            spot = size + extra % per
            small.append(ref[extra // per, spot : spot + 1, :].astype(F32))
            extra += 1
        for g in range(4):
            edge_in[4 * L + 2 * g + layer : 4 * L + 2 * g + layer + 1, :] = small[g]
        edge_bias[layer : layer + 1, :] = small[4]
        node_bias[layer : layer + 1, :] = small[5]
        gain[layer : layer + 1, :] = small[6]


def rows_of(array):
    return jnp.transpose(array, (1, 0, 2)).reshape(-1, array.shape[2])


def vmem(count):
    return [pl.BlockSpec(memory_space=pltpu.VMEM)] * count


def solution(mesh):
    n_space = mesh.shape["space"]
    n_x = mesh.shape["replicas"]
    n_c = 2
    n_z = min(16, n_space // n_c)
    n_y = n_space // (n_c * n_z)
    n_l = 2 if n_z > 4 else 1
    n_h = n_z // n_l
    fine = Mesh(mesh.devices.reshape(n_y, n_h, n_l, n_c, n_x), ("y", "zh", "zl", "c", "x"))
    space = ("y", "zh", "zl", "c")
    group = ("zl", "y", "x")
    chunks = n_y * n_l * n_x
    size = MAIN // chunks
    chunk_rows = size + -(-(-(-EXTRA // chunks)) // 8) * 8
    params = pltpu.CompilerParams(vmem_limit_bytes=VMEM_LIMIT)

    def on_device(latents, pairs, geometry, pair_count, cotangent, leaving, *weights):
        sent = jax.ShapeDtypeStruct((SENT, L), BF16)
        to_b, to_a = pl.pallas_call(
            pack_kernel,
            out_shape=(sent, sent),
            in_specs=[pl.BlockSpec(memory_space=pltpu.HBM)] * 6,
            out_specs=tuple(vmem(2)),
            scratch_shapes=[
                pltpu.VMEM((1, 1), jnp.int32),
                pltpu.VMEM((2, EMAX), jnp.int32),
                pltpu.VMEM((4, EMAX), BF16),
                pltpu.VMEM((2, MIG), jnp.int32),
                pltpu.SemaphoreType.DMA((8,)),
            ],
            compiler_params=pltpu.CompilerParams(vmem_limit_bytes=60 * 1024 * 1024),
            name="pack",
        )(pair_count, latents, cotangent, pairs, geometry, leaving)
        half = range(n_space // 2)
        near = [(2 * i, 2 * i + 1) for i in half]
        cross = [(2 * i + 1, (2 * i + 2) % n_space) for i in half]
        from_b = lax.ppermute(to_b, space, cross + [(j, i) for i, j in cross])
        from_a = lax.ppermute(to_a, space, near + [(j, i) for i, j in near])
        own = pl.pallas_call(
            own_kernel,
            out_shape=(
                jax.ShapeDtypeStruct((2, EMAX, ROWS), BF16),
                jax.ShapeDtypeStruct((2, ROWS, EMAX), BF16),
                jax.ShapeDtypeStruct((EMAX, L), F32),
                jax.ShapeDtypeStruct((EMAX, 8), BF16),
                jax.ShapeDtypeStruct((8, EMAX), BF16),
            )
            + (jax.ShapeDtypeStruct((2, L), F32),) * 3,
            in_specs=vmem(6),
            out_specs=tuple(vmem(8)),
            compiler_params=pltpu.CompilerParams(vmem_limit_bytes=16 * 1024 * 1024),
            cost_estimate=pl.CostEstimate(flops=4000000000, bytes_accessed=40000000, transcendentals=0),
            name="own",
        )(pair_count, pairs, geometry, weights[1], weights[4], weights[6])
        final, grad, arrivals, packed = pl.pallas_call(
            lambda *refs: main_kernel(chunks, *refs),
            out_shape=(
                jax.ShapeDtypeStruct((1, ROWS, L), BF16),
                jax.ShapeDtypeStruct((1, ROWS, L), F32),
                jax.ShapeDtypeStruct((1, 2, MIG, L), BF16),
                jax.ShapeDtypeStruct((chunks, chunk_rows, L), BF16),
            ),
            in_specs=vmem(16),
            out_specs=tuple([pl.BlockSpec(memory_space=pl.ANY)] * 3 + vmem(1)),
            scratch_shapes=[
                pltpu.VMEM((SENT, L), BF16),
                pltpu.VMEM((SENT, L), BF16),
                pltpu.VMEM((2, 2 * EMAX, ROWS), BF16),
                pltpu.VMEM((2, ROWS, 2 * EMAX), BF16),
                pltpu.VMEM((2 * EMAX, L), F32),
                pltpu.VMEM((2 * EMAX, 8), BF16),
                pltpu.VMEM((2, ALL_PAIRS, 2 * L), F32),
                pltpu.VMEM((NB_BLOCKS, 8, BLK), F32),
                pltpu.VMEM((ALL_PAIRS, 2 * L), BF16),
                pltpu.VMEM((ALL_PAIRS, 2 * L), F32),
                pltpu.VMEM((ALL_PAIRS, 2 * L), BF16),
                pltpu.VMEM((ALL_PAIRS, 2 * L), BF16),
                pltpu.VMEM((ALL_PAIRS, L), F32),
                pltpu.VMEM((ROWS, 2 * L), F32),
                pltpu.VMEM((2 * ROWS, 2 * L), F32),
                pltpu.VMEM((ROWS, L), BF16),
                pltpu.VMEM((2, MIG, L), BF16),
                pltpu.VMEM((ROWS, L), F32),
                pltpu.VMEM((2 * weights[0].shape[1], L), F32),
                pltpu.VMEM(weights[0].shape, BF16),
                pltpu.SemaphoreType.DMA((3,)),
            ],
            compiler_params=params,
            name="steps",
        )(
            latents, cotangent, *own[:5], from_b, from_a,
            rows_of(weights[0]), own[5], weights[2], weights[3], own[6], weights[5], own[7],
        )

        got = fold(None, lax.all_to_all(packed, group, 0, 0, tiled=True))
        got = fold(n_h, got[None], lax.ppermute(got, "c", [(0, 1), (1, 0)]))
        got = lax.all_to_all(got, "zh", 0, 0, tiled=True)
        got = lax.all_to_all(fold(chunks, got), group, 0, 0, tiled=True)

        grads = pl.pallas_call(
            lambda *refs: unpack_kernel(chunks, *refs),
            out_shape=(jax.ShapeDtypeStruct((2 * weights[0].shape[1], L), F32),)
            + tuple(jax.ShapeDtypeStruct(w.shape, F32) for w in weights[1:]),
            in_specs=vmem(1),
            out_specs=tuple(vmem(7)),
            compiler_params=params,
            name="unpack",
        )(got)
        edge_in_grad = jnp.transpose(grads[0].reshape(-1, 2, L), (1, 0, 2))
        return (final, grad, arrivals, edge_in_grad) + tuple(grads[1:])

    return jax.shard_map(
        on_device,
        mesh=fine,
        in_specs=(
            P("x", space, None),
            P("x", None, space),
            P("x", None, space),
            P("x", space),
            P("x", space, None),
            P("x", space, None),
        )
        + (P(),) * 7,
        out_specs=(P("x", space, None), P("x", space, None), P("x", space, None, None)) + (P(),) * 7,
        check_vma=False,
    )
```

```python
import jax
import jax.numpy as jnp
from jax import lax
from jax.experimental import pallas as pl
from jax.experimental.pallas import tpu as pltpu
from jax.sharding import Mesh, PartitionSpec as P


F32 = jnp.float32
BF16 = jnp.bfloat16
L = 128
ROWS = 256
EMAX = 1024
BLK = 256
OWN_BLOCKS = EMAX // BLK
SIDE = 128
NB_BLOCKS = EMAX // SIDE
ALL_PAIRS = EMAX + 2 * EMAX
SURE = (1, 2, 3, 4)
CHUNK = 64
LAT_HALO = 128
COT_HALO = 64
SENT = LAT_HALO + COT_HALO + 64 + 16
D_AT = LAT_HALO + COT_HALO
X_AT = D_AT + 64
MIG = 16
MAIN = 1536
EXTRA = 14
EPS = 1e-05
VMEM_LIMIT = 48 * 1024 * 1024


def dot(a, b):
    return jnp.dot(a, b, preferred_element_type=F32)


def dot_nt(a, b):
    return lax.dot_general(a, b, (((1,), (1,)), ((), ())), preferred_element_type=F32)


def dot_tn(a, b):
    return lax.dot_general(a, b, (((0,), (0,)), ((), ())), preferred_element_type=F32)


def place(row):
    below = row < 0
    above = row >= ROWS
    out = jnp.where(below, -1 - row, row - ROWS)
    block = lax.shift_right_arithmetic(out, 5)
    inner = jnp.where(below, row + 32 * (block + 1), row - ROWS - 32 * block + 32)
    outside = jnp.logical_or(below, above)
    return jnp.where(outside, 64 * block + inner, row), outside


def masked(flag):
    return jnp.where(flag, 1.0, 0.0).astype(BF16)


def pack_kernel(
    count_ref, lat_ref, cot_ref, pairs_ref, geo_ref, leav_ref, b_ref, a_ref, count_v, pairs_v, geo_v, leav_v, sems
):
    first = lax.axis_index("c") == 0
    copies = [
        pltpu.make_async_copy(pairs_ref.at[0], pairs_v, sems.at[0]),
        pltpu.make_async_copy(geo_ref.at[0], geo_v, sems.at[1]),
        pltpu.make_async_copy(leav_ref.at[0], leav_v, sems.at[2]),
        pltpu.make_async_copy(count_ref, count_v, sems.at[7]),
    ]
    ups = (first, jnp.logical_not(first))
    for k, ref in enumerate((a_ref, b_ref)):
        lat_at = pl.multiple_of(jnp.where(ups[k], ROWS - LAT_HALO, 0), LAT_HALO)
        cot_at = pl.multiple_of(jnp.where(ups[k], ROWS - COT_HALO, 0), COT_HALO)
        lat = lat_ref.at[0, pl.ds(lat_at, LAT_HALO), :]
        cot = cot_ref.at[0, pl.ds(cot_at, COT_HALO), :]
        copies.append(pltpu.make_async_copy(lat, ref.at[pl.ds(0, LAT_HALO), :], sems.at[3 + 2 * k]))
        copies.append(pltpu.make_async_copy(cot, ref.at[pl.ds(LAT_HALO, COT_HALO), :], sems.at[4 + 2 * k]))
    for copy in copies:
        copy.start()
    for copy in copies[:4]:
        copy.wait()

    live = lax.broadcasted_iota(jnp.int32, (1, EMAX), 1) < count_v[...]
    own = pairs_v[0:1, :]
    other = pairs_v[1:2, :]
    geo = geo_v[...].astype(F32)
    leav = leav_v[...].astype(F32)
    rows, kinds = [], []
    for k in range(2):
        up = ups[k]
        shift = jnp.where(up, -32 - ROWS, ROWS - 32)
        i_row = own + shift
        j_row = other + shift
        far = jnp.where(up, -1 - jnp.maximum(i_row, j_row), jnp.minimum(i_row, j_row) - ROWS)
        kind = jnp.where(far < 0, 0, lax.shift_right_arithmetic(far, 5) + 1)
        kind = jnp.where(jnp.logical_and(live, kind < 4), kind, 4).astype(F32)
        i_at, _ = place(i_row)
        j_at, j_hi = place(j_row)
        keep = kind < 3.5
        i_at = jnp.where(keep, i_at + 1, 0).astype(F32)
        j_at = jnp.where(keep, j_at + 1, 0).astype(F32)
        hi = jnp.where(j_hi, 1.0, 0.0).astype(F32)
        rows.append(jnp.concatenate([i_at, j_at, hi, jnp.ones((1, EMAX), F32), geo], axis=0).astype(BF16))
        kinds.append(jnp.concatenate([kind[:, 128 * t : 128 * t + 128] for t in range(8)], axis=0))

    flags = [jnp.where(kinds[k] == c, 1.0, 0.0).astype(F32) for k in range(2) for c in range(4)]
    marks = jnp.concatenate(flags, axis=0).astype(BF16)
    row_i = lax.broadcasted_iota(jnp.int32, (128, 128), 0)
    col_i = lax.broadcasted_iota(jnp.int32, (128, 128), 1)
    inside = dot(marks, masked(row_i < col_i))
    sums = dot(marks, jnp.ones((128, 128), BF16))
    row_b = lax.broadcasted_iota(jnp.int32, (64, 64), 0)
    col_b = lax.broadcasted_iota(jnp.int32, (64, 64), 1)
    same = lax.shift_right_logical(row_b, 5) == lax.shift_right_logical(col_b, 5)
    before = dot(masked(jnp.logical_and(same, col_b < row_b)), sums.astype(BF16))
    at = inside + before
    lane = lax.broadcasted_iota(jnp.int32, (1, 128), 1)
    slots = lax.broadcasted_iota(jnp.int32, (BLK, EMAX), 0).astype(F32)
    places = []
    for k in range(2):
        rank = jnp.full((8, 128), -1.0, F32)
        for c in range(4):
            here = 32 * k + 8 * c
            rank = jnp.where(kinds[k] == c, at[here : here + 8, :], rank)
        places.append(jnp.concatenate([rank[q : q + 1, :] for q in range(8)], axis=1))

    def move(k, t, shift):
        moved = jnp.transpose(dot_nt(masked(places[k] - shift == slots), rows[k]))
        ref = (a_ref, b_ref)[k]
        spot = D_AT + 16 * t
        if not isinstance(t, int):
            spot = pl.multiple_of(spot, 16)
        ref[pl.ds(spot, 16), :] = jnp.concatenate([moved[:, :128], moved[:, 128:]], axis=0).astype(BF16)

    for t in range(2):
        for k in range(2):
            move(k, t, float(BLK * t))
    for k, ref in enumerate((a_ref, b_ref)):
        up = ups[k]
        ends = [before[32 * k + 8 * c + 7, 0] + sums[32 * k + 8 * c + 7, 0] for c in range(4)]
        trips = lax.shift_right_logical(ends[3].astype(jnp.int32) + (BLK - 1), 8)
        ref[D_AT + 32 : X_AT, :] = jnp.zeros((X_AT - D_AT - 32, L), BF16)

        def body(t, carry, k=k):
            move(k, t, (t * BLK).astype(F32))
            return carry

        lax.fori_loop(2, trips, body, 0)
        movers = jnp.where(up, leav[1:2, :] - 224.0, leav[0:1, :] + 32.0)
        tail = jnp.concatenate([movers, jnp.zeros((1, 128 - MIG), F32)], axis=1)
        for c in range(4):
            blocks = ((ends[c].astype(jnp.int32) + (SIDE - 1)) // SIDE).astype(F32)
            tail = jnp.where(lane == MIG + c, blocks, tail)
        ref[X_AT:SENT, :] = jnp.broadcast_to(tail, (16, 128)).astype(BF16)
    for copy in copies[4:]:
        copy.wait()


def grids():
    lanes = lax.broadcasted_iota(jnp.int32, (BLK, ROWS), 1).astype(F32) + 1.0
    subs = lax.broadcasted_iota(jnp.int32, (ROWS, BLK), 0).astype(F32) + 1.0
    return lanes, subs


def set_block(at, rows, lanes, subs, oh, oht, hi, col):
    here = pl.ds(at, BLK)
    cols = jnp.transpose(rows)
    for e in range(2):
        oh[e, here, :] = masked(cols[:, e : e + 1] == lanes)
        oht[e, :, here] = masked(rows[e : e + 1, :] == subs)
    hi[here, :] = jnp.broadcast_to(cols[:, 2:3], (BLK, L))
    col[here, :] = cols.astype(BF16)


def own_kernel(count_ref, pairs_ref, geo_ref, bias_e, bias_n, gain, oh, oht, hi, col, row, bias_e_out, bias_n_out, gain_out):
    bias_e_out[...] = bias_e[...]
    bias_n_out[...] = bias_n[...]
    gain_out[...] = gain[...]
    live = lax.broadcasted_iota(jnp.int32, (1, EMAX), 1) < count_ref[...]
    i_at = pairs_ref[0, 0:1, :] - 32
    j_at, j_out = place(pairs_ref[0, 1:2, :] - 32)
    rows = jnp.concatenate(
        [
            jnp.where(live, i_at + 1, 0).astype(F32),
            jnp.where(live, j_at + 1, 0).astype(F32),
            jnp.where(j_out, 1.0, 0.0).astype(F32),
            jnp.ones((1, EMAX), F32),
            geo_ref[0].astype(F32),
        ],
        axis=0,
    )
    row[...] = rows.astype(BF16)
    lanes, subs = grids()
    for k in range(OWN_BLOCKS):
        set_block(BLK * k, rows[:, BLK * k : BLK * k + BLK], lanes, subs, oh, oht, hi, col)


def main_kernel(
    chunks,
    lat_ref,
    cot_ref,
    own_oh,
    own_oht,
    own_hi,
    own_col,
    own_row,
    b_ref,
    a_ref,
    edge_in_rows,
    edge_bias_ref,
    edge_out_ref,
    node_in_ref,
    node_bias_ref,
    node_out_ref,
    gain_ref,
    final_ref,
    grad_ref,
    arr_ref,
    packed_ref,
    low_ref,
    upp_ref,
    nb_oh,
    nb_oht,
    nb_hi,
    nb_col,
    slope,
    nb_rows,
    work_x,
    work_p,
    work_d,
    work_e,
    work_s,
    from_geo,
    t_nb,
    q_nb,
    final_v,
    arr_v,
    grad_v,
    edge_in_wide,
    edge_in_ref,
    sems,
):
    first = lax.axis_index("c") == 0

    @pl.when(first)
    def _():
        low_ref[...] = b_ref[...]
        upp_ref[...] = a_ref[...]

    @pl.when(jnp.logical_not(first))
    def _():
        low_ref[...] = a_ref[...]
        upp_ref[...] = b_ref[...]

    lanes, subs = grids()
    own_refs = (own_oh, own_oht, own_hi, own_col)
    nb_refs = (nb_oh, nb_oht, nb_hi, nb_col)
    own_part = (own_refs, 0, EMAX, 0)

    def nb_part(at, size):
        return nb_refs, at, size, EMAX + at

    info = jnp.maximum(low_ref[X_AT:SENT, :].astype(F32), upp_ref[X_AT:SENT, :].astype(F32))[0:1, :]
    lane = lax.broadcasted_iota(jnp.int32, (1, L), 1)
    reach = [jnp.sum(jnp.where(lane == MIG + c, info, 0.0)).astype(jnp.int32) for c in range(4)]
    low_rows = low_ref[D_AT:X_AT, :].astype(F32)
    upp_rows = upp_ref[D_AT:X_AT, :].astype(F32)
    for k in range(NB_BLOCKS):
        nb_rows[k] = jnp.concatenate([low_rows[8 * k : 8 * k + 8], upp_rows[8 * k : 8 * k + 8]], axis=1)
    def further(last, body):
        def step(k, carry):
            body(pl.multiple_of(BLK * k, BLK))
            return carry

        lax.fori_loop(SURE[last], reach[last], step, 0)

    edge_in_wide[...] = edge_in_rows[...].astype(F32)
    for layer in range(2):
        edge_in_ref[layer] = edge_in_wide[pl.ds(layer, edge_in_wide.shape[0] // 2, stride=2), :].astype(BF16)

    def around(source_low, source_upp, width, height):
        parts = []
        for b in range(width // 32):
            parts.append(source_low[width - 32 * (b + 1) : width - 32 * b])
            parts.append(source_upp[32 * b : 32 * b + 32])
        if height > 2 * width:
            parts.append(jnp.zeros((height - 2 * width, L), parts[0].dtype))
        return jnp.concatenate(parts, axis=0)

    def edge_weights(layer):
        top = edge_in_ref[layer, 0:L, :]
        bottom = edge_in_ref[layer, L : 2 * L, :]
        straight = jnp.concatenate([top, bottom], axis=1)
        return straight, jnp.concatenate([bottom, top], axis=1)

    def whole(parts):
        return pl.ds(parts[0][3], sum(part[2] for part in parts))

    def pieces(parts):
        for refs, at, size, to in parts:
            for r in range(0, size, CHUNK):
                yield refs[2].at[pl.ds(at + r, CHUNK), :], pl.ds(to + r, CHUNK)

    def gather(parts, sources, both, by_i):
        for (refs, at, size, to), source in zip(parts, sources):
            by_i[pl.ds(to, size), :L] = dot(refs[0][0, pl.ds(at, size), :], source).astype(by_i.dtype)
            work_p[pl.ds(to, size), :] = dot(refs[0][1, pl.ds(at, size), :], both)

    def forward_pre(parts, sources, constants):
        both, weights, _ = constants
        gather(parts, sources, both, work_x)
        for hi, here in pieces(parts):
            is_hi = hi[...] > 0.5
            work_x[here, L:] = jnp.where(is_hi, work_p[here, L:], work_p[here, :L]).astype(BF16)
        for _, _, size, to in parts:
            work_p[pl.ds(to, size), :] = dot(work_x[pl.ds(to, size), :], weights)

    def forward_act(layer, parts, constants):
        bias = constants[2]
        for hi, here in pieces(parts):
            by_pair = from_geo[here, L * layer : L * layer + L]
            fwd = work_p[here, :L] + (bias + by_pair)
            rev = work_p[here, L:] + (bias - by_pair)
            pre = jnp.concatenate([fwd, rev], axis=1)
            sig = 0.5 * jnp.tanh(0.5 * pre) + 0.5
            act = pre * sig
            slope[layer, here, :] = sig + act * (1.0 - sig)
            diff = act[:, :L] - act[:, L:]
            is_hi = hi[...] > 0.5
            none = jnp.zeros_like(diff)
            work_d[here, :L] = diff.astype(BF16)
            work_e[here, :L] = jnp.where(is_hi, none, diff).astype(BF16)
            work_e[here, L:] = jnp.where(is_hi, diff, none).astype(BF16)

    def edge_constants(layer, h_lo, h_hi):
        straight, crossed = edge_weights(layer)
        weights = jnp.concatenate([straight, crossed], axis=0)
        return jnp.concatenate([h_lo, h_hi], axis=1), weights, edge_bias_ref[layer : layer + 1, :]

    def edge_forward(layer, h_lo, h_hi, last, constants, begun):
        t_nb[...] = jnp.zeros_like(t_nb)

        def collect(part):
            refs, at, size, to = part
            rows = pl.ds(to, size)
            by_j = dot(refs[1][1, :, pl.ds(at, size)], work_e[rows, :])
            return dot(refs[1][0, :, pl.ds(at, size)], work_d[rows, :L]), by_j

        def more(at):
            part = nb_part(at, BLK)
            forward_pre([part], [h_hi], constants)
            forward_act(layer, [part], constants)
            by_i, by_j = collect(part)
            t_nb[:, :L] += -by_j[:, :L]
            t_nb[:, L:] += by_i - by_j[:, L:]

        further(last, more)
        parts = [own_part, nb_part(0, BLK * SURE[last])]
        if begun:
            forward_pre(parts[1:], [h_hi], constants)
        else:
            forward_pre(parts, [h_lo, h_hi], constants)
        forward_act(layer, parts, constants)
        by_i, by_j = collect(parts[0])
        nb_i, nb_j = collect(parts[1])
        own = (by_i - by_j[:, :L], -by_j[:, L:])
        total = (own[0] - nb_j[:, :L] + t_nb[:, :L], own[1] + nb_i - nb_j[:, L:] + t_nb[:, L:])
        return own, total

    def node_forward(layer, h, total):
        total = total.astype(BF16)
        weights = jnp.concatenate([node_in_ref[layer, :L, :], through[layer]], axis=0)
        pre = dot(jnp.concatenate([h, total], axis=1), weights) + node_bias_ref[layer : layer + 1, :]
        agg = dot(total[:ROWS], edge_out_ref[layer]).astype(BF16)
        joined = jnp.concatenate([h[:ROWS], agg], axis=1)
        sig = 0.5 * jnp.tanh(0.5 * pre) + 0.5
        act = pre * sig
        hidden = act.astype(BF16)
        out = dot(hidden, node_out_ref[layer])
        centred = out - jnp.mean(out, axis=1, keepdims=True)
        inv = lax.rsqrt(jnp.mean(centred * centred, axis=1, keepdims=True) + EPS)
        normed = centred * inv
        new = (h.astype(F32) + normed * gain_ref[layer : layer + 1, :]).astype(BF16)
        return new, (joined, sig + act * (1.0 - sig), hidden, normed, inv)

    def node_backward(layer, grad, kept):
        size = grad.shape[0]
        joined = kept[0]
        node_slope, hidden, normed, inv = (v[:size] for v in kept[1:])
        gain_term = jnp.sum(grad[:ROWS] * normed[:ROWS], axis=0, keepdims=True)
        dnorm = grad * gain_ref[layer : layer + 1, :]
        mean_a = jnp.mean(dnorm, axis=1, keepdims=True)
        mean_b = jnp.mean(dnorm * normed, axis=1, keepdims=True)
        dout = ((dnorm - mean_a - normed * mean_b) * inv).astype(BF16)
        out_term = dot_tn(hidden[:ROWS], dout[:ROWS])
        dpre = (dot_nt(dout, node_out_ref[layer]) * node_slope).astype(BF16)
        in_term = dot_tn(joined, dpre[:ROWS])
        bias_term = jnp.sum(dpre[:ROWS].astype(F32), axis=0, keepdims=True)
        dx = dot_nt(dpre, node_in_ref[layer])
        e = dot_nt(dpre, through[layer]).astype(BF16)
        return grad + dx[:, :L], dx[:, L:].astype(BF16), e, (in_term, bias_term, out_term, gain_term)

    def backward_rows(layer, parts, sources, both):
        gather(parts, sources, both, work_s)
        for hi, here in pieces(parts):
            is_hi = hi[...] > 0.5
            dd = work_s[here, :] - jnp.where(is_hi, work_p[here, L:], work_p[here, :L])
            dfwd = dd * slope[layer, here, :L]
            drev = -dd * slope[layer, here, L:]
            none = jnp.zeros_like(dfwd)
            work_d[here, :L] = dfwd.astype(BF16)
            work_d[here, L:] = drev.astype(BF16)
            work_x[here, :L] = jnp.where(is_hi, none, drev).astype(BF16)
            work_x[here, L:] = jnp.where(is_hi, none, dfwd).astype(BF16)
            work_e[here, :L] = jnp.where(is_hi, drev, none).astype(BF16)
            work_e[here, L:] = jnp.where(is_hi, dfwd, none).astype(BF16)

    def edge_backward(layer, e_lo, e_hi, last):
        both = jnp.concatenate([e_lo, e_hi], axis=1)
        q_nb[...] = jnp.zeros_like(q_nb)

        def nb_collect(part):
            refs, at, size, to = part
            rows, cols = pl.ds(to, size), pl.ds(at, size)
            lo = dot(refs[1][1, :, cols], work_x[rows, :])
            if last == 0:
                return lo, None
            return lo, dot(refs[1][1, :, cols], work_e[rows, :]) + dot(refs[1][0, :, cols], work_d[rows, :])

        def more(at):
            part = nb_part(at, BLK)
            backward_rows(layer, [part], [e_hi], both)
            lo, up = nb_collect(part)
            q_nb[0:ROWS, :] += lo
            if last:
                q_nb[ROWS:, :] += up

        further(last, more)
        parts = [own_part, nb_part(0, BLK * SURE[last])]
        backward_rows(layer, parts, [e_lo, e_hi], both)
        rows = pl.ds(0, EMAX)
        q_lo = dot(own_oht[0], work_d[rows, :]) + dot(own_oht[1], work_x[rows, :])
        q_hi = dot(own_oht[1], work_e[rows, :])
        nb_lo, nb_up = nb_collect(parts[1])
        own = jnp.concatenate([q_lo, q_hi], axis=0)
        if last == 0:
            total = q_lo + nb_lo + q_nb[0:ROWS, :]
        else:
            total = own + jnp.concatenate([nb_lo, nb_up], axis=0) + q_nb[...]
        return own, total, dot(own_row[...], work_d[rows, :])

    h0_lo = lat_ref[0]
    h0_hi = around(low_ref[0:LAT_HALO, :], upp_ref[0:LAT_HALO, :], LAT_HALO, ROWS)
    constants0 = edge_constants(0, h0_lo, h0_hi)
    geo_weights = jnp.concatenate([edge_in_ref[s, 2 * L : 2 * L + 4, :].astype(F32) for s in range(2)], axis=1)
    geo_weights = jnp.concatenate([jnp.zeros((4, 2 * L), F32), geo_weights], axis=0).astype(BF16)

    def set_geo(part):
        refs, at, size, to = part
        from_geo[pl.ds(to, size), :] = dot(refs[3][pl.ds(at, size), :], geo_weights)

    def set_further(at):
        set_block(at, nb_rows[at // BLK], lanes, subs, *nb_refs)
        set_geo(nb_part(at, BLK))

    forward_pre([own_part], [h0_lo], constants0)
    set_geo(own_part)
    for k in range(SURE[3]):
        set_block(BLK * k, nb_rows[k], lanes, subs, *nb_refs)
    through = [dot(edge_out_ref[s], node_in_ref[s, L:, :]).astype(BF16) for s in range(2)]
    set_geo(nb_part(0, BLK * SURE[3]))
    further(3, set_further)
    own0, total0 = (jnp.concatenate(t, axis=0) for t in edge_forward(0, h0_lo, h0_hi, 3, constants0, True))
    h0 = jnp.concatenate([h0_lo, h0_hi], axis=0)
    h1, kept0 = node_forward(0, h0, total0)
    h1_lo, h1_hi = h1[:ROWS], h1[ROWS:]
    constants1 = edge_constants(1, h1_lo, h1_hi)
    own1, total1 = (jnp.concatenate(t, axis=0) for t in edge_forward(1, h1_lo, h1_hi, 2, constants1, False))
    near = ROWS + 2 * COT_HALO
    h2, kept1 = node_forward(1, h1[:near], total1[:near])
    final_v[...] = h2[:ROWS]

    few = lax.broadcasted_iota(jnp.int32, (MIG, 2 * COT_HALO), 1).astype(F32)
    for k, ref in ((0, upp_ref), (1, low_ref)):
        movers = jnp.transpose(ref[X_AT:SENT, :].astype(F32))[0:MIG, 0:1]
        arr_v[k] = dot(masked(movers == few), h2[ROWS:]).astype(BF16)
    copies = [
        pltpu.make_async_copy(final_v, final_ref.at[0], sems.at[0]),
        pltpu.make_async_copy(arr_v, arr_ref.at[0], sems.at[1]),
        pltpu.make_async_copy(grad_v, grad_ref.at[0], sems.at[2]),
    ]
    copies[0].start()
    copies[1].start()

    def with_zeros(value):
        return jnp.concatenate([value, jnp.zeros((2 * ROWS - value.shape[0],) + value.shape[1:], value.dtype)], axis=0)

    def layer_back(layer, grad, kept, own_total, h, last, keep_rows):
        part, dagg, e, node_terms = node_backward(layer, grad, kept)
        spread = with_zeros(dagg)
        e = with_zeros(e)
        q_own, q_all, geo = edge_backward(layer, e[:ROWS], e[ROWS:], last)
        out_term = dot_tn(own_total.astype(BF16), spread)
        in_term = dot_tn(h, q_own.astype(BF16))
        straight, _ = edge_weights(layer)
        new = part[:keep_rows] + dot_nt(q_all[:keep_rows].astype(BF16), straight)
        return new, (in_term, geo, out_term) + node_terms

    cot = jnp.concatenate(
        [cot_ref[0], around(low_ref[LAT_HALO:D_AT, :], upp_ref[LAT_HALO:D_AT, :], COT_HALO, 2 * COT_HALO)], axis=0
    ).astype(F32)
    grad1, terms1 = layer_back(1, cot, kept1, own1, h1, 1, ROWS + 64)
    grad0, terms0 = layer_back(0, grad1, kept0, own0, h0, 0, ROWS)
    grad_v[...] = grad0
    copies[2].start()

    size = MAIN // chunks
    per = -(-EXTRA // chunks)
    packed_ref[:, size:, :] = jnp.zeros((chunks, packed_ref.shape[1] - size, L), BF16)
    at = 0
    extra = 0
    for terms in (terms0, terms1):
        in_term, geo, out_term, node_in_term, node_bias_term, node_out_term, gain_term = terms
        for value in (in_term[:, :L], in_term[:, L:], out_term, node_in_term, node_out_term):
            value = value.astype(BF16)
            while value.shape[0]:
                take = min(value.shape[0], size - at % size)
                packed_ref[at // size, at % size : at % size + take, :] = value[:take]
                value = value[take:]
                at += take
        small = [geo[4 + g : 5 + g, :L] - geo[4 + g : 5 + g, L:] for g in range(4)]
        small += [geo[3:4, :L] + geo[3:4, L:], node_bias_term, gain_term]
        for value in small:
            spot = size + extra % per
            packed_ref[extra // per, spot : spot + 1, :] = value.astype(BF16)
            extra += 1

    for copy in copies:
        copy.wait()


def fold_kernel(copies, in_ref, *refs):
    total = in_ref[0].astype(F32)
    for k in range(1, in_ref.shape[0]):
        total += in_ref[k].astype(F32)
    if len(refs) > 1:
        total += refs[0][...].astype(F32)
    total = total.astype(BF16)
    if copies is None:
        refs[-1][...] = total
    else:
        for k in range(copies):
            refs[-1][k] = total


def fold(copies, array, *more):
    shape = array.shape[1:] if copies is None else (copies,) + array.shape[1:]
    return pl.pallas_call(
        lambda *refs: fold_kernel(copies, *refs),
        out_shape=jax.ShapeDtypeStruct(shape, BF16),
        in_specs=vmem(1 + len(more)),
        out_specs=pl.BlockSpec(memory_space=pltpu.VMEM),
        compiler_params=pltpu.CompilerParams(vmem_limit_bytes=VMEM_LIMIT),
        name="fold",
    )(array, *more)


def unpack_kernel(chunks, ref, edge_in, edge_bias, edge_out, node_in, node_bias, node_out, gain):
    size = MAIN // chunks
    per = -(-EXTRA // chunks)
    at = 0
    extra = 0
    for layer in range(2):
        for out, rows in ((edge_in, 2 * L), (edge_out, L), (node_in, 2 * L), (node_out, L)):
            r = 0
            while r < rows:
                take = min(rows - r, size - at % size)
                value = ref[at // size, at % size : at % size + take, :].astype(F32)
                if out is edge_in:
                    out[pl.ds(2 * r + layer, take, stride=2), :] = value
                else:
                    out[layer, r : r + take, :] = value
                r += take
                at += take
        small = []
        for _ in range(7):
            spot = size + extra % per
            small.append(ref[extra // per, spot : spot + 1, :].astype(F32))
            extra += 1
        for g in range(4):
            edge_in[4 * L + 2 * g + layer : 4 * L + 2 * g + layer + 1, :] = small[g]
        edge_bias[layer : layer + 1, :] = small[4]
        node_bias[layer : layer + 1, :] = small[5]
        gain[layer : layer + 1, :] = small[6]


def rows_of(array):
    return jnp.transpose(array, (1, 0, 2)).reshape(-1, array.shape[2])


def vmem(count):
    return [pl.BlockSpec(memory_space=pltpu.VMEM)] * count


def solution(mesh):
    n_space = mesh.shape["space"]
    n_x = mesh.shape["replicas"]
    n_c = 2
    n_z = min(16, n_space // n_c)
    n_y = n_space // (n_c * n_z)
    n_l = 2 if n_z > 4 else 1
    n_h = n_z // n_l
    n_b = 2 if n_h > 4 else 1
    fine = Mesh(mesh.devices.reshape(n_y, n_h // n_b, n_b, n_l, n_c, n_x), ("y", "za", "zb", "zl", "c", "x"))
    space = ("y", "za", "zb", "zl", "c")
    group = ("zl", "y", "x")
    chunks = n_y * n_l * n_x
    size = MAIN // chunks
    chunk_rows = size + -(-(-(-EXTRA // chunks)) // 8) * 8
    params = pltpu.CompilerParams(vmem_limit_bytes=VMEM_LIMIT)

    def on_device(latents, pairs, geometry, pair_count, cotangent, leaving, *weights):
        sent = jax.ShapeDtypeStruct((SENT, L), BF16)
        to_b, to_a = pl.pallas_call(
            pack_kernel,
            out_shape=(sent, sent),
            in_specs=[pl.BlockSpec(memory_space=pltpu.HBM)] * 6,
            out_specs=tuple(vmem(2)),
            scratch_shapes=[
                pltpu.VMEM((1, 1), jnp.int32),
                pltpu.VMEM((2, EMAX), jnp.int32),
                pltpu.VMEM((4, EMAX), BF16),
                pltpu.VMEM((2, MIG), jnp.int32),
                pltpu.SemaphoreType.DMA((8,)),
            ],
            compiler_params=pltpu.CompilerParams(vmem_limit_bytes=60 * 1024 * 1024),
            name="pack",
        )(pair_count, latents, cotangent, pairs, geometry, leaving)
        half = range(n_space // 2)
        near = [(2 * i, 2 * i + 1) for i in half]
        cross = [(2 * i + 1, (2 * i + 2) % n_space) for i in half]
        from_b = lax.ppermute(to_b, space, cross + [(j, i) for i, j in cross])
        from_a = lax.ppermute(to_a, space, near + [(j, i) for i, j in near])
        own = pl.pallas_call(
            own_kernel,
            out_shape=(
                jax.ShapeDtypeStruct((2, EMAX, ROWS), BF16),
                jax.ShapeDtypeStruct((2, ROWS, EMAX), BF16),
                jax.ShapeDtypeStruct((EMAX, L), F32),
                jax.ShapeDtypeStruct((EMAX, 8), BF16),
                jax.ShapeDtypeStruct((8, EMAX), BF16),
            )
            + (jax.ShapeDtypeStruct((2, L), F32),) * 3,
            in_specs=vmem(6),
            out_specs=tuple(vmem(8)),
            compiler_params=pltpu.CompilerParams(vmem_limit_bytes=16 * 1024 * 1024),
            cost_estimate=pl.CostEstimate(flops=4000000000, bytes_accessed=40000000, transcendentals=0),
            name="own",
        )(pair_count, pairs, geometry, weights[1], weights[4], weights[6])
        final, grad, arrivals, packed = pl.pallas_call(
            lambda *refs: main_kernel(chunks, *refs),
            out_shape=(
                jax.ShapeDtypeStruct((1, ROWS, L), BF16),
                jax.ShapeDtypeStruct((1, ROWS, L), F32),
                jax.ShapeDtypeStruct((1, 2, MIG, L), BF16),
                jax.ShapeDtypeStruct((chunks, chunk_rows, L), BF16),
            ),
            in_specs=vmem(16),
            out_specs=tuple([pl.BlockSpec(memory_space=pl.ANY)] * 3 + vmem(1)),
            scratch_shapes=[
                pltpu.VMEM((SENT, L), BF16),
                pltpu.VMEM((SENT, L), BF16),
                pltpu.VMEM((2, 2 * EMAX, ROWS), BF16),
                pltpu.VMEM((2, ROWS, 2 * EMAX), BF16),
                pltpu.VMEM((2 * EMAX, L), F32),
                pltpu.VMEM((2 * EMAX, 8), BF16),
                pltpu.VMEM((2, ALL_PAIRS, 2 * L), F32),
                pltpu.VMEM((NB_BLOCKS, 8, BLK), F32),
                pltpu.VMEM((ALL_PAIRS, 2 * L), BF16),
                pltpu.VMEM((ALL_PAIRS, 2 * L), F32),
                pltpu.VMEM((ALL_PAIRS, 2 * L), BF16),
                pltpu.VMEM((ALL_PAIRS, 2 * L), BF16),
                pltpu.VMEM((ALL_PAIRS, L), F32),
                pltpu.VMEM((ALL_PAIRS, 2 * L), F32),
                pltpu.VMEM((ROWS, 2 * L), F32),
                pltpu.VMEM((2 * ROWS, 2 * L), F32),
                pltpu.VMEM((ROWS, L), BF16),
                pltpu.VMEM((2, MIG, L), BF16),
                pltpu.VMEM((ROWS, L), F32),
                pltpu.VMEM((2 * weights[0].shape[1], L), F32),
                pltpu.VMEM(weights[0].shape, BF16),
                pltpu.SemaphoreType.DMA((3,)),
            ],
            compiler_params=params,
            name="steps",
        )(
            latents, cotangent, *own[:5], from_b, from_a,
            rows_of(weights[0]), own[5], weights[2], weights[3], own[6], weights[5], own[7],
        )

        got = fold(None, lax.all_to_all(packed, group, 0, 0, tiled=True))
        got = fold(n_h, got[None], lax.ppermute(got, "c", [(0, 1), (1, 0)]))
        got = lax.all_to_all(got, ("zb", "za"), 0, 0, tiled=True)
        got = lax.all_to_all(fold(chunks, got), group, 0, 0, tiled=True)

        grads = pl.pallas_call(
            lambda *refs: unpack_kernel(chunks, *refs),
            out_shape=(jax.ShapeDtypeStruct((2 * weights[0].shape[1], L), F32),)
            + tuple(jax.ShapeDtypeStruct(w.shape, F32) for w in weights[1:]),
            in_specs=vmem(1),
            out_specs=tuple(vmem(7)),
            compiler_params=params,
            name="unpack",
        )(got)
        edge_in_grad = jnp.transpose(grads[0].reshape(-1, 2, L), (1, 0, 2))
        return (final, grad, arrivals, edge_in_grad) + tuple(grads[1:])

    return jax.shard_map(
        on_device,
        mesh=fine,
        in_specs=(
            P("x", space, None),
            P("x", None, space),
            P("x", None, space),
            P("x", space),
            P("x", space, None),
            P("x", space, None),
        )
        + (P(),) * 7,
        out_specs=(P("x", space, None), P("x", space, None), P("x", space, None, None)) + (P(),) * 7,
        check_vma=False,
    )
```

```python
import jax
import jax.numpy as jnp
from jax import lax
from jax.experimental import pallas as pl
from jax.experimental.pallas import tpu as pltpu
from jax.sharding import Mesh, PartitionSpec as P


F32 = jnp.float32
BF16 = jnp.bfloat16
L = 128
ROWS = 256
EMAX = 1024
BLK = 256
OWN_BLOCKS = EMAX // BLK
SIDE = 128
NB_BLOCKS = EMAX // SIDE
ALL_PAIRS = EMAX + 2 * EMAX
SURE = (1, 2, 3, 4)
CHUNK = 32
LAT_HALO = 128
COT_HALO = 64
SENT = LAT_HALO + COT_HALO + 64 + 16
D_AT = LAT_HALO + COT_HALO
X_AT = D_AT + 64
MIG = 16
MAIN = 1536
EXTRA = 14
EPS = 1e-05
VMEM_LIMIT = 48 * 1024 * 1024


def dot(a, b):
    return jnp.dot(a, b, preferred_element_type=F32)


def dot_nt(a, b):
    return lax.dot_general(a, b, (((1,), (1,)), ((), ())), preferred_element_type=F32)


def dot_tn(a, b):
    return lax.dot_general(a, b, (((0,), (0,)), ((), ())), preferred_element_type=F32)


def place(row):
    below = row < 0
    above = row >= ROWS
    out = jnp.where(below, -1 - row, row - ROWS)
    block = lax.shift_right_arithmetic(out, 5)
    inner = jnp.where(below, row + 32 * (block + 1), row - ROWS - 32 * block + 32)
    outside = jnp.logical_or(below, above)
    return jnp.where(outside, 64 * block + inner, row), outside


def masked(flag):
    return jnp.where(flag, 1.0, 0.0).astype(BF16)


def pack_kernel(
    count_ref, lat_ref, cot_ref, pairs_ref, geo_ref, leav_ref, b_ref, a_ref, count_v, pairs_v, geo_v, leav_v, sems
):
    first = lax.axis_index("c") == 0
    copies = [
        pltpu.make_async_copy(pairs_ref.at[0], pairs_v, sems.at[0]),
        pltpu.make_async_copy(geo_ref.at[0], geo_v, sems.at[1]),
        pltpu.make_async_copy(leav_ref.at[0], leav_v, sems.at[2]),
        pltpu.make_async_copy(count_ref, count_v, sems.at[7]),
    ]
    ups = (first, jnp.logical_not(first))
    for k, ref in enumerate((a_ref, b_ref)):
        lat_at = pl.multiple_of(jnp.where(ups[k], ROWS - LAT_HALO, 0), LAT_HALO)
        cot_at = pl.multiple_of(jnp.where(ups[k], ROWS - COT_HALO, 0), COT_HALO)
        lat = lat_ref.at[0, pl.ds(lat_at, LAT_HALO), :]
        cot = cot_ref.at[0, pl.ds(cot_at, COT_HALO), :]
        copies.append(pltpu.make_async_copy(lat, ref.at[pl.ds(0, LAT_HALO), :], sems.at[3 + 2 * k]))
        copies.append(pltpu.make_async_copy(cot, ref.at[pl.ds(LAT_HALO, COT_HALO), :], sems.at[4 + 2 * k]))
    for copy in copies:
        copy.start()
    for copy in copies[:4]:
        copy.wait()

    live = lax.broadcasted_iota(jnp.int32, (1, EMAX), 1) < count_v[...]
    own = pairs_v[0:1, :]
    other = pairs_v[1:2, :]
    geo = geo_v[...].astype(F32)
    leav = leav_v[...].astype(F32)
    rows, kinds = [], []
    for k in range(2):
        up = ups[k]
        shift = jnp.where(up, -32 - ROWS, ROWS - 32)
        i_row = own + shift
        j_row = other + shift
        far = jnp.where(up, -1 - jnp.maximum(i_row, j_row), jnp.minimum(i_row, j_row) - ROWS)
        kind = jnp.where(far < 0, 0, lax.shift_right_arithmetic(far, 5) + 1)
        kind = jnp.where(jnp.logical_and(live, kind < 4), kind, 4).astype(F32)
        i_at, _ = place(i_row)
        j_at, j_hi = place(j_row)
        keep = kind < 3.5
        i_at = jnp.where(keep, i_at + 1, 0).astype(F32)
        j_at = jnp.where(keep, j_at + 1, 0).astype(F32)
        hi = jnp.where(j_hi, 1.0, 0.0).astype(F32)
        rows.append(jnp.concatenate([i_at, j_at, hi, jnp.ones((1, EMAX), F32), geo], axis=0).astype(BF16))
        kinds.append(jnp.concatenate([kind[:, 128 * t : 128 * t + 128] for t in range(8)], axis=0))

    flags = [jnp.where(kinds[k] == c, 1.0, 0.0).astype(F32) for k in range(2) for c in range(4)]
    marks = jnp.concatenate(flags, axis=0).astype(BF16)
    row_i = lax.broadcasted_iota(jnp.int32, (128, 128), 0)
    col_i = lax.broadcasted_iota(jnp.int32, (128, 128), 1)
    inside = dot(marks, masked(row_i < col_i))
    sums = dot(marks, jnp.ones((128, 128), BF16))
    row_b = lax.broadcasted_iota(jnp.int32, (64, 64), 0)
    col_b = lax.broadcasted_iota(jnp.int32, (64, 64), 1)
    same = lax.shift_right_logical(row_b, 5) == lax.shift_right_logical(col_b, 5)
    before = dot(masked(jnp.logical_and(same, col_b < row_b)), sums.astype(BF16))
    at = inside + before
    lane = lax.broadcasted_iota(jnp.int32, (1, 128), 1)
    slots = lax.broadcasted_iota(jnp.int32, (BLK, EMAX), 0).astype(F32)
    places = []
    for k in range(2):
        rank = jnp.full((8, 128), -1.0, F32)
        for c in range(4):
            here = 32 * k + 8 * c
            rank = jnp.where(kinds[k] == c, at[here : here + 8, :], rank)
        places.append(jnp.concatenate([rank[q : q + 1, :] for q in range(8)], axis=1))

    def move(k, t, shift):
        moved = jnp.transpose(dot_nt(masked(places[k] - shift == slots), rows[k]))
        ref = (a_ref, b_ref)[k]
        spot = D_AT + 16 * t
        if not isinstance(t, int):
            spot = pl.multiple_of(spot, 16)
        ref[pl.ds(spot, 16), :] = jnp.concatenate([moved[:, :128], moved[:, 128:]], axis=0).astype(BF16)

    for t in range(2):
        for k in range(2):
            move(k, t, float(BLK * t))
    for k, ref in enumerate((a_ref, b_ref)):
        up = ups[k]
        ends = [before[32 * k + 8 * c + 7, 0] + sums[32 * k + 8 * c + 7, 0] for c in range(4)]
        trips = lax.shift_right_logical(ends[3].astype(jnp.int32) + (BLK - 1), 8)
        ref[D_AT + 32 : X_AT, :] = jnp.zeros((X_AT - D_AT - 32, L), BF16)

        def body(t, carry, k=k):
            move(k, t, (t * BLK).astype(F32))
            return carry

        lax.fori_loop(2, trips, body, 0)
        movers = jnp.where(up, leav[1:2, :] - 224.0, leav[0:1, :] + 32.0)
        tail = jnp.concatenate([movers, jnp.zeros((1, 128 - MIG), F32)], axis=1)
        for c in range(4):
            blocks = ((ends[c].astype(jnp.int32) + (SIDE - 1)) // SIDE).astype(F32)
            tail = jnp.where(lane == MIG + c, blocks, tail)
        ref[X_AT:SENT, :] = jnp.broadcast_to(tail, (16, 128)).astype(BF16)
    for copy in copies[4:]:
        copy.wait()


def grids():
    lanes = lax.broadcasted_iota(jnp.int32, (BLK, ROWS), 1).astype(F32) + 1.0
    subs = lax.broadcasted_iota(jnp.int32, (ROWS, BLK), 0).astype(F32) + 1.0
    return lanes, subs


def set_block(at, rows, lanes, subs, oh, oht, hi, col):
    here = pl.ds(at, BLK)
    cols = jnp.transpose(rows)
    for e in range(2):
        oh[e, here, :] = masked(cols[:, e : e + 1] == lanes)
        oht[e, :, here] = masked(rows[e : e + 1, :] == subs)
    hi[here, :] = jnp.broadcast_to(cols[:, 2:3], (BLK, L))
    col[here, :] = cols.astype(BF16)


def own_kernel(count_ref, pairs_ref, geo_ref, bias_e, bias_n, gain, oh, oht, hi, col, row, bias_e_out, bias_n_out, gain_out):
    bias_e_out[...] = bias_e[...]
    bias_n_out[...] = bias_n[...]
    gain_out[...] = gain[...]
    live = lax.broadcasted_iota(jnp.int32, (1, EMAX), 1) < count_ref[...]
    i_at = pairs_ref[0, 0:1, :] - 32
    j_at, j_out = place(pairs_ref[0, 1:2, :] - 32)
    rows = jnp.concatenate(
        [
            jnp.where(live, i_at + 1, 0).astype(F32),
            jnp.where(live, j_at + 1, 0).astype(F32),
            jnp.where(j_out, 1.0, 0.0).astype(F32),
            jnp.ones((1, EMAX), F32),
            geo_ref[0].astype(F32),
        ],
        axis=0,
    )
    row[...] = rows.astype(BF16)
    lanes, subs = grids()
    for k in range(OWN_BLOCKS):
        set_block(BLK * k, rows[:, BLK * k : BLK * k + BLK], lanes, subs, oh, oht, hi, col)


def main_kernel(
    chunks,
    lat_ref,
    cot_ref,
    own_oh,
    own_oht,
    own_hi,
    own_col,
    own_row,
    b_ref,
    a_ref,
    edge_in_rows,
    edge_bias_ref,
    edge_out_ref,
    node_in_ref,
    node_bias_ref,
    node_out_ref,
    gain_ref,
    final_ref,
    grad_ref,
    arr_ref,
    packed_ref,
    low_ref,
    upp_ref,
    nb_oh,
    nb_oht,
    nb_hi,
    nb_col,
    slope,
    nb_rows,
    work_x,
    work_p,
    work_d,
    work_e,
    work_s,
    from_geo,
    t_nb,
    q_nb,
    final_v,
    arr_v,
    grad_v,
    edge_in_wide,
    edge_in_ref,
    sems,
):
    first = lax.axis_index("c") == 0

    @pl.when(first)
    def _():
        low_ref[...] = b_ref[...]
        upp_ref[...] = a_ref[...]

    @pl.when(jnp.logical_not(first))
    def _():
        low_ref[...] = a_ref[...]
        upp_ref[...] = b_ref[...]

    lanes, subs = grids()
    own_refs = (own_oh, own_oht, own_hi, own_col)
    nb_refs = (nb_oh, nb_oht, nb_hi, nb_col)
    own_part = (own_refs, 0, EMAX, 0)

    def nb_part(at, size):
        return nb_refs, at, size, EMAX + at

    info = jnp.maximum(low_ref[X_AT:SENT, :].astype(F32), upp_ref[X_AT:SENT, :].astype(F32))[0:1, :]
    lane = lax.broadcasted_iota(jnp.int32, (1, L), 1)
    reach = [jnp.sum(jnp.where(lane == MIG + c, info, 0.0)).astype(jnp.int32) for c in range(4)]
    low_rows = low_ref[D_AT:X_AT, :].astype(F32)
    upp_rows = upp_ref[D_AT:X_AT, :].astype(F32)
    for k in range(NB_BLOCKS):
        nb_rows[k] = jnp.concatenate([low_rows[8 * k : 8 * k + 8], upp_rows[8 * k : 8 * k + 8]], axis=1)
    def further(last, body):
        def step(k, carry):
            body(pl.multiple_of(BLK * k, BLK))
            return carry

        lax.fori_loop(SURE[last], reach[last], step, 0)

    edge_in_wide[...] = edge_in_rows[...].astype(F32)
    for layer in range(2):
        edge_in_ref[layer] = edge_in_wide[pl.ds(layer, edge_in_wide.shape[0] // 2, stride=2), :].astype(BF16)

    def around(source_low, source_upp, width, height):
        parts = []
        for b in range(width // 32):
            parts.append(source_low[width - 32 * (b + 1) : width - 32 * b])
            parts.append(source_upp[32 * b : 32 * b + 32])
        if height > 2 * width:
            parts.append(jnp.zeros((height - 2 * width, L), parts[0].dtype))
        return jnp.concatenate(parts, axis=0)

    def edge_weights(layer):
        top = edge_in_ref[layer, 0:L, :]
        bottom = edge_in_ref[layer, L : 2 * L, :]
        straight = jnp.concatenate([top, bottom], axis=1)
        return straight, jnp.concatenate([bottom, top], axis=1)

    def whole(parts):
        return pl.ds(parts[0][3], sum(part[2] for part in parts))

    def pieces(parts):
        for refs, at, size, to in parts:
            for r in range(0, size, CHUNK):
                yield refs[2].at[pl.ds(at + r, CHUNK), :], pl.ds(to + r, CHUNK)

    def gather(parts, sources, both, by_i):
        for (refs, at, size, to), source in zip(parts, sources):
            by_i[pl.ds(to, size), :L] = dot(refs[0][0, pl.ds(at, size), :], source).astype(by_i.dtype)
            work_p[pl.ds(to, size), :] = dot(refs[0][1, pl.ds(at, size), :], both)

    def forward_pre(parts, sources, constants):
        both, weights, _ = constants
        gather(parts, sources, both, work_x)
        for hi, here in pieces(parts):
            is_hi = hi[...] > 0.5
            work_x[here, L:] = jnp.where(is_hi, work_p[here, L:], work_p[here, :L]).astype(BF16)
        for _, _, size, to in parts:
            work_p[pl.ds(to, size), :] = dot(work_x[pl.ds(to, size), :], weights)

    def forward_act(layer, parts, constants):
        bias = constants[2]
        for hi, here in pieces(parts):
            by_pair = from_geo[here, L * layer : L * layer + L]
            fwd = work_p[here, :L] + (bias + by_pair)
            rev = work_p[here, L:] + (bias - by_pair)
            pre = jnp.concatenate([fwd, rev], axis=1)
            sig = 0.5 * jnp.tanh(0.5 * pre) + 0.5
            act = pre * sig
            slope[layer, here, :] = sig + act * (1.0 - sig)
            diff = act[:, :L] - act[:, L:]
            is_hi = hi[...] > 0.5
            none = jnp.zeros_like(diff)
            work_d[here, :L] = diff.astype(BF16)
            work_e[here, :L] = jnp.where(is_hi, none, diff).astype(BF16)
            work_e[here, L:] = jnp.where(is_hi, diff, none).astype(BF16)

    def edge_constants(layer, h_lo, h_hi):
        straight, crossed = edge_weights(layer)
        weights = jnp.concatenate([straight, crossed], axis=0)
        return jnp.concatenate([h_lo, h_hi], axis=1), weights, edge_bias_ref[layer : layer + 1, :]

    def edge_forward(layer, h_lo, h_hi, last, constants, begun):
        t_nb[...] = jnp.zeros_like(t_nb)

        def collect(part):
            refs, at, size, to = part
            rows = pl.ds(to, size)
            by_j = dot(refs[1][1, :, pl.ds(at, size)], work_e[rows, :])
            return dot(refs[1][0, :, pl.ds(at, size)], work_d[rows, :L]), by_j

        def more(at):
            part = nb_part(at, BLK)
            forward_pre([part], [h_hi], constants)
            forward_act(layer, [part], constants)
            by_i, by_j = collect(part)
            t_nb[:, :L] += -by_j[:, :L]
            t_nb[:, L:] += by_i - by_j[:, L:]

        further(last, more)
        parts = [own_part, nb_part(0, BLK * SURE[last])]
        if begun:
            forward_pre(parts[1:], [h_hi], constants)
        else:
            forward_pre(parts, [h_lo, h_hi], constants)
        forward_act(layer, parts, constants)
        by_i, by_j = collect(parts[0])
        nb_i, nb_j = collect(parts[1])
        own = (by_i - by_j[:, :L], -by_j[:, L:])
        total = (own[0] - nb_j[:, :L] + t_nb[:, :L], own[1] + nb_i - nb_j[:, L:] + t_nb[:, L:])
        return own, total

    def node_forward(layer, h, total):
        total = total.astype(BF16)
        weights = jnp.concatenate([node_in_ref[layer, :L, :], through[layer]], axis=0)
        pre = dot(jnp.concatenate([h, total], axis=1), weights) + node_bias_ref[layer : layer + 1, :]
        agg = dot(total[:ROWS], edge_out_ref[layer]).astype(BF16)
        joined = jnp.concatenate([h[:ROWS], agg], axis=1)
        sig = 0.5 * jnp.tanh(0.5 * pre) + 0.5
        act = pre * sig
        hidden = act.astype(BF16)
        out = dot(hidden, node_out_ref[layer])
        centred = out - jnp.mean(out, axis=1, keepdims=True)
        inv = lax.rsqrt(jnp.mean(centred * centred, axis=1, keepdims=True) + EPS)
        normed = centred * inv
        new = (h.astype(F32) + normed * gain_ref[layer : layer + 1, :]).astype(BF16)
        return new, (joined, sig + act * (1.0 - sig), hidden, normed, inv)

    def node_backward(layer, grad, kept):
        size = grad.shape[0]
        joined = kept[0]
        node_slope, hidden, normed, inv = (v[:size] for v in kept[1:])
        gain_term = jnp.sum(grad[:ROWS] * normed[:ROWS], axis=0, keepdims=True)
        dnorm = grad * gain_ref[layer : layer + 1, :]
        mean_a = jnp.mean(dnorm, axis=1, keepdims=True)
        mean_b = jnp.mean(dnorm * normed, axis=1, keepdims=True)
        dout = ((dnorm - mean_a - normed * mean_b) * inv).astype(BF16)
        out_term = dot_tn(hidden[:ROWS], dout[:ROWS])
        dpre = (dot_nt(dout, node_out_ref[layer]) * node_slope).astype(BF16)
        in_term = dot_tn(joined, dpre[:ROWS])
        bias_term = jnp.sum(dpre[:ROWS].astype(F32), axis=0, keepdims=True)
        dx = dot_nt(dpre, node_in_ref[layer])
        e = dot_nt(dpre, through[layer]).astype(BF16)
        return grad + dx[:, :L], dx[:, L:].astype(BF16), e, (in_term, bias_term, out_term, gain_term)

    def backward_rows(layer, parts, sources, both):
        gather(parts, sources, both, work_s)
        for hi, here in pieces(parts):
            is_hi = hi[...] > 0.5
            dd = work_s[here, :] - jnp.where(is_hi, work_p[here, L:], work_p[here, :L])
            dfwd = dd * slope[layer, here, :L]
            drev = -dd * slope[layer, here, L:]
            none = jnp.zeros_like(dfwd)
            work_d[here, :L] = dfwd.astype(BF16)
            work_d[here, L:] = drev.astype(BF16)
            work_x[here, :L] = jnp.where(is_hi, none, drev).astype(BF16)
            work_x[here, L:] = jnp.where(is_hi, none, dfwd).astype(BF16)
            work_e[here, :L] = jnp.where(is_hi, drev, none).astype(BF16)
            work_e[here, L:] = jnp.where(is_hi, dfwd, none).astype(BF16)

    def edge_backward(layer, e_lo, e_hi, last):
        both = jnp.concatenate([e_lo, e_hi], axis=1)
        q_nb[...] = jnp.zeros_like(q_nb)

        def nb_collect(part):
            refs, at, size, to = part
            rows, cols = pl.ds(to, size), pl.ds(at, size)
            lo = dot(refs[1][1, :, cols], work_x[rows, :])
            if last == 0:
                return lo, None
            return lo, dot(refs[1][1, :, cols], work_e[rows, :]) + dot(refs[1][0, :, cols], work_d[rows, :])

        def more(at):
            part = nb_part(at, BLK)
            backward_rows(layer, [part], [e_hi], both)
            lo, up = nb_collect(part)
            q_nb[0:ROWS, :] += lo
            if last:
                q_nb[ROWS:, :] += up

        further(last, more)
        parts = [own_part, nb_part(0, BLK * SURE[last])]
        backward_rows(layer, parts, [e_lo, e_hi], both)
        rows = pl.ds(0, EMAX)
        q_lo = dot(own_oht[0], work_d[rows, :]) + dot(own_oht[1], work_x[rows, :])
        q_hi = dot(own_oht[1], work_e[rows, :])
        nb_lo, nb_up = nb_collect(parts[1])
        own = jnp.concatenate([q_lo, q_hi], axis=0)
        if last == 0:
            total = q_lo + nb_lo + q_nb[0:ROWS, :]
        else:
            total = own + jnp.concatenate([nb_lo, nb_up], axis=0) + q_nb[...]
        return own, total, dot(own_row[...], work_d[rows, :])

    h0_lo = lat_ref[0]
    h0_hi = around(low_ref[0:LAT_HALO, :], upp_ref[0:LAT_HALO, :], LAT_HALO, ROWS)
    constants0 = edge_constants(0, h0_lo, h0_hi)
    geo_weights = jnp.concatenate([edge_in_ref[s, 2 * L : 2 * L + 4, :].astype(F32) for s in range(2)], axis=1)
    geo_weights = jnp.concatenate([jnp.zeros((4, 2 * L), F32), geo_weights], axis=0).astype(BF16)

    def set_geo(part):
        refs, at, size, to = part
        from_geo[pl.ds(to, size), :] = dot(refs[3][pl.ds(at, size), :], geo_weights)

    def set_further(at):
        set_block(at, nb_rows[at // BLK], lanes, subs, *nb_refs)
        set_geo(nb_part(at, BLK))

    forward_pre([own_part], [h0_lo], constants0)
    set_geo(own_part)
    for k in range(SURE[3]):
        set_block(BLK * k, nb_rows[k], lanes, subs, *nb_refs)
    through = [dot(edge_out_ref[s], node_in_ref[s, L:, :]).astype(BF16) for s in range(2)]
    set_geo(nb_part(0, BLK * SURE[3]))
    further(3, set_further)
    own0, total0 = (jnp.concatenate(t, axis=0) for t in edge_forward(0, h0_lo, h0_hi, 3, constants0, True))
    h0 = jnp.concatenate([h0_lo, h0_hi], axis=0)
    h1, kept0 = node_forward(0, h0, total0)
    h1_lo, h1_hi = h1[:ROWS], h1[ROWS:]
    constants1 = edge_constants(1, h1_lo, h1_hi)
    own1, total1 = (jnp.concatenate(t, axis=0) for t in edge_forward(1, h1_lo, h1_hi, 2, constants1, False))
    near = ROWS + 2 * COT_HALO
    h2, kept1 = node_forward(1, h1[:near], total1[:near])
    final_v[...] = h2[:ROWS]

    few = lax.broadcasted_iota(jnp.int32, (MIG, 2 * COT_HALO), 1).astype(F32)
    for k, ref in ((0, upp_ref), (1, low_ref)):
        movers = jnp.transpose(ref[X_AT:SENT, :].astype(F32))[0:MIG, 0:1]
        arr_v[k] = dot(masked(movers == few), h2[ROWS:]).astype(BF16)
    copies = [
        pltpu.make_async_copy(final_v, final_ref.at[0], sems.at[0]),
        pltpu.make_async_copy(arr_v, arr_ref.at[0], sems.at[1]),
        pltpu.make_async_copy(grad_v, grad_ref.at[0], sems.at[2]),
    ]
    copies[0].start()
    copies[1].start()

    def with_zeros(value):
        return jnp.concatenate([value, jnp.zeros((2 * ROWS - value.shape[0],) + value.shape[1:], value.dtype)], axis=0)

    def layer_back(layer, grad, kept, own_total, h, last, keep_rows):
        part, dagg, e, node_terms = node_backward(layer, grad, kept)
        reached = ROWS + 64
        e = with_zeros(e)
        q_own, q_all, geo = edge_backward(layer, e[:ROWS], e[ROWS:], last)
        out_term = dot_tn(own_total[:reached].astype(BF16), dagg[:reached])
        in_term = dot_tn(h[:reached], q_own[:reached].astype(BF16))
        straight, _ = edge_weights(layer)
        new = part[:keep_rows] + dot_nt(q_all[:keep_rows].astype(BF16), straight)
        return new, (in_term, geo, out_term) + node_terms

    cot = jnp.concatenate(
        [cot_ref[0], around(low_ref[LAT_HALO:D_AT, :], upp_ref[LAT_HALO:D_AT, :], COT_HALO, 2 * COT_HALO)], axis=0
    ).astype(F32)
    size = MAIN // chunks
    per = -(-EXTRA // chunks)
    packed_ref[:, size:, :] = jnp.zeros((chunks, packed_ref.shape[1] - size, L), BF16)

    def put(layer, terms):
        in_term, geo, out_term, node_in_term, node_bias_term, node_out_term, gain_term = terms
        at = layer * (MAIN // 2)
        for value in (in_term[:, :L], in_term[:, L:], out_term, node_in_term, node_out_term):
            value = value.astype(BF16)
            while value.shape[0]:
                take = min(value.shape[0], size - at % size)
                packed_ref[at // size, at % size : at % size + take, :] = value[:take]
                value = value[take:]
                at += take
        small = [geo[4 + g : 5 + g, :L] - geo[4 + g : 5 + g, L:] for g in range(4)]
        small += [geo[3:4, :L] + geo[3:4, L:], node_bias_term, gain_term]
        for extra, value in enumerate(small, layer * (EXTRA // 2)):
            spot = size + extra % per
            packed_ref[extra // per, spot : spot + 1, :] = value.astype(BF16)

    grad1, terms1 = layer_back(1, cot, kept1, own1, h1, 1, ROWS + 64)
    put(1, terms1)
    grad0, terms0 = layer_back(0, grad1, kept0, own0, h0, 0, ROWS)
    grad_v[...] = grad0
    copies[2].start()
    put(0, terms0)

    for copy in copies:
        copy.wait()


def fold_kernel(copies, in_ref, *refs):
    total = in_ref[0].astype(F32)
    for k in range(1, in_ref.shape[0]):
        total += in_ref[k].astype(F32)
    if len(refs) > 1:
        total += refs[0][...].astype(F32)
    total = total.astype(BF16)
    if copies is None:
        refs[-1][...] = total
    else:
        for k in range(copies):
            refs[-1][k] = total


def fold(copies, array, *more):
    shape = array.shape[1:] if copies is None else (copies,) + array.shape[1:]
    return pl.pallas_call(
        lambda *refs: fold_kernel(copies, *refs),
        out_shape=jax.ShapeDtypeStruct(shape, BF16),
        in_specs=vmem(1 + len(more)),
        out_specs=pl.BlockSpec(memory_space=pltpu.VMEM),
        compiler_params=pltpu.CompilerParams(vmem_limit_bytes=VMEM_LIMIT),
        name="fold",
    )(array, *more)


def unpack_kernel(chunks, ref, edge_in, edge_bias, edge_out, node_in, node_bias, node_out, gain):
    size = MAIN // chunks
    per = -(-EXTRA // chunks)
    at = 0
    extra = 0
    for layer in range(2):
        for out, rows in ((edge_in, 2 * L), (edge_out, L), (node_in, 2 * L), (node_out, L)):
            r = 0
            while r < rows:
                take = min(rows - r, size - at % size)
                value = ref[at // size, at % size : at % size + take, :].astype(F32)
                if out is edge_in:
                    out[pl.ds(2 * r + layer, take, stride=2), :] = value
                else:
                    out[layer, r : r + take, :] = value
                r += take
                at += take
        small = []
        for _ in range(7):
            spot = size + extra % per
            small.append(ref[extra // per, spot : spot + 1, :].astype(F32))
            extra += 1
        for g in range(4):
            edge_in[4 * L + 2 * g + layer : 4 * L + 2 * g + layer + 1, :] = small[g]
        edge_bias[layer : layer + 1, :] = small[4]
        node_bias[layer : layer + 1, :] = small[5]
        gain[layer : layer + 1, :] = small[6]


def rows_of(array):
    return jnp.transpose(array, (1, 0, 2)).reshape(-1, array.shape[2])


def vmem(count):
    return [pl.BlockSpec(memory_space=pltpu.VMEM)] * count


def solution(mesh):
    n_space = mesh.shape["space"]
    n_x = mesh.shape["replicas"]
    n_c = 2
    n_z = min(16, n_space // n_c)
    n_y = n_space // (n_c * n_z)
    n_l = 2 if n_z > 4 else 1
    n_h = n_z // n_l
    n_b = 2 if n_h > 4 else 1
    fine = Mesh(mesh.devices.reshape(n_y, n_h // n_b, n_b, n_l, n_c, n_x), ("y", "za", "zb", "zl", "c", "x"))
    space = ("y", "za", "zb", "zl", "c")
    group = ("zl", "y", "x")
    chunks = n_y * n_l * n_x
    size = MAIN // chunks
    chunk_rows = size + -(-(-(-EXTRA // chunks)) // 8) * 8
    params = pltpu.CompilerParams(vmem_limit_bytes=VMEM_LIMIT)

    def on_device(latents, pairs, geometry, pair_count, cotangent, leaving, *weights):
        sent = jax.ShapeDtypeStruct((SENT, L), BF16)
        to_b, to_a = pl.pallas_call(
            pack_kernel,
            out_shape=(sent, sent),
            in_specs=[pl.BlockSpec(memory_space=pltpu.HBM)] * 6,
            out_specs=tuple(vmem(2)),
            scratch_shapes=[
                pltpu.VMEM((1, 1), jnp.int32),
                pltpu.VMEM((2, EMAX), jnp.int32),
                pltpu.VMEM((4, EMAX), BF16),
                pltpu.VMEM((2, MIG), jnp.int32),
                pltpu.SemaphoreType.DMA((8,)),
            ],
            compiler_params=pltpu.CompilerParams(vmem_limit_bytes=60 * 1024 * 1024),
            name="pack",
        )(pair_count, latents, cotangent, pairs, geometry, leaving)
        half = range(n_space // 2)
        near = [(2 * i, 2 * i + 1) for i in half]
        cross = [(2 * i + 1, (2 * i + 2) % n_space) for i in half]
        from_b = lax.ppermute(to_b, space, cross + [(j, i) for i, j in cross])
        from_a = lax.ppermute(to_a, space, near + [(j, i) for i, j in near])
        own = pl.pallas_call(
            own_kernel,
            out_shape=(
                jax.ShapeDtypeStruct((2, EMAX, ROWS), BF16),
                jax.ShapeDtypeStruct((2, ROWS, EMAX), BF16),
                jax.ShapeDtypeStruct((EMAX, L), F32),
                jax.ShapeDtypeStruct((EMAX, 8), BF16),
                jax.ShapeDtypeStruct((8, EMAX), BF16),
            )
            + (jax.ShapeDtypeStruct((2, L), F32),) * 3,
            in_specs=vmem(6),
            out_specs=tuple(vmem(8)),
            compiler_params=pltpu.CompilerParams(vmem_limit_bytes=16 * 1024 * 1024),
            cost_estimate=pl.CostEstimate(flops=4000000000, bytes_accessed=40000000, transcendentals=0),
            name="own",
        )(pair_count, pairs, geometry, weights[1], weights[4], weights[6])
        final, grad, arrivals, packed = pl.pallas_call(
            lambda *refs: main_kernel(chunks, *refs),
            out_shape=(
                jax.ShapeDtypeStruct((1, ROWS, L), BF16),
                jax.ShapeDtypeStruct((1, ROWS, L), F32),
                jax.ShapeDtypeStruct((1, 2, MIG, L), BF16),
                jax.ShapeDtypeStruct((chunks, chunk_rows, L), BF16),
            ),
            in_specs=vmem(16),
            out_specs=tuple([pl.BlockSpec(memory_space=pl.ANY)] * 3 + vmem(1)),
            scratch_shapes=[
                pltpu.VMEM((SENT, L), BF16),
                pltpu.VMEM((SENT, L), BF16),
                pltpu.VMEM((2, 2 * EMAX, ROWS), BF16),
                pltpu.VMEM((2, ROWS, 2 * EMAX), BF16),
                pltpu.VMEM((2 * EMAX, L), F32),
                pltpu.VMEM((2 * EMAX, 8), BF16),
                pltpu.VMEM((2, ALL_PAIRS, 2 * L), F32),
                pltpu.VMEM((NB_BLOCKS, 8, BLK), F32),
                pltpu.VMEM((ALL_PAIRS, 2 * L), BF16),
                pltpu.VMEM((ALL_PAIRS, 2 * L), F32),
                pltpu.VMEM((ALL_PAIRS, 2 * L), BF16),
                pltpu.VMEM((ALL_PAIRS, 2 * L), BF16),
                pltpu.VMEM((ALL_PAIRS, L), F32),
                pltpu.VMEM((ALL_PAIRS, 2 * L), F32),
                pltpu.VMEM((ROWS, 2 * L), F32),
                pltpu.VMEM((2 * ROWS, 2 * L), F32),
                pltpu.VMEM((ROWS, L), BF16),
                pltpu.VMEM((2, MIG, L), BF16),
                pltpu.VMEM((ROWS, L), F32),
                pltpu.VMEM((2 * weights[0].shape[1], L), F32),
                pltpu.VMEM(weights[0].shape, BF16),
                pltpu.SemaphoreType.DMA((3,)),
            ],
            compiler_params=params,
            name="steps",
        )(
            latents, cotangent, *own[:5], from_b, from_a,
            rows_of(weights[0]), own[5], weights[2], weights[3], own[6], weights[5], own[7],
        )

        got = lax.all_to_all(packed, group, 0, 0, tiled=True)
        got = fold(None, lax.all_to_all(fold(n_h, got), ("zb", "za"), 0, 0, tiled=True))
        got = fold(chunks, got[None], lax.ppermute(got, "c", [(0, 1), (1, 0)]))
        got = lax.all_to_all(got, group, 0, 0, tiled=True)

        grads = pl.pallas_call(
            lambda *refs: unpack_kernel(chunks, *refs),
            out_shape=(jax.ShapeDtypeStruct((2 * weights[0].shape[1], L), F32),)
            + tuple(jax.ShapeDtypeStruct(w.shape, F32) for w in weights[1:]),
            in_specs=vmem(1),
            out_specs=tuple(vmem(7)),
            compiler_params=params,
            name="unpack",
        )(got)
        edge_in_grad = jnp.transpose(grads[0].reshape(-1, 2, L), (1, 0, 2))
        return (final, grad, arrivals, edge_in_grad) + tuple(grads[1:])

    return jax.shard_map(
        on_device,
        mesh=fine,
        in_specs=(
            P("x", space, None),
            P("x", None, space),
            P("x", None, space),
            P("x", space),
            P("x", space, None),
            P("x", space, None),
        )
        + (P(),) * 7,
        out_specs=(P("x", space, None), P("x", space, None), P("x", space, None, None)) + (P(),) * 7,
        check_vma=False,
    )
```
